128 devices in a mesh: layer: 4 (over x), tile: 32 (over z, y, core).
Axes of the slice: x: 4, y: 4, z: 4, core: 2. Of those that a mesh axis runs over, the one named last changes fastest.
Arguments:
- frames: bfloat16 [6, 32, 16, 8, 256], P(None, 'tile'), may hold values from -6 to 6
- weight: bfloat16 [4, 4608, 1024], P('layer'), may hold values from -0.09375 to 0.09375
- cotangent: bfloat16 [6, 32, 16, 8, 256], P(None, 'tile'), may hold values from -6 to 6
Outputs:
- hidden_maps: bfloat16 [4, 6, 32, 16, 8, 256], P('layer', None, 'tile')
- grad_inputs: bfloat16 [4, 6, 32, 16, 8, 256], P('layer', None, 'tile')
- weight_grad: float32 [4, 4608, 1024], P('layer', 'tile')
The draws below stay inside these ranges and needn't reach their ends.
All inputs are finite; a program needn't handle non-finite values.
Results may differ from the reference program's by a relative error of at most 0.02.
Values may be sent and summed in bfloat16 or wider, within the bound.
A program may use at most 128 MiB of HBM per device.

```python
import jax
import jax.numpy as jnp
from jax import lax

C = 256
GATES = 1024
KK = 4608
STEPS = 6
TH = 16
TW = 8
TX = 8
LAYERS = 4
TILES = 32
TY = 4
HEIGHT = 64
WIDTH = 64


def steps_of(rng, dims, cuts, least, top_value):
    level = 1.0
    for position, blocks in cuts:
        steps = jax.random.uniform(jax.random.fold_in(jax.random.fold_in(rng, 6), position), (blocks,), jnp.float32, least / len(cuts), top_value / len(cuts))
        level = level * jnp.repeat(jnp.exp(steps), dims[position] // blocks).reshape((-1,) + (1,) * (len(dims) - 1 - position))
    return level


def noise(rng, dims, width, reach, shards=(), held_as=jnp.bfloat16):
    drawn = jax.random.normal(rng, dims, jnp.float32) * width
    if len(shards) > 0:
        drawn = steps_of(rng, dims, shards, -0.22, 0.18) * drawn
    return jnp.clip(drawn, min=-reach, max=reach).astype(held_as)


def setup_inputs(seed: int = 0) -> dict:
    key_list = jax.random.split(jax.random.key(seed), 4)
    return {
        "frames": noise(key_list[0], (STEPS, TILES, TH, TW, C), 1.0, 6.0, ((1, 32),)),
        "weight": noise(key_list[1], (LAYERS, KK, GATES), KK ** -0.5, 0.09375, ((0, 4),)),
        "cotangent": noise(key_list[2], (STEPS, TILES, TH, TW, C), 1.0, 6.0, ((1, 32),)),
    }


FORGET_SHIFT = 1.0


def cell_forward(gate_sums, cell_prev):
    channels = cell_prev.shape[-1]
    in_gate = jax.nn.sigmoid(gate_sums[:, :channels])
    forget = jax.nn.sigmoid(gate_sums[:, channels:2 * channels] + FORGET_SHIFT)
    out_gate = jax.nn.sigmoid(gate_sums[:, 2 * channels:3 * channels])
    update = jnp.tanh(gate_sums[:, 3 * channels:])
    cell_state = forget * cell_prev + in_gate * update
    hidden = out_gate * jnp.tanh(cell_state)
    return jnp.concatenate([in_gate, forget, out_gate, update], axis=1), cell_state, hidden


def cell_backward(activations, cell_state, cell_prev, grad_hidden, carried):
    channels = cell_state.shape[-1]
    in_gate = activations[:, :channels]
    forget = activations[:, channels:2 * channels]
    out_gate = activations[:, 2 * channels:3 * channels]
    update = activations[:, 3 * channels:]
    squashed = jnp.tanh(cell_state)
    grad_cell = grad_hidden * out_gate * (1.0 - squashed * squashed) + carried
    grad_gates = jnp.concatenate([
        grad_cell * update * in_gate * (1.0 - in_gate),
        grad_cell * cell_prev * forget * (1.0 - forget),
        grad_hidden * squashed * out_gate * (1.0 - out_gate),
        grad_cell * in_gate * (1.0 - update * update)], axis=1)
    return grad_gates, grad_cell * forget


def patch_rows(padded, tile_rows, tile_cols):
    pieces = [padded[tap_row:tap_row + tile_rows, tap_col:tap_col + tile_cols] for tap_row in range(3) for tap_col in range(3)]
    return jnp.concatenate(pieces, axis=-1).reshape(tile_rows * tile_cols, -1)


def to_crop(tiled):
    frame_count = tiled.shape[0]
    return tiled.reshape(frame_count, TY, TX, TH, TW, C).transpose(0, 1, 3, 2, 4, 5).reshape(frame_count, HEIGHT, WIDTH, C)


def to_tiles(crop):
    frame_count = crop.shape[0]
    return crop.reshape(frame_count, TY, TH, TX, TW, C).transpose(0, 1, 3, 2, 4, 5).reshape(frame_count, TILES, TH, TW, C)


def reference(frames, weight, cotangent):
    pixels = HEIGHT * WIDTH
    layer_input = to_crop(frames)
    hidden_list, cell_lists, act_lists, pad_lists = [], [], [], []
    for layer_index in range(LAYERS):
        hidden = jnp.zeros((HEIGHT, WIDTH, C), jnp.bfloat16)
        cell_state = jnp.zeros((pixels, C), jnp.float32)
        cell_steps, act_steps, pad_steps, out_steps = [cell_state], [], [], []
        for time_step in range(STEPS):
            stacked = jnp.concatenate([layer_input[time_step], hidden], axis=-1)
            padded = jnp.pad(stacked, ((1, 1), (1, 1), (0, 0)))
            gate_sums = jnp.dot(patch_rows(padded, HEIGHT, WIDTH), weight[layer_index], preferred_element_type=jnp.float32)
            activations, cell_state, fresh = cell_forward(gate_sums, cell_state)
            hidden = fresh.astype(jnp.bfloat16).reshape(HEIGHT, WIDTH, C)
            cell_steps.append(cell_state)
            act_steps.append(activations)
            pad_steps.append(padded)
            out_steps.append(hidden)
        layer_input = jnp.stack(out_steps)
        hidden_list.append(to_tiles(layer_input))
        cell_lists.append(cell_steps)
        act_lists.append(act_steps)
        pad_lists.append(pad_steps)
    from_top = to_crop(cotangent)
    grad_list = [None] * LAYERS
    weight_list = [None] * LAYERS
    for layer_index in reversed(range(LAYERS)):
        recurrent = jnp.zeros((pixels, C), jnp.float32)
        carried = jnp.zeros((pixels, C), jnp.float32)
        grad_steps = [None] * STEPS
        weight_total = jnp.zeros((KK, GATES), jnp.float32)
        for time_step in reversed(range(STEPS)):
            grad_hidden = from_top[time_step].astype(jnp.float32).reshape(pixels, C) + recurrent
            grad_gates, carried = cell_backward(act_lists[layer_index][time_step], cell_lists[layer_index][time_step + 1], cell_lists[layer_index][time_step], grad_hidden, carried)
            grad_gates = grad_gates.astype(jnp.bfloat16)
            spread = lax.dot_general(grad_gates, weight[layer_index], (((1,), (1,)), ((), ())), preferred_element_type=jnp.float32)
            local_sums = jnp.zeros((HEIGHT + 2, WIDTH + 2, 2 * C), jnp.float32)
            for tap_row in range(3):
                for tap_col in range(3):
                    tap_index = 3 * tap_row + tap_col
                    term = spread[:, tap_index * 2 * C:(tap_index + 1) * 2 * C].reshape(HEIGHT, WIDTH, 2 * C)
                    local_sums = local_sums.at[tap_row:tap_row + HEIGHT, tap_col:tap_col + WIDTH].add(term)
            grad_stacked = local_sums[1:-1, 1:-1].reshape(pixels, 2 * C)
            grad_steps[time_step] = grad_stacked[:, :C].astype(jnp.bfloat16).reshape(HEIGHT, WIDTH, C)
            recurrent = grad_stacked[:, C:]
            patches = patch_rows(pad_lists[layer_index][time_step], HEIGHT, WIDTH)
            weight_total = weight_total + jnp.dot(patches.T, grad_gates, preferred_element_type=jnp.float32)
        from_top = jnp.stack(grad_steps)
        grad_list[layer_index] = to_tiles(from_top)
        weight_list[layer_index] = weight_total
    return jnp.stack(hidden_list), jnp.stack(grad_list), jnp.stack(weight_list)
```

```python
import jax
import jax.numpy as jnp
from jax import lax
from jax.experimental import pallas as pl
from jax.experimental.pallas import tpu as pltpu
from jax.sharding import PartitionSpec as P

MESH = pl.DeviceIdType.MESH
F32 = jnp.float32
BF16 = jnp.bfloat16

C = 256
GC = 1024
STEPS = 6
COLS = 8
ROWS = 16
PIX = COLS * ROWS
ROWS_OUT = 288
HALF = 144
FORGET_SHIFT = 1.0
DIRS = ((-1, -1), (-1, 0), (-1, 1), (0, -1), (0, 1), (1, -1), (1, 0), (1, 1))


def sigmoid(value):
    return 0.5 * jnp.tanh(0.5 * value) + 0.5


def kernel(
    frames, weight, cotangent, hid_out, gin_out, wg_out,
    w, wt, acc, xc, xst, xrim, hs, hst, hrim, st, pst, act, cell, squash, up, gates, gst, grim, sg, pg, gin,
    recurrent, carried, sums, part, from_l, from_r, full_l, full_r, total, from2_l, from2_r, full2_l, full2_r, res, pres,
    w_sem, in_sem, out_sem, xs_send, fr_send, hs_send, gs_send, u_send, ps_send, pg_send,
    xc_recv, x_recv, h_recv, g_recv, u_recv, ps_recv, pg_recv,
    t_send, t_recv, f_send, f_recv, t2_send, t2_recv, f2_send, f2_recv, r_send, r_recv,
):
    layer = lax.axis_index("layer")
    tile = lax.axis_index("tile")
    trow, tcol = tile // 8, lax.rem(tile, 8)
    ypos, core = tcol // 2, lax.rem(tcol, 2)
    mate = tile + 1 - 2 * core

    def there(d):
        dy, dx = DIRS[d]
        found = jnp.bool_(True)
        if dy < 0:
            found = found & (trow > 0)
        if dy > 0:
            found = found & (trow < 3)
        if dx < 0:
            found = found & (tcol > 0)
        if dx > 0:
            found = found & (tcol < 7)
        return found, tile + 8 * dy + dx

    def remote(src, dst, send, recv, to_layer, to_tile):
        return pltpu.make_async_remote_copy(
            src_ref=src, dst_ref=dst, send_sem=send, recv_sem=recv,
            device_id={"layer": to_layer, "tile": to_tile}, device_id_type=MESH,
        )

    def at_ring(along_y, step):
        if along_y:
            return trow * 8 + lax.rem(ypos + step, 4) * 2 + core
        return lax.rem(trow + step, 4) * 8 + tcol

    w_copy = pltpu.make_async_copy(weight, w, w_sem)
    w_copy.start()

    @pl.when(layer == 0)
    def _():
        pltpu.make_async_copy(frames, xc, in_sem).start()

    @pl.when(layer == 3)
    def _():
        pltpu.make_async_copy(cotangent, up, in_sem).start()

    barrier = pltpu.get_barrier_semaphore()
    expected = jnp.int32(0)

    def greet(found, to_layer, to_tile):
        @pl.when(found)
        def _():
            pl.semaphore_signal(barrier, inc=1, device_id={"layer": to_layer, "tile": to_tile}, device_id_type=MESH)

        return found.astype(jnp.int32)

    for d in range(8):
        found, other = there(d)
        expected += greet(found, layer, other)
        expected += greet(found & (layer > 0), layer - 1, other)
        expected += greet(found & (layer < 3), layer + 1, other)
    expected += greet(layer > 0, layer - 1, tile)
    expected += greet(layer < 3, layer + 1, tile)
    for along_y in (True, False):
        for step in (1, 3):
            expected += greet(jnp.bool_(True), layer, at_ring(along_y, step))

    acc[...] = jnp.zeros_like(acc)
    recurrent[...] = jnp.zeros_like(recurrent)
    carried[...] = jnp.zeros_like(carried)
    cell[0] = jnp.zeros((PIX, C), F32)
    st[0, :, :, :, C:] = jnp.zeros((3, COLS + 2, ROWS, C), BF16)
    for d in range(8):
        found, _ = there(d)

        @pl.when(jnp.logical_not(found))
        def _(d=d):
            xrim[d] = jnp.zeros((STEPS, ROWS, C), BF16)
            hrim[d] = jnp.zeros((STEPS, ROWS, C), BF16)
            grim[d] = jnp.zeros((STEPS, ROWS, GC), BF16)

    pl.semaphore_wait(barrier, expected)

    pixel_row = lax.broadcasted_iota(jnp.int32, (ROWS, 1), 0)
    is_top = pixel_row == 0
    is_bottom = pixel_row == ROWS - 1

    def put_centre(dst, lanes, value):
        wide = value.shape[-1]
        dst[0, 1:9, :, lanes] = pltpu.roll(value, 1, 0).astype(BF16).reshape(COLS, ROWS, wide)
        dst[1, 1:9, :, lanes] = value.astype(BF16).reshape(COLS, ROWS, wide)
        dst[2, 1:9, :, lanes] = pltpu.roll(value, PIX - 1, 0).astype(BF16).reshape(COLS, ROWS, wide)

    def put_rim(dst, lanes, rim, t):
        wide = rim.shape[-1]
        top = rim[1, t].astype(F32)[0:8].reshape(COLS, 1, wide)
        bottom = rim[6, t].astype(F32)[0:8].reshape(COLS, 1, wide)
        dst[0, 1:9, :, lanes] = jnp.where(is_top[None], top, dst[0, 1:9, :, lanes].astype(F32)).astype(BF16)
        dst[2, 1:9, :, lanes] = jnp.where(is_bottom[None], bottom, dst[2, 1:9, :, lanes].astype(F32)).astype(BF16)
        for column, side, above, below, at in ((0, 3, 0, 5, 7), (9, 4, 2, 7, 0)):
            value = rim[side, t].astype(F32)
            upper = rim[above, t].astype(F32)[at : at + 1]
            lower = rim[below, t].astype(F32)[at : at + 1]
            dst[0, column, :, lanes] = jnp.where(is_top, upper, pltpu.roll(value, 1, 0)).astype(BF16)
            dst[1, column, :, lanes] = rim[side, t]
            dst[2, column, :, lanes] = jnp.where(is_bottom, lower, pltpu.roll(value, ROWS - 1, 0)).astype(BF16)

    def put_stage(stage, t, lanes, value):
        cut = value.reshape(COLS, ROWS, value.shape[-1])
        for side, at in ((0, 0), (1, ROWS - 1)):
            row = cut[:, at, :]
            stage[t, side, :, lanes] = jnp.concatenate([row, row], axis=0).astype(BF16)

    def rim_source(d, store, stage, t):
        dy, dx = DIRS[d]
        if dy < 0:
            return stage.at[t, 0]
        if dy > 0:
            return stage.at[t, 1]
        return store.at[t, 0 if dx < 0 else COLS - 1]

    def send_rims(store, stage, rim, t, send, recv, to_layer, first):
        for d in range(8):
            found, other = there(d)

            @pl.when(found)
            def _(d=d, other=other):
                copy = remote(
                    rim_source(d, store, stage, t), rim.at[7 - d, t], send.at[d], recv.at[7 - d, t], to_layer, other
                )

                @pl.when(jnp.logical_not(first))
                def _():
                    copy.wait_send()

                copy.start()

    def end_rims(store, stage, rim, send, recv):
        for d in range(8):
            found, other = there(d)

            @pl.when(found)
            def _(d=d, other=other):
                remote(
                    rim_source(d, store, stage, 0), rim.at[7 - d, 0], send.at[d], recv.at[7 - d, 0], layer, other
                ).wait_send()

    def wait_rims(rim, t, send, recv):
        for d in range(8):
            found, other = there(d)

            @pl.when(found)
            def _(d=d, other=other):
                remote(rim.at[d, t], rim.at[d, t], send.at[d], recv.at[d, t], layer, other).wait_recv()

    def turn_weight():
        def one(k, _):
            rows = pl.multiple_of(k * 512, 512)
            wt[pl.ds(pl.multiple_of(k * GC, GC), GC), :] = w[pl.ds(rows, 512), :].T
            return 0

        lax.fori_loop(0, 9, one, 0)

    @pl.when(layer == 0)
    def _():
        pltpu.make_async_copy(frames, xc, in_sem).wait()

        def one(t, _):
            put_stage(xst, t, slice(0, C), xc[t].astype(F32).reshape(PIX, C))
            send_rims(xc, xst, xrim, t, fr_send, x_recv, layer, t == 0)
            return 0

        lax.fori_loop(0, STEPS, one, 0)
        end_rims(xc, xst, xrim, fr_send, x_recv)

    w_copy.wait()

    @pl.when(layer == 3)
    def _():
        pltpu.make_async_copy(cotangent, up, in_sem).wait()
        turn_weight()

    def mate_patches(t):
        return remote(st.at[t], pst.at[t], ps_send, ps_recv.at[t], layer, mate)

    def above_map(t):
        return remote(hs.at[t], xc.at[t], xs_send.at[8], xc_recv.at[t], layer + 1, tile)

    def forward(t, _):
        @pl.when(layer > 0)
        def _():
            remote(xc.at[t], xc.at[t], xs_send.at[8], xc_recv.at[t], layer - 1, tile).wait_recv()

        put_centre(st.at[t], slice(0, C), xc[t].astype(F32).reshape(PIX, C))
        wait_rims(xrim, t, xs_send, x_recv)
        put_rim(st.at[t], slice(0, C), xrim, t)

        @pl.when(t > 0)
        def _():
            wait_rims(hrim, t - 1, hs_send, h_recv)
            put_rim(st.at[t], slice(C, 2 * C), hrim, t - 1)
            mate_patches(t - 1).wait_send()

        mate_patches(t).start()
        patches = jnp.concatenate(
            [st[t, p, q : q + 8].reshape(PIX, 2 * C) for p in range(3) for q in range(3)], axis=1
        )
        sums[...] = jnp.dot(patches, w[...], preferred_element_type=F32)
        in_gate = sigmoid(sums[:, 0:C])
        forget = sigmoid(sums[:, C : 2 * C] + FORGET_SHIFT)
        out_gate = sigmoid(sums[:, 2 * C : 3 * C])
        update = jnp.tanh(sums[:, 3 * C :])
        fresh = forget * cell[t] + in_gate * update
        squashed = jnp.tanh(fresh)
        hidden = out_gate * squashed
        hs[t] = hidden.astype(BF16).reshape(COLS, ROWS, C)
        put_stage(hst, t, slice(0, C), hidden)

        @pl.when(t < STEPS - 1)
        def _():
            send_rims(hs, hst, hrim, t, hs_send, h_recv, layer, t == 0)

        @pl.when(layer < 3)
        def _():
            @pl.when(t > 0)
            def _():
                above_map(t - 1).wait_send()

            above_map(t).start()
            send_rims(hs, hst, xrim, t, xs_send, x_recv, layer + 1, t == 0)

        act[t, :, 0:C] = in_gate
        act[t, :, C : 2 * C] = forget
        act[t, :, 2 * C : 3 * C] = out_gate
        act[t, :, 3 * C :] = update
        cell[t + 1] = fresh
        squash[t] = squashed

        @pl.when(t < STEPS - 1)
        def _():
            put_centre(st.at[t + 1], slice(C, 2 * C), hidden)

        return 0

    lax.fori_loop(0, STEPS, forward, 0)
    mate_patches(STEPS - 1).wait_send()
    end_rims(hs, hst, hrim, hs_send, h_recv)

    hid_copy = pltpu.make_async_copy(hs, hid_out, out_sem.at[0])
    hid_copy.start()

    @pl.when(layer < 3)
    def _():
        turn_weight()
        above_map(STEPS - 1).wait_send()
        end_rims(hs, hst, xrim, xs_send, x_recv)

    mine = pl.ds(pl.multiple_of(core * 512, 512), 512)
    theirs = pl.ds(pl.multiple_of((1 - core) * 512, 512), 512)

    def mate_gates(t):
        return remote(gates.at[t, :, theirs], pg.at[t], pg_send, pg_recv.at[t], layer, mate)

    def weight_terms(t, p, q):
        lhs = jnp.concatenate(
            [st[t, p, q : q + 8].reshape(PIX, 2 * C), pst[t, p, q : q + 8].reshape(PIX, 2 * C)], axis=0
        )
        rhs = jnp.concatenate([gates[t, :, mine], pg[t]], axis=0)
        return lax.dot_general(lhs, rhs, (((0,), (0,)), ((), ())), preferred_element_type=F32)

    def wait_mate(t):
        mate_patches(t).wait_recv()
        mate_gates(t).wait_recv()

    def below_grad(t):
        return remote(gin.at[t], up.at[t], u_send, u_recv.at[t], layer - 1, tile)

    def backward(i, _):
        t = STEPS - 1 - i

        @pl.when(layer < 3)
        def _():
            remote(up.at[t], up.at[t], u_send, u_recv.at[t], layer + 1, tile).wait_recv()

        grad_hidden = up[t].astype(F32).reshape(PIX, C) + recurrent[...]
        in_gate = act[t, :, 0:C]
        forget = act[t, :, C : 2 * C]
        out_gate = act[t, :, 2 * C : 3 * C]
        update = act[t, :, 3 * C :]
        squashed = squash[t]
        grad_cell = grad_hidden * out_gate * (1.0 - squashed * squashed) + carried[...]
        carried[...] = grad_cell * forget
        parts = (
            grad_cell * update * in_gate * (1.0 - in_gate),
            grad_cell * cell[t] * forget * (1.0 - forget),
            grad_hidden * squashed * out_gate * (1.0 - out_gate),
            grad_cell * in_gate * (1.0 - update * update),
        )
        for n, value in enumerate(parts):
            lanes = slice(C * n, C * n + C)
            gates[t, :, lanes] = value.astype(BF16)
            put_stage(gst, t, lanes, value)
            sg[1, 1:9, :, lanes] = value.astype(BF16).reshape(COLS, ROWS, C)
            gst[t, 2, :, lanes] = value[0:ROWS].astype(BF16)
            gst[t, 3, :, lanes] = value[PIX - ROWS :].astype(BF16)
        for d in range(8):
            found, other = there(d)

            @pl.when(found)
            def _(d=d, other=other):
                dy, dx = DIRS[d]
                side = 0 if dy < 0 else 1 if dy > 0 else 2 if dx < 0 else 3
                copy = remote(gst.at[t, side], grim.at[7 - d, t], gs_send.at[d], g_recv.at[7 - d, t], layer, other)

                @pl.when(i > 0)
                def _():
                    copy.wait_send()

                copy.start()

        @pl.when(i > 0)
        def _():
            mate_gates(t + 1).wait_send()

        mate_gates(t).start()
        for n, value in enumerate(parts):
            lanes = slice(C * n, C * n + C)
            sg[0, 1:9, :, lanes] = pltpu.roll(value, 1, 0).astype(BF16).reshape(COLS, ROWS, C)
            sg[2, 1:9, :, lanes] = pltpu.roll(value, PIX - 1, 0).astype(BF16).reshape(COLS, ROWS, C)

        @pl.when(i > 0)
        def _():
            wait_mate(t + 1)
            for p in range(3):
                for q in range(3):
                    k = 3 * p + q
                    acc[512 * k : 512 * k + 512] += weight_terms(t + 1, p, q)

        wait_rims(grim, t, gs_send, g_recv)
        put_rim(sg, slice(0, GC), grim, t)
        patches = jnp.concatenate(
            [sg[2 - p, 2 - q : 10 - q].reshape(PIX, GC) for p in range(3) for q in range(3)], axis=1
        )
        gin[t] = jnp.dot(patches, wt[:, 0:C], preferred_element_type=F32).astype(BF16).reshape(COLS, ROWS, C)

        @pl.when(layer > 0)
        def _():
            @pl.when(i > 0)
            def _():
                below_grad(t + 1).wait_send()

            below_grad(t).start()

        @pl.when(t > 0)
        def _():
            again = jnp.concatenate(
                [sg[2 - p, 2 - q : 10 - q].reshape(PIX, GC) for p in range(3) for q in range(3)], axis=1
            )
            recurrent[...] = jnp.dot(again, wt[:, C:], preferred_element_type=F32)

        return 0

    lax.fori_loop(0, STEPS, backward, 0)
    gin_copy = pltpu.make_async_copy(gin, gin_out, out_sem.at[1])
    gin_copy.start()
    wait_mate(0)
    mate_gates(0).wait_send()
    for p in range(3):
        for q in range(3):
            k = 3 * p + q
            value = (acc[512 * k : 512 * k + 512] + weight_terms(0, p, q)).astype(BF16)
            low = 512 * k
            while low < 512 * k + 512:
                block = low // ROWS_OUT
                high = min(512 * k + 512, ROWS_OUT * (block + 1))
                rows = slice(low - ROWS_OUT * block, high - ROWS_OUT * block)
                z, y = block // 4, block % 4
                part[0, y, z, rows] = value[low - 512 * k : high - 512 * k, 0:256]
                part[1, z, y, rows] = value[low - 512 * k : high - 512 * k, 256:512]
                low = high

    @pl.when(layer > 0)
    def _():
        below_grad(0).wait_send()

    for d in range(8):
        found, other = there(d)

        @pl.when(found)
        def _(d=d, other=other):
            remote(gst.at[0, 0], grim.at[7 - d, 0], gs_send.at[d], g_recv.at[7 - d, 0], layer, other).wait_send()

    def plus(left, right):
        return (left.astype(F32) + right.astype(F32)).astype(BF16)

    def own(n):
        return (ypos, trow) if n == 0 else (trow, ypos)

    rights, lefts = (2, 1), (3, 0)
    sent = []

    def go(copy):
        copy.start()
        sent.append(copy)
        return copy

    def hop(n, first, to_right):
        return at_ring((n == 0) == first, 1 if to_right else 3)

    hand = {}
    full = {}
    for n in range(2):
        a, b = own(n)
        for m in range(2):
            for right in (True, False):
                j = (rights if right else lefts)[m]
                hand[n, m, right] = go(remote(
                    part.at[n, lax.rem(a + 2, 4), lax.rem(b + j, 4)], (from_l if right else from_r).at[n, m],
                    t_send.at[n, m, int(right)], t_recv.at[n, m, int(right)], layer, hop(n, True, right),
                ))

    def send_full(n, j, right):
        a, b = own(n)
        full[n, j, right] = go(remote(
            part.at[n, lax.rem(a + (1 if right else 3), 4), lax.rem(b + j, 4)], (full_l if right else full_r).at[n, j],
            f_send.at[n, j, int(right)], f_recv.at[n, j, int(right)], layer, hop(n, True, right),
        ))

    for m in range(2):
        for n in range(2):
            send_full(n, lefts[m], True)
            send_full(n, rights[m], False)
    for m in range(2):
        for n in range(2):
            a, b = own(n)
            for right in (True, False):
                j = (rights if right else lefts)[m]
                hand[n, m, right].wait_recv()
                to = (n, lax.rem(a + (1 if right else 3), 4), lax.rem(b + j, 4))
                part[to] = plus(part[to], (from_l if right else from_r)[n, m])
                send_full(n, j, right)

    def gather(n, j):
        a, b = own(n)
        full[n, j, True].wait_recv()
        full[n, j, False].wait_recv()
        total[n, j] = (
            part[n, a, lax.rem(b + j, 4)].astype(F32) + full_l[n, j].astype(F32) + full_r[n, j].astype(F32)
        ).astype(BF16)

    upper, lower = pl.ds(0, HALF), pl.ds(HALF, HALF)
    hand2 = {}
    full2 = {}

    def send_full2(n, right, first):
        rows = lower if right == first else upper
        full2[n, right, first] = go(remote(
            total.at[n, 1 if right else 3, rows], (full2_l if right else full2_r).at[n, rows],
            f2_send.at[n, int(right), int(first)], f2_recv.at[n, int(right), int(first)], layer, hop(n, False, right),
        ))

    for n in range(2):
        gather(n, 2)
        for right in (True, False):
            hand2[n, right] = go(remote(
                total.at[n, 2, upper if right else lower], (from2_l if right else from2_r).at[n],
                t2_send.at[n, int(right)], t2_recv.at[n, int(right)], layer, hop(n, False, right),
            ))
    for right in (True, False):
        for n in range(2):
            gather(n, 1 if right else 3)
            send_full2(n, right, True)
    for n in range(2):
        for right in (True, False):
            hand2[n, right].wait_recv()
            at = (n, 1 if right else 3, upper if right else lower)
            total[at] = plus(total[at], (from2_l if right else from2_r)[n])
            send_full2(n, right, False)
    for n in range(2):
        gather(n, 0)
    for n in range(2):
        for right in (True, False):
            for first in (True, False):
                full2[n, right, first].wait_recv()
        res[:, 256 * n : 256 * n + 256] = plus(
            total[n, 0].astype(F32) + full2_l[n].astype(F32), full2_r[n]
        )
    last = go(remote(
        res.at[pl.ds(pl.multiple_of((1 - core) * HALF, HALF), HALF)], pres, r_send, r_recv, layer, mate
    ))
    wg_out[:, mine] = res[pl.ds(pl.multiple_of(core * HALF, HALF), HALF), :].astype(F32)
    last.wait_recv()
    wg_out[:, theirs] = pres[...].astype(F32)
    for copy in sent:
        copy.wait_send()
    hid_copy.wait()
    gin_copy.wait()


def local(frames, weight, cotangent):
    maps = jax.ShapeDtypeStruct((STEPS, COLS, ROWS, C), BF16)
    vmem = pltpu.VMEM
    dma = pltpu.SemaphoreType.DMA
    shape = (STEPS, COLS, ROWS, C)
    block = (ROWS_OUT, 256)
    hidden, grads, weight_grad = pl.pallas_call(
        kernel,
        out_shape=(maps, maps, jax.ShapeDtypeStruct((HALF, GC), F32)),
        in_specs=[pl.BlockSpec(memory_space=pl.ANY)] * 3,
        out_specs=(
            pl.BlockSpec(memory_space=pl.ANY),
            pl.BlockSpec(memory_space=pl.ANY),
            pl.BlockSpec(memory_space=pltpu.VMEM),
        ),
        scratch_shapes=[
            vmem((4608, GC), BF16),
            vmem((9 * GC, 2 * C), BF16),
            vmem((4608, 512), F32),
            vmem(shape, BF16),
            vmem((STEPS, 2, ROWS, C), BF16),
            vmem((8, STEPS, ROWS, C), BF16),
            vmem(shape, BF16),
            vmem((STEPS, 2, ROWS, C), BF16),
            vmem((8, STEPS, ROWS, C), BF16),
            vmem((STEPS, 3, COLS + 2, ROWS, 2 * C), BF16),
            vmem((STEPS, 3, COLS + 2, ROWS, 2 * C), BF16),
            vmem((STEPS, PIX, GC), F32),
            vmem((STEPS + 1, PIX, C), F32),
            vmem((STEPS, PIX, C), F32),
            vmem(shape, BF16),
            vmem((STEPS, PIX, GC), BF16),
            vmem((STEPS, 4, ROWS, GC), BF16),
            vmem((8, STEPS, ROWS, GC), BF16),
            vmem((3, COLS + 2, ROWS, GC), BF16),
            vmem((STEPS, PIX, 512), BF16),
            vmem(shape, BF16),
            vmem((PIX, C), F32),
            vmem((PIX, C), F32),
            vmem((PIX, GC), F32),
            vmem((2, 4, 4) + block, BF16),
            vmem((2, 2) + block, BF16),
            vmem((2, 2) + block, BF16),
            vmem((2, 4) + block, BF16),
            vmem((2, 4) + block, BF16),
            vmem((2, 4) + block, BF16),
            vmem((2, HALF, 256), BF16),
            vmem((2, HALF, 256), BF16),
            vmem((2,) + block, BF16),
            vmem((2,) + block, BF16),
            vmem((ROWS_OUT, 512), BF16),
            vmem((HALF, 512), BF16),
            dma, dma, dma((2,)),
            dma((9,)), dma((8,)), dma((8,)), dma((8,)), dma, dma, dma,
            dma((STEPS,)), dma((8, STEPS)), dma((8, STEPS)), dma((8, STEPS)),
            dma((STEPS,)), dma((STEPS,)), dma((STEPS,)),
            dma((2, 2, 2)), dma((2, 2, 2)), dma((2, 4, 2)), dma((2, 4, 2)),
            dma((2, 2)), dma((2, 2)), dma((2, 2, 2)), dma((2, 2, 2)), dma, dma,
        ],
        compiler_params=pltpu.CompilerParams(
            collective_id=0, has_side_effects=True, vmem_limit_bytes=63 * 2**20
        ),
    )(
        frames[:, 0].transpose(0, 2, 1, 3),
        weight[0],
        cotangent[:, 0].transpose(0, 2, 1, 3),
    )
    hidden = hidden.transpose(0, 2, 1, 3)
    grads = grads.transpose(0, 2, 1, 3)
    return hidden[None, :, None], grads[None, :, None], weight_grad[None]


def solution(mesh):
    in_specs = (
        P(None, "tile", None, None, None),
        P("layer", None, None),
        P(None, "tile", None, None, None),
    )
    out_specs = (
        P("layer", None, "tile", None, None, None),
        P("layer", None, "tile", None, None, None),
        P("layer", "tile", None),
    )
    return jax.shard_map(local, mesh=mesh, in_specs=in_specs, out_specs=out_specs, check_vma=False)
```

```python
import jax
import jax.numpy as jnp
from jax import lax
from jax.experimental import pallas as pl
from jax.experimental.pallas import tpu as pltpu
from jax.sharding import PartitionSpec as P

MESH = pl.DeviceIdType.MESH
F32 = jnp.float32
BF16 = jnp.bfloat16

C = 256
GC = 1024
STEPS = 6
COLS = 8
ROWS = 16
PIX = COLS * ROWS
ROWS_OUT = 288
HALF = 144
FORGET_SHIFT = 1.0
DIRS = ((-1, -1), (-1, 0), (-1, 1), (0, -1), (0, 1), (1, -1), (1, 0), (1, 1))


def sigmoid(value):
    return 0.5 * jnp.tanh(0.5 * value) + 0.5


def kernel(
    frames, weight, cotangent, hid_out, gin_out, wg_out,
    w, wt, acc, xc, xst, xrim, hs, hst, hrim, st, pst, act, cell, squash, up, gates, pg, hrow, gin,
    rrim, urim, grim, rstage, gstage, gown, gsum, spread,
    recurrent, carried, sums, part, from_l, from_r, full_l, full_r, total, from2_l, from2_r, full2_l, full2_r, res, pres,
    w_sem, in_sem, out_sem, xs_send, fr_send, hs_send, rs_send, us_send, gs_send, ps_send, pg_send,
    xc_recv, x_recv, h_recv, r_recv_rim, u_recv_rim, g_recv_rim, u_recv, ps_recv, pg_recv,
    t_send, t_recv, f_send, f_recv, t2_send, t2_recv, f2_send, f2_recv, r_send, r_recv,
):
    layer = lax.axis_index("layer")
    tile = lax.axis_index("tile")
    trow, tcol = tile // 8, lax.rem(tile, 8)
    ypos, core = tcol // 2, lax.rem(tcol, 2)
    mate = tile + 1 - 2 * core

    def there(d):
        dy, dx = DIRS[d]
        found = jnp.bool_(True)
        if dy < 0:
            found = found & (trow > 0)
        if dy > 0:
            found = found & (trow < 3)
        if dx < 0:
            found = found & (tcol > 0)
        if dx > 0:
            found = found & (tcol < 7)
        return found, tile + 8 * dy + dx

    def remote(src, dst, send, recv, to_layer, to_tile):
        return pltpu.make_async_remote_copy(
            src_ref=src, dst_ref=dst, send_sem=send, recv_sem=recv,
            device_id={"layer": to_layer, "tile": to_tile}, device_id_type=MESH,
        )

    def at_ring(along_y, step):
        if along_y:
            return trow * 8 + lax.rem(ypos + step, 4) * 2 + core
        return lax.rem(trow + step, 4) * 8 + tcol

    @pl.when(layer == 0)
    def _():
        pltpu.make_async_copy(frames, gin, in_sem).start()

    @pl.when(layer == 3)
    def _():
        pltpu.make_async_copy(cotangent, gin, in_sem).start()

    w_copies = [pltpu.make_async_copy(weight.at[:, n], w.at[n], w_sem.at[n]) for n in range(2)]
    for copy in w_copies:
        copy.start()

    barrier = pltpu.get_barrier_semaphore()
    expected = jnp.int32(0)

    def greet(found, to_layer, to_tile):
        @pl.when(found)
        def _():
            pl.semaphore_signal(barrier, inc=1, device_id={"layer": to_layer, "tile": to_tile}, device_id_type=MESH)

        return found.astype(jnp.int32)

    for d in range(8):
        found, other = there(d)
        expected += greet(found, layer, other)
        expected += greet(found & (layer > 0), layer - 1, other)
        expected += greet(found & (layer < 3), layer + 1, other)
    expected += greet(layer > 0, layer - 1, tile)
    expected += greet(layer < 3, layer + 1, tile)
    for along_y in (True, False):
        for step in (1, 3):
            expected += greet(jnp.bool_(True), layer, at_ring(along_y, step))

    acc[...] = jnp.zeros_like(acc)
    recurrent[...] = jnp.zeros_like(recurrent)
    carried[...] = jnp.zeros_like(carried)
    cell[0] = jnp.zeros((PIX, C), F32)
    st[0, 1] = jnp.zeros((3, COLS + 2, ROWS, C), BF16)
    for d in range(8):
        found, _ = there(d)

        @pl.when(jnp.logical_not(found))
        def _(d=d):
            xrim[d] = jnp.zeros((STEPS, ROWS, C), BF16)
            hrim[d] = jnp.zeros((STEPS, ROWS, C), BF16)
            rrim[d] = jnp.zeros((STEPS, ROWS, C), F32)
            urim[d] = jnp.zeros((STEPS, ROWS, C), F32)
            grim[d] = jnp.zeros((STEPS, ROWS, C), F32)

    pl.semaphore_wait(barrier, expected)

    pixel_row = lax.broadcasted_iota(jnp.int32, (ROWS, 1), 0)
    is_top = pixel_row == 0
    is_bottom = pixel_row == ROWS - 1

    def put_centre(dst, value):
        dst[0, 1:9] = pltpu.roll(value, 1, 0).astype(BF16).reshape(COLS, ROWS, C)
        dst[1, 1:9] = value.astype(BF16).reshape(COLS, ROWS, C)
        dst[2, 1:9] = pltpu.roll(value, PIX - 1, 0).astype(BF16).reshape(COLS, ROWS, C)

    def put_rim(dst, rim, t):
        top = rim[1, t].astype(F32)[0:8].reshape(COLS, 1, C)
        bottom = rim[6, t].astype(F32)[0:8].reshape(COLS, 1, C)
        dst[0, 1:9] = jnp.where(is_top[None], top, dst[0, 1:9].astype(F32)).astype(BF16)
        dst[2, 1:9] = jnp.where(is_bottom[None], bottom, dst[2, 1:9].astype(F32)).astype(BF16)
        for column, side, above, below, at in ((0, 3, 0, 5, 7), (9, 4, 2, 7, 0)):
            value = rim[side, t].astype(F32)
            upper = rim[above, t].astype(F32)[at : at + 1]
            lower = rim[below, t].astype(F32)[at : at + 1]
            dst[0, column] = jnp.where(is_top, upper, pltpu.roll(value, 1, 0)).astype(BF16)
            dst[1, column] = rim[side, t]
            dst[2, column] = jnp.where(is_bottom, lower, pltpu.roll(value, ROWS - 1, 0)).astype(BF16)

    def put_stage(stage, t, value):
        cut = value.reshape(COLS, ROWS, C)
        for side, at in ((0, 0), (1, ROWS - 1)):
            row = cut[:, at, :]
            stage[t, side] = jnp.concatenate([row, row], axis=0).astype(BF16)

    def add_rims(value, rim, t):
        cut = value.reshape(COLS, ROWS, C)
        cut = cut + jnp.where(is_top[None], rim[1, t, 0:8].reshape(COLS, 1, C), 0.0)
        cut = cut + jnp.where(is_bottom[None], rim[6, t, 0:8].reshape(COLS, 1, C), 0.0)
        sides = []
        for side, above, below in ((3, 0, 5), (4, 2, 7)):
            column = rim[side, t] + jnp.where(is_top, rim[above, t, 0:1], 0.0)
            sides.append((column + jnp.where(is_bottom, rim[below, t, 0:1], 0.0))[None])
        cut = jnp.concatenate([cut[0:1] + sides[0], cut[1:7], cut[7:8] + sides[1]], axis=0)
        return cut.reshape(PIX, C)

    def by_columns(value):
        return jnp.transpose(value.astype(F32).reshape(ROWS, COLS, C), (1, 0, 2))

    def by_rows(value):
        return jnp.transpose(value.reshape(COLS, ROWS, C), (1, 0, 2)).reshape(PIX, C).astype(BF16)

    def rim_source(d, store, stage, t):
        dy, dx = DIRS[d]
        if dy < 0:
            return stage.at[t, 0]
        if dy > 0:
            return stage.at[t, 1]
        return store.at[t, 0 if dx < 0 else COLS - 1]

    def send_rims(store, stage, rim, t, send, recv, to_layer, first):
        for d in range(8):
            found, other = there(d)

            @pl.when(found)
            def _(d=d, other=other):
                copy = remote(
                    rim_source(d, store, stage, t), rim.at[7 - d, t], send.at[d], recv.at[7 - d, t], to_layer, other
                )

                @pl.when(jnp.logical_not(first))
                def _():
                    copy.wait_send()

                copy.start()

    def end_rims(store, stage, rim, send, recv):
        for d in range(8):
            found, other = there(d)

            @pl.when(found)
            def _(d=d, other=other):
                remote(
                    rim_source(d, store, stage, 0), rim.at[7 - d, 0], send.at[d], recv.at[7 - d, 0], layer, other
                ).wait_send()

    def wait_rims(rim, t, send, recv):
        for d in range(8):
            found, other = there(d)

            @pl.when(found)
            def _(d=d, other=other):
                remote(rim.at[d, t], rim.at[d, t], send.at[d], recv.at[d, t], layer, other).wait_recv()

    def turn_weight():
        def one(k, _):
            for n in range(2):
                wt[n, k] = w[n, k].T
            return 0

        lax.fori_loop(0, 9, one, 0)

    @pl.when(layer == 0)
    def _():
        pltpu.make_async_copy(frames, gin, in_sem).wait()

        def one(t, _):
            value = by_columns(gin[t])
            xc[t] = value.astype(BF16)
            put_stage(xst, t, value.reshape(PIX, C))
            send_rims(xc, xst, xrim, t, fr_send, x_recv, layer, t == 0)
            return 0

        lax.fori_loop(0, STEPS, one, 0)
        end_rims(xc, xst, xrim, fr_send, x_recv)

    for copy in w_copies:
        copy.wait()

    @pl.when(layer == 3)
    def _():
        pltpu.make_async_copy(cotangent, gin, in_sem).wait()

        def one(t, _):
            up[t] = by_columns(gin[t]).astype(BF16)
            return 0

        lax.fori_loop(0, STEPS, one, 0)
        turn_weight()

    def mate_patches(t):
        return remote(st.at[t], pst.at[t], ps_send, ps_recv.at[t], layer, mate)

    def above_map(t):
        return remote(hs.at[t], xc.at[t], xs_send.at[8], xc_recv.at[t], layer + 1, tile)

    def patches(t, n):
        taps = [st[t, n, p, q : q + 8].reshape(PIX, C) for p in range(3) for q in range(3)]
        return jnp.concatenate(taps, axis=1)

    def forward(t, _):
        @pl.when(layer > 0)
        def _():
            remote(xc.at[t], xc.at[t], xs_send.at[8], xc_recv.at[t], layer - 1, tile).wait_recv()

        put_centre(st.at[t, 0], xc[t].astype(F32).reshape(PIX, C))
        wait_rims(xrim, t, xs_send, x_recv)
        put_rim(st.at[t, 0], xrim, t)
        sums[...] = jnp.dot(patches(t, 0), w[0].reshape(9 * C, GC), preferred_element_type=F32)

        @pl.when(t > 0)
        def _():
            wait_rims(hrim, t - 1, hs_send, h_recv)
            put_rim(st.at[t, 1], hrim, t - 1)
            mate_patches(t - 1).wait_send()
            sums[...] += jnp.dot(patches(t, 1), w[1].reshape(9 * C, GC), preferred_element_type=F32)

        in_gate = sigmoid(sums[:, 0:C])
        forget = sigmoid(sums[:, C : 2 * C] + FORGET_SHIFT)
        out_gate = sigmoid(sums[:, 2 * C : 3 * C])
        update = jnp.tanh(sums[:, 3 * C :])
        fresh = forget * cell[t] + in_gate * update
        squashed = jnp.tanh(fresh)
        hidden = out_gate * squashed
        hs[t] = hidden.astype(BF16).reshape(COLS, ROWS, C)
        put_stage(hst, t, hidden)

        @pl.when(t < STEPS - 1)
        def _():
            send_rims(hs, hst, hrim, t, hs_send, h_recv, layer, t == 0)

        @pl.when(layer < 3)
        def _():
            @pl.when(t > 0)
            def _():
                above_map(t - 1).wait_send()

            above_map(t).start()
            send_rims(hs, hst, xrim, t, xs_send, x_recv, layer + 1, t == 0)

        mate_patches(t).start()
        act[t, :, 0:C] = in_gate
        act[t, :, C : 2 * C] = forget
        act[t, :, 2 * C : 3 * C] = out_gate
        act[t, :, 3 * C :] = update
        cell[t + 1] = fresh
        squash[t] = squashed
        hrow[t] = by_rows(hidden)

        @pl.when(t < STEPS - 1)
        def _():
            put_centre(st.at[t + 1, 1], hidden)

        return 0

    lax.fori_loop(0, STEPS, forward, 0)
    mate_patches(STEPS - 1).wait_send()
    end_rims(hs, hst, hrim, hs_send, h_recv)

    hid_copy = pltpu.make_async_copy(hrow, hid_out, out_sem.at[0])
    hid_copy.start()

    @pl.when(layer < 3)
    def _():
        turn_weight()
        above_map(STEPS - 1).wait_send()
        end_rims(hs, hst, xrim, xs_send, x_recv)

    mine = pl.ds(pl.multiple_of(core * 512, 512), 512)
    theirs = pl.ds(pl.multiple_of((1 - core) * 512, 512), 512)

    def mate_gates(t):
        return remote(gates.at[t, :, theirs], pg.at[t], pg_send, pg_recv.at[t], layer, mate)

    def weight_terms(t, n, p, q):
        lhs = jnp.concatenate(
            [st[t, n, p, q : q + 8].reshape(PIX, C), pst[t, n, p, q : q + 8].reshape(PIX, C)], axis=0
        )
        rhs = jnp.concatenate([gates[t, :, mine], pg[t]], axis=0)
        return lax.dot_general(lhs, rhs, (((0,), (0,)), ((), ())), preferred_element_type=F32)

    def wait_mate(t):
        mate_patches(t).wait_recv()
        mate_gates(t).wait_recv()

    def below_grad(t):
        return remote(gown.at[t], up.at[t], us_send.at[8], u_recv.at[t], layer - 1, tile)

    def spread_out(t, n, stage):
        for p in range(3):
            for q in range(3):
                term = jnp.dot(gates[t], wt[n, 3 * p + q], preferred_element_type=F32)
                if q == 0:
                    spread[p, 0:PIX] = term
                    spread[p, PIX:] = jnp.zeros((2 * ROWS, C), F32)
                else:
                    spread[p, ROWS * q : ROWS * q + PIX] += term
        row = lax.rem(lax.broadcasted_iota(jnp.int32, (PIX + 2 * ROWS, 1), 0), ROWS)
        upper, lower = spread[0], spread[2]
        centre = spread[1] + jnp.where(row == ROWS - 1, 0.0, pltpu.roll(upper, PIX + 2 * ROWS - 1, 0))
        centre = centre + jnp.where(row == 0, 0.0, pltpu.roll(lower, 1, 0))
        stage[1, 0:8] = upper.reshape(COLS + 2, ROWS, C)[1:9, 0, :]
        stage[6, 0:8] = lower.reshape(COLS + 2, ROWS, C)[1:9, ROWS - 1, :]
        stage[3] = centre[0:ROWS]
        stage[4] = centre[PIX + ROWS :]
        for d, source, at in ((0, upper, 0), (2, upper, PIX + ROWS), (5, lower, ROWS - 1), (7, lower, PIX + 2 * ROWS - 1)):
            stage[d, 0:8] = jnp.broadcast_to(source[at : at + 1], (8, C))
        return centre[ROWS : PIX + ROWS]

    def rim_copies(stage, rim, t, send, recv, to_layer, act_on):
        for d in range(8):
            found, other = there(d)
            rows = pl.ds(0, ROWS if d in (3, 4) else 8)

            @pl.when(found)
            def _(d=d, other=other, rows=rows):
                act_on(remote(
                    stage.at[d, rows], rim.at[7 - d, t, rows], send.at[d], recv.at[7 - d, t], to_layer, other
                ))

    def rim_arrivals(rim, t, send, recv):
        for d in range(8):
            found, other = there(d)
            rows = pl.ds(0, ROWS if d in (3, 4) else 8)

            @pl.when(found)
            def _(d=d, other=other, rows=rows):
                here = rim.at[d, t, rows]
                remote(here, here, send.at[d], recv.at[d, t], layer, other).wait_recv()

    def begin(copy):
        copy.start()

    def settle(copy):
        copy.wait_send()

    def settle_inputs(t):
        rim_copies(gstage, grim, t, gs_send, g_recv_rim, layer, settle)

        @pl.when(layer > 0)
        def _():
            below_grad(t).wait_send()
            rim_copies(gstage, urim, t, us_send, u_recv_rim, layer - 1, settle)

    def finish_inputs(t):
        rim_arrivals(grim, t, gs_send, g_recv_rim)
        gin[t] = by_rows(add_rims(gsum[t], grim, t))

    @pl.when(layer == 3)
    def _():
        urim[...] = jnp.zeros_like(urim)

    def backward(i, _):
        t = STEPS - 1 - i

        @pl.when(i > 0)
        def _():
            rim_arrivals(rrim, t + 1, rs_send, r_recv_rim)
            recurrent[...] = add_rims(recurrent[...], rrim, t + 1)

        @pl.when(layer < 3)
        def _():
            remote(up.at[t], up.at[t], us_send.at[8], u_recv.at[t], layer + 1, tile).wait_recv()
            rim_arrivals(urim, t, us_send, u_recv_rim)

        grad_hidden = add_rims(up[t].astype(F32).reshape(PIX, C) + recurrent[...], urim, t)
        in_gate = act[t, :, 0:C]
        forget = act[t, :, C : 2 * C]
        out_gate = act[t, :, 2 * C : 3 * C]
        update = act[t, :, 3 * C :]
        squashed = squash[t]
        grad_cell = grad_hidden * out_gate * (1.0 - squashed * squashed) + carried[...]
        carried[...] = grad_cell * forget
        gates[t, :, 0:C] = (grad_cell * update * in_gate * (1.0 - in_gate)).astype(BF16)
        gates[t, :, C : 2 * C] = (grad_cell * cell[t] * forget * (1.0 - forget)).astype(BF16)
        gates[t, :, 2 * C : 3 * C] = (grad_hidden * squashed * out_gate * (1.0 - out_gate)).astype(BF16)
        gates[t, :, 3 * C :] = (grad_cell * in_gate * (1.0 - update * update)).astype(BF16)

        @pl.when(i > 0)
        def _():
            mate_gates(t + 1).wait_send()

        mate_gates(t).start()

        @pl.when(t > 0)
        def _():
            @pl.when(i > 0)
            def _():
                rim_copies(rstage, rrim, t + 1, rs_send, r_recv_rim, layer, settle)

            recurrent[...] = spread_out(t, 1, rstage)
            rim_copies(rstage, rrim, t, rs_send, r_recv_rim, layer, begin)

        @pl.when(i > 0)
        def _():
            settle_inputs(t + 1)

        own = spread_out(t, 0, gstage)
        gown[t] = own.astype(BF16).reshape(COLS, ROWS, C)

        @pl.when(layer > 0)
        def _():
            below_grad(t).start()
            rim_copies(gstage, urim, t, us_send, u_recv_rim, layer - 1, begin)

        rim_copies(gstage, grim, t, gs_send, g_recv_rim, layer, begin)
        gsum[t] = own

        @pl.when(i > 0)
        def _():
            wait_mate(t + 1)
            for p in range(3):
                for q in range(3):
                    for n in range(2):
                        low = 512 * (3 * p + q) + C * n
                        acc[low : low + C] += weight_terms(t + 1, n, p, q)
            finish_inputs(t + 1)

        return 0

    lax.fori_loop(0, STEPS, backward, 0)
    rim_copies(rstage, rrim, 1, rs_send, r_recv_rim, layer, settle)
    wait_mate(0)
    mate_gates(0).wait_send()
    for p in range(3):
        for q in range(3):
            for n in range(2):
                start = 512 * (3 * p + q) + C * n
                value = (acc[start : start + C] + weight_terms(0, n, p, q)).astype(BF16)
                low = start
                while low < start + C:
                    block = low // ROWS_OUT
                    high = min(start + C, ROWS_OUT * (block + 1))
                    rows = slice(low - ROWS_OUT * block, high - ROWS_OUT * block)
                    z, y = block // 4, block % 4
                    part[0, y, z, rows] = value[low - start : high - start, 0:256]
                    part[1, z, y, rows] = value[low - start : high - start, 256:512]
                    low = high

    def plus(left, right):
        return (left.astype(F32) + right.astype(F32)).astype(BF16)

    def own(n):
        return (ypos, trow) if n == 0 else (trow, ypos)

    rights, lefts = (2, 1), (3, 0)
    sent = []

    def go(copy):
        copy.start()
        sent.append(copy)
        return copy

    def hop(n, first, to_right):
        return at_ring((n == 0) == first, 1 if to_right else 3)

    hand = {}
    full = {}
    for n in range(2):
        a, b = own(n)
        for m in range(2):
            for right in (True, False):
                j = (rights if right else lefts)[m]
                hand[n, m, right] = go(remote(
                    part.at[n, lax.rem(a + 2, 4), lax.rem(b + j, 4)], (from_l if right else from_r).at[n, m],
                    t_send.at[n, m, int(right)], t_recv.at[n, m, int(right)], layer, hop(n, True, right),
                ))

    def send_full(n, j, right):
        a, b = own(n)
        full[n, j, right] = go(remote(
            part.at[n, lax.rem(a + (1 if right else 3), 4), lax.rem(b + j, 4)], (full_l if right else full_r).at[n, j],
            f_send.at[n, j, int(right)], f_recv.at[n, j, int(right)], layer, hop(n, True, right),
        ))

    for m in range(2):
        for n in range(2):
            send_full(n, lefts[m], True)
            send_full(n, rights[m], False)
    finish_inputs(0)
    gin_copy = pltpu.make_async_copy(gin, gin_out, out_sem.at[1])
    gin_copy.start()
    settle_inputs(0)
    for m in range(2):
        for n in range(2):
            a, b = own(n)
            for right in (True, False):
                j = (rights if right else lefts)[m]
                hand[n, m, right].wait_recv()
                to = (n, lax.rem(a + (1 if right else 3), 4), lax.rem(b + j, 4))
                part[to] = plus(part[to], (from_l if right else from_r)[n, m])
                send_full(n, j, right)

    def gather(n, j):
        a, b = own(n)
        full[n, j, True].wait_recv()
        full[n, j, False].wait_recv()
        total[n, j] = (
            part[n, a, lax.rem(b + j, 4)].astype(F32) + full_l[n, j].astype(F32) + full_r[n, j].astype(F32)
        ).astype(BF16)

    upper, lower = pl.ds(0, HALF), pl.ds(HALF, HALF)
    hand2 = {}
    full2 = {}

    def send_full2(n, right, first):
        rows = lower if right == first else upper
        full2[n, right, first] = go(remote(
            total.at[n, 1 if right else 3, rows], (full2_l if right else full2_r).at[n, rows],
            f2_send.at[n, int(right), int(first)], f2_recv.at[n, int(right), int(first)], layer, hop(n, False, right),
        ))

    for n in range(2):
        gather(n, 2)
        for right in (True, False):
            hand2[n, right] = go(remote(
                total.at[n, 2, upper if right else lower], (from2_l if right else from2_r).at[n],
                t2_send.at[n, int(right)], t2_recv.at[n, int(right)], layer, hop(n, False, right),
            ))
    for right in (True, False):
        for n in range(2):
            gather(n, 1 if right else 3)
            send_full2(n, right, True)
    for n in range(2):
        for right in (True, False):
            hand2[n, right].wait_recv()
            at = (n, 1 if right else 3, upper if right else lower)
            total[at] = plus(total[at], (from2_l if right else from2_r)[n])
            send_full2(n, right, False)
    for n in range(2):
        gather(n, 0)
    for n in range(2):
        for right in (True, False):
            for first in (True, False):
                full2[n, right, first].wait_recv()
        res[:, 256 * n : 256 * n + 256] = plus(
            total[n, 0].astype(F32) + full2_l[n].astype(F32), full2_r[n]
        )
    last = go(remote(
        res.at[pl.ds(pl.multiple_of((1 - core) * HALF, HALF), HALF)], pres, r_send, r_recv, layer, mate
    ))
    wg_out[:, mine] = res[pl.ds(pl.multiple_of(core * HALF, HALF), HALF), :].astype(F32)
    last.wait_recv()
    wg_out[:, theirs] = pres[...].astype(F32)
    for copy in sent:
        copy.wait_send()
    hid_copy.wait()
    gin_copy.wait()


def copy_out(a, b, c, a_out, b_out, c_out, sem):
    copies = [pltpu.make_async_copy(*pair, sem.at[n]) for n, pair in enumerate(((a, a_out), (b, b_out), (c, c_out)))]
    for copy in copies:
        copy.start()
    for copy in copies:
        copy.wait()


def local(frames, weight, cotangent):
    maps = jax.ShapeDtypeStruct((STEPS, PIX, C), BF16)
    vmem = pltpu.VMEM
    dma = pltpu.SemaphoreType.DMA
    shape = (STEPS, COLS, ROWS, C)
    block = (ROWS_OUT, 256)
    hidden, grads, weight_grad = pl.pallas_call(
        kernel,
        out_shape=(maps, maps, jax.ShapeDtypeStruct((HALF, GC), F32)),
        in_specs=[pl.BlockSpec(memory_space=pl.ANY)] * 3,
        out_specs=(
            pl.BlockSpec(memory_space=pl.ANY),
            pl.BlockSpec(memory_space=pl.ANY),
            pl.BlockSpec(memory_space=pltpu.VMEM),
        ),
        scratch_shapes=[
            vmem((2, 9, C, GC), BF16),
            vmem((2, 9, GC, C), BF16),
            vmem((4608, 512), F32),
            vmem(shape, BF16),
            vmem((STEPS, 2, ROWS, C), BF16),
            vmem((8, STEPS, ROWS, C), BF16),
            vmem(shape, BF16),
            vmem((STEPS, 2, ROWS, C), BF16),
            vmem((8, STEPS, ROWS, C), BF16),
            vmem((STEPS, 2, 3, COLS + 2, ROWS, C), BF16),
            vmem((STEPS, 2, 3, COLS + 2, ROWS, C), BF16),
            vmem((STEPS, PIX, GC), F32),
            vmem((STEPS + 1, PIX, C), F32),
            vmem((STEPS, PIX, C), F32),
            vmem(shape, BF16),
            vmem((STEPS, PIX, GC), BF16),
            vmem((STEPS, PIX, 512), BF16),
            vmem((STEPS, PIX, C), BF16),
            vmem((STEPS, PIX, C), BF16),
            vmem((8, STEPS, ROWS, C), F32),
            vmem((8, STEPS, ROWS, C), F32),
            vmem((8, STEPS, ROWS, C), F32),
            vmem((8, ROWS, C), F32),
            vmem((8, ROWS, C), F32),
            vmem(shape, BF16),
            vmem((STEPS, PIX, C), F32),
            vmem((3, PIX + 2 * ROWS, C), F32),
            vmem((PIX, C), F32),
            vmem((PIX, C), F32),
            vmem((PIX, GC), F32),
            vmem((2, 4, 4) + block, BF16),
            vmem((2, 2) + block, BF16),
            vmem((2, 2) + block, BF16),
            vmem((2, 4) + block, BF16),
            vmem((2, 4) + block, BF16),
            vmem((2, 4) + block, BF16),
            vmem((2, HALF, 256), BF16),
            vmem((2, HALF, 256), BF16),
            vmem((2,) + block, BF16),
            vmem((2,) + block, BF16),
            vmem((ROWS_OUT, 512), BF16),
            vmem((HALF, 512), BF16),
            dma((2,)), dma, dma((2,)),
            dma((9,)), dma((8,)), dma((8,)), dma((8,)), dma((9,)), dma((8,)), dma, dma,
            dma((STEPS,)), dma((8, STEPS)), dma((8, STEPS)),
            dma((8, STEPS)), dma((8, STEPS)), dma((8, STEPS)),
            dma((STEPS,)), dma((STEPS,)), dma((STEPS,)),
            dma((2, 2, 2)), dma((2, 2, 2)), dma((2, 4, 2)), dma((2, 4, 2)),
            dma((2, 2)), dma((2, 2)), dma((2, 2, 2)), dma((2, 2, 2)), dma, dma,
        ],
        compiler_params=pltpu.CompilerParams(
            collective_id=0, has_side_effects=True, vmem_limit_bytes=63 * 2**20
        ),
    )(
        frames.reshape(STEPS, PIX, C),
        weight.reshape(9, 2, C, GC),
        cotangent.reshape(STEPS, PIX, C),
    )
    hidden, grads, weight_grad = pl.pallas_call(
        copy_out,
        out_shape=(maps, maps, jax.ShapeDtypeStruct((HALF, GC), F32)),
        in_specs=[pl.BlockSpec(memory_space=pl.ANY)] * 3,
        out_specs=(pl.BlockSpec(memory_space=pl.ANY),) * 3,
        scratch_shapes=[dma((3,))],
    )(hidden, grads, weight_grad)
    tiled = (1, STEPS, 1, ROWS, COLS, C)
    return hidden.reshape(tiled), grads.reshape(tiled), weight_grad[None]


def solution(mesh):
    in_specs = (
        P(None, "tile", None, None, None),
        P("layer", None, None),
        P(None, "tile", None, None, None),
    )
    out_specs = (
        P("layer", None, "tile", None, None, None),
        P("layer", None, "tile", None, None, None),
        P("layer", "tile", None),
    )
    return jax.shard_map(local, mesh=mesh, in_specs=in_specs, out_specs=out_specs, check_vma=False)
```

```python
import jax
import jax.numpy as jnp
from jax import lax
from jax.experimental import pallas as pl
from jax.experimental.pallas import tpu as pltpu
from jax.sharding import PartitionSpec as P

MESH = pl.DeviceIdType.MESH
F32 = jnp.float32
BF16 = jnp.bfloat16

C = 256
GC = 1024
STEPS = 6
COLS = 8
ROWS = 16
PIX = COLS * ROWS
ROWS_OUT = 288
HALF = 144
FORGET_SHIFT = 1.0
DIRS = ((-1, -1), (-1, 0), (-1, 1), (0, -1), (0, 1), (1, -1), (1, 0), (1, 1))


def sigmoid(value):
    return 0.5 * jnp.tanh(0.5 * value) + 0.5


def kernel(
    frames, weight, cotangent, hid_out, gin_out, wg_out,
    w, wt, acc, xc, xst, xrim, hs, hst, hrim, st, pst, act, cell, squash, up, gates, pg, hrow, gin,
    rrim, urim, grim, rstage, gstage, gown, gsum, spread,
    recurrent, carried, sums, part, from_l, from_r, full_l, full_r, total, from2_l, from2_r, full2_l, full2_r, res, pres,
    w_sem, in_sem, out_sem, xs_send, fr_send, hs_send, rs_send, us_send, gs_send, ps_send, pg_send,
    xc_recv, x_recv, h_recv, r_recv_rim, u_recv_rim, g_recv_rim, u_recv, ps_recv, pg_recv,
    t_send, t_recv, f_send, f_recv, t2_send, t2_recv, f2_send, f2_recv, r_send, r_recv,
):
    layer = lax.axis_index("layer")
    tile = lax.axis_index("tile")
    trow, tcol = tile // 8, lax.rem(tile, 8)
    ypos, core = tcol // 2, lax.rem(tcol, 2)
    mate = tile + 1 - 2 * core

    def there(d):
        dy, dx = DIRS[d]
        found = jnp.bool_(True)
        if dy < 0:
            found = found & (trow > 0)
        if dy > 0:
            found = found & (trow < 3)
        if dx < 0:
            found = found & (tcol > 0)
        if dx > 0:
            found = found & (tcol < 7)
        return found, tile + 8 * dy + dx

    def remote(src, dst, send, recv, to_layer, to_tile):
        return pltpu.make_async_remote_copy(
            src_ref=src, dst_ref=dst, send_sem=send, recv_sem=recv,
            device_id={"layer": to_layer, "tile": to_tile}, device_id_type=MESH,
        )

    def at_ring(along_y, step):
        if along_y:
            return trow * 8 + lax.rem(ypos + step, 4) * 2 + core
        return lax.rem(trow + step, 4) * 8 + tcol

    @pl.when(layer == 0)
    def _():
        pltpu.make_async_copy(frames, gin, in_sem).start()

    @pl.when(layer == 3)
    def _():
        pltpu.make_async_copy(cotangent, gin, in_sem).start()

    w_copies = [pltpu.make_async_copy(weight.at[:, n], w.at[n], w_sem.at[n]) for n in range(2)]
    for copy in w_copies:
        copy.start()

    barrier = pltpu.get_barrier_semaphore()
    expected = jnp.int32(0)

    def greet(found, to_layer, to_tile):
        @pl.when(found)
        def _():
            pl.semaphore_signal(barrier, inc=1, device_id={"layer": to_layer, "tile": to_tile}, device_id_type=MESH)

        return found.astype(jnp.int32)

    for d in range(8):
        found, other = there(d)
        expected += greet(found, layer, other)
        expected += greet(found & (layer > 0), layer - 1, other)
        expected += greet(found & (layer < 3), layer + 1, other)
    expected += greet(layer > 0, layer - 1, tile)
    expected += greet(layer < 3, layer + 1, tile)
    for along_y in (True, False):
        for step in (1, 3):
            expected += greet(jnp.bool_(True), layer, at_ring(along_y, step))

    acc[...] = jnp.zeros_like(acc)
    recurrent[...] = jnp.zeros_like(recurrent)
    carried[...] = jnp.zeros_like(carried)
    cell[0] = jnp.zeros((PIX, C), F32)
    st[0, 1] = jnp.zeros((3, COLS + 2, ROWS, C), BF16)
    for d in range(8):
        found, _ = there(d)

        @pl.when(jnp.logical_not(found))
        def _(d=d):
            xrim[d] = jnp.zeros((STEPS, ROWS, C), BF16)
            hrim[d] = jnp.zeros((STEPS, ROWS, C), BF16)
            rrim[d] = jnp.zeros((STEPS, ROWS, C), F32)
            urim[d] = jnp.zeros((STEPS, ROWS, C), F32)
            grim[d] = jnp.zeros((STEPS, ROWS, C), F32)

    pl.semaphore_wait(barrier, expected)

    pixel_row = lax.broadcasted_iota(jnp.int32, (ROWS, 1), 0)
    is_top = pixel_row == 0
    is_bottom = pixel_row == ROWS - 1

    def put_centre(dst, value):
        dst[0, 1:9] = pltpu.roll(value, 1, 0).astype(BF16).reshape(COLS, ROWS, C)
        dst[1, 1:9] = value.astype(BF16).reshape(COLS, ROWS, C)
        dst[2, 1:9] = pltpu.roll(value, PIX - 1, 0).astype(BF16).reshape(COLS, ROWS, C)

    def put_rim(dst, rim, t):
        top = rim[1, t].astype(F32)[0:8].reshape(COLS, 1, C)
        bottom = rim[6, t].astype(F32)[0:8].reshape(COLS, 1, C)
        dst[0, 1:9] = jnp.where(is_top[None], top, dst[0, 1:9].astype(F32)).astype(BF16)
        dst[2, 1:9] = jnp.where(is_bottom[None], bottom, dst[2, 1:9].astype(F32)).astype(BF16)
        for column, side, above, below, at in ((0, 3, 0, 5, 7), (9, 4, 2, 7, 0)):
            value = rim[side, t].astype(F32)
            upper = rim[above, t].astype(F32)[at : at + 1]
            lower = rim[below, t].astype(F32)[at : at + 1]
            dst[0, column] = jnp.where(is_top, upper, pltpu.roll(value, 1, 0)).astype(BF16)
            dst[1, column] = rim[side, t]
            dst[2, column] = jnp.where(is_bottom, lower, pltpu.roll(value, ROWS - 1, 0)).astype(BF16)

    def put_stage(stage, t, value):
        cut = value.reshape(COLS, ROWS, C)
        for side, at in ((0, 0), (1, ROWS - 1)):
            row = cut[:, at, :]
            stage[t, side] = jnp.concatenate([row, row], axis=0).astype(BF16)

    def add_rims(value, rim, t):
        cut = value.reshape(COLS, ROWS, C)
        cut = cut + jnp.where(is_top[None], rim[1, t, 0:8].reshape(COLS, 1, C), 0.0)
        cut = cut + jnp.where(is_bottom[None], rim[6, t, 0:8].reshape(COLS, 1, C), 0.0)
        sides = []
        for side, above, below in ((3, 0, 5), (4, 2, 7)):
            column = rim[side, t] + jnp.where(is_top, rim[above, t, 0:1], 0.0)
            sides.append((column + jnp.where(is_bottom, rim[below, t, 0:1], 0.0))[None])
        cut = jnp.concatenate([cut[0:1] + sides[0], cut[1:7], cut[7:8] + sides[1]], axis=0)
        return cut.reshape(PIX, C)

    def by_columns(value):
        return jnp.transpose(value.astype(F32).reshape(ROWS, COLS, C), (1, 0, 2))

    def by_rows(value):
        return jnp.transpose(value.reshape(COLS, ROWS, C), (1, 0, 2)).reshape(PIX, C).astype(BF16)

    def rim_source(d, store, stage, t):
        dy, dx = DIRS[d]
        if dy < 0:
            return stage.at[t, 0]
        if dy > 0:
            return stage.at[t, 1]
        return store.at[t, 0 if dx < 0 else COLS - 1]

    def send_rims(store, stage, rim, t, send, recv, to_layer, first):
        for d in range(8):
            found, other = there(d)

            @pl.when(found)
            def _(d=d, other=other):
                copy = remote(
                    rim_source(d, store, stage, t), rim.at[7 - d, t], send.at[d], recv.at[7 - d, t], to_layer, other
                )

                @pl.when(jnp.logical_not(first))
                def _():
                    copy.wait_send()

                copy.start()

    def end_rims(store, stage, rim, send, recv):
        for d in range(8):
            found, other = there(d)

            @pl.when(found)
            def _(d=d, other=other):
                remote(
                    rim_source(d, store, stage, 0), rim.at[7 - d, 0], send.at[d], recv.at[7 - d, 0], layer, other
                ).wait_send()

    def wait_rims(rim, t, send, recv):
        for d in range(8):
            found, other = there(d)

            @pl.when(found)
            def _(d=d, other=other):
                remote(rim.at[d, t], rim.at[d, t], send.at[d], recv.at[d, t], layer, other).wait_recv()

    def turn_weight():
        def one(k, _):
            for n in range(2):
                wt[n, k] = w[n, k].T
            return 0

        lax.fori_loop(0, 9, one, 0)

    @pl.when(layer == 0)
    def _():
        pltpu.make_async_copy(frames, gin, in_sem).wait()

        def one(t, _):
            value = by_columns(gin[t])
            xc[t] = value.astype(BF16)
            put_stage(xst, t, value.reshape(PIX, C))
            send_rims(xc, xst, xrim, t, fr_send, x_recv, layer, t == 0)
            return 0

        lax.fori_loop(0, STEPS, one, 0)
        end_rims(xc, xst, xrim, fr_send, x_recv)

    for copy in w_copies:
        copy.wait()

    @pl.when(layer == 3)
    def _():
        pltpu.make_async_copy(cotangent, gin, in_sem).wait()

        def one(t, _):
            up[t] = by_columns(gin[t]).astype(BF16)
            return 0

        lax.fori_loop(0, STEPS, one, 0)
        turn_weight()

    def mate_patches(t):
        return remote(st.at[t], pst.at[t], ps_send, ps_recv.at[t], layer, mate)

    def above_map(t):
        return remote(hs.at[t], xc.at[t], xs_send.at[8], xc_recv.at[t], layer + 1, tile)

    def patches(t, n):
        taps = [st[t, n, p, q : q + 8].reshape(PIX, C) for p in range(3) for q in range(3)]
        return jnp.concatenate(taps, axis=1)

    def forward(t, _):
        @pl.when(layer > 0)
        def _():
            remote(xc.at[t], xc.at[t], xs_send.at[8], xc_recv.at[t], layer - 1, tile).wait_recv()

        put_centre(st.at[t, 0], xc[t].astype(F32).reshape(PIX, C))
        wait_rims(xrim, t, xs_send, x_recv)
        put_rim(st.at[t, 0], xrim, t)
        sums[...] = jnp.dot(patches(t, 0), w[0].reshape(9 * C, GC), preferred_element_type=F32)

        @pl.when(t > 0)
        def _():
            wait_rims(hrim, t - 1, hs_send, h_recv)
            put_rim(st.at[t, 1], hrim, t - 1)
            mate_patches(t - 1).wait_send()
            sums[...] += jnp.dot(patches(t, 1), w[1].reshape(9 * C, GC), preferred_element_type=F32)

        in_gate = sigmoid(sums[:, 0:C])
        forget = sigmoid(sums[:, C : 2 * C] + FORGET_SHIFT)
        out_gate = sigmoid(sums[:, 2 * C : 3 * C])
        update = jnp.tanh(sums[:, 3 * C :])
        fresh = forget * cell[t] + in_gate * update
        squashed = jnp.tanh(fresh)
        hidden = out_gate * squashed
        hs[t] = hidden.astype(BF16).reshape(COLS, ROWS, C)
        put_stage(hst, t, hidden)

        @pl.when(t < STEPS - 1)
        def _():
            send_rims(hs, hst, hrim, t, hs_send, h_recv, layer, t == 0)

        @pl.when(layer < 3)
        def _():
            @pl.when(t > 0)
            def _():
                above_map(t - 1).wait_send()

            above_map(t).start()
            send_rims(hs, hst, xrim, t, xs_send, x_recv, layer + 1, t == 0)

        mate_patches(t).start()
        act[t, :, 0:C] = in_gate
        act[t, :, C : 2 * C] = forget
        act[t, :, 2 * C : 3 * C] = out_gate
        act[t, :, 3 * C :] = update
        cell[t + 1] = fresh
        squash[t] = squashed
        hrow[t] = by_rows(hidden)

        @pl.when(t < STEPS - 1)
        def _():
            put_centre(st.at[t + 1, 1], hidden)

        return 0

    lax.fori_loop(0, STEPS, forward, 0)
    mate_patches(STEPS - 1).wait_send()
    end_rims(hs, hst, hrim, hs_send, h_recv)

    hid_copy = pltpu.make_async_copy(hrow, hid_out, out_sem.at[0])
    hid_copy.start()

    @pl.when(layer < 3)
    def _():
        turn_weight()
        above_map(STEPS - 1).wait_send()
        end_rims(hs, hst, xrim, xs_send, x_recv)

    mine = pl.ds(pl.multiple_of(core * 512, 512), 512)
    theirs = pl.ds(pl.multiple_of((1 - core) * 512, 512), 512)

    def mate_gates(t):
        return remote(gates.at[t, :, theirs], pg.at[t], pg_send, pg_recv.at[t], layer, mate)

    def weight_terms(t, n, p, q):
        lhs = jnp.concatenate(
            [st[t, n, p, q : q + 8].reshape(PIX, C), pst[t, n, p, q : q + 8].reshape(PIX, C)], axis=0
        )
        rhs = jnp.concatenate([gates[t, :, mine], pg[t]], axis=0)
        return lax.dot_general(lhs, rhs, (((0,), (0,)), ((), ())), preferred_element_type=F32)

    def wait_mate(t):
        mate_patches(t).wait_recv()
        mate_gates(t).wait_recv()

    def below_grad(t):
        return remote(gown.at[t], up.at[t], us_send.at[8], u_recv.at[t], layer - 1, tile)

    def spread_out(t, n, stage):
        for p in range(3):
            for q in range(3):
                term = jnp.dot(gates[t], wt[n, 3 * p + q], preferred_element_type=F32)
                if q == 0:
                    spread[p, 0:PIX] = term
                    spread[p, PIX:] = jnp.zeros((2 * ROWS, C), F32)
                else:
                    spread[p, ROWS * q : ROWS * q + PIX] += term
        row = lax.rem(lax.broadcasted_iota(jnp.int32, (PIX + 2 * ROWS, 1), 0), ROWS)
        upper, lower = spread[0], spread[2]
        centre = spread[1] + jnp.where(row == ROWS - 1, 0.0, pltpu.roll(upper, PIX + 2 * ROWS - 1, 0))
        centre = centre + jnp.where(row == 0, 0.0, pltpu.roll(lower, 1, 0))
        stage[1, 0:8] = upper.reshape(COLS + 2, ROWS, C)[1:9, 0, :]
        stage[6, 0:8] = lower.reshape(COLS + 2, ROWS, C)[1:9, ROWS - 1, :]
        stage[3] = centre[0:ROWS]
        stage[4] = centre[PIX + ROWS :]
        for d, source, at in ((0, upper, 0), (2, upper, PIX + ROWS), (5, lower, ROWS - 1), (7, lower, PIX + 2 * ROWS - 1)):
            stage[d, 0:8] = jnp.broadcast_to(source[at : at + 1], (8, C))
        return centre[ROWS : PIX + ROWS]

    def rim_copies(stage, rim, t, send, recv, to_layer, act_on):
        for d in range(8):
            found, other = there(d)
            rows = pl.ds(0, ROWS if d in (3, 4) else 8)

            @pl.when(found)
            def _(d=d, other=other, rows=rows):
                act_on(remote(
                    stage.at[d, rows], rim.at[7 - d, t, rows], send.at[d], recv.at[7 - d, t], to_layer, other
                ))

    def rim_arrivals(rim, t, send, recv):
        for d in range(8):
            found, other = there(d)
            rows = pl.ds(0, ROWS if d in (3, 4) else 8)

            @pl.when(found)
            def _(d=d, other=other, rows=rows):
                here = rim.at[d, t, rows]
                remote(here, here, send.at[d], recv.at[d, t], layer, other).wait_recv()

    def begin(copy):
        copy.start()

    def settle(copy):
        copy.wait_send()

    def settle_inputs(t):
        rim_copies(gstage, grim, t, gs_send, g_recv_rim, layer, settle)

        @pl.when(layer > 0)
        def _():
            below_grad(t).wait_send()
            rim_copies(gstage, urim, t, us_send, u_recv_rim, layer - 1, settle)

    def finish_inputs(t):
        rim_arrivals(grim, t, gs_send, g_recv_rim)
        gin[t] = by_rows(add_rims(gsum[t], grim, t))

    @pl.when(layer == 3)
    def _():
        urim[...] = jnp.zeros_like(urim)

    def backward(i, _):
        t = STEPS - 1 - i

        @pl.when(i > 0)
        def _():
            rim_arrivals(rrim, t + 1, rs_send, r_recv_rim)
            recurrent[...] = add_rims(recurrent[...], rrim, t + 1)

        @pl.when(layer < 3)
        def _():
            remote(up.at[t], up.at[t], us_send.at[8], u_recv.at[t], layer + 1, tile).wait_recv()
            rim_arrivals(urim, t, us_send, u_recv_rim)

        grad_hidden = add_rims(up[t].astype(F32).reshape(PIX, C) + recurrent[...], urim, t)
        in_gate = act[t, :, 0:C]
        forget = act[t, :, C : 2 * C]
        out_gate = act[t, :, 2 * C : 3 * C]
        update = act[t, :, 3 * C :]
        squashed = squash[t]
        grad_cell = grad_hidden * out_gate * (1.0 - squashed * squashed) + carried[...]
        carried[...] = grad_cell * forget
        gates[t, :, 0:C] = (grad_cell * update * in_gate * (1.0 - in_gate)).astype(BF16)
        gates[t, :, C : 2 * C] = (grad_cell * cell[t] * forget * (1.0 - forget)).astype(BF16)
        gates[t, :, 2 * C : 3 * C] = (grad_hidden * squashed * out_gate * (1.0 - out_gate)).astype(BF16)
        gates[t, :, 3 * C :] = (grad_cell * in_gate * (1.0 - update * update)).astype(BF16)

        @pl.when(i > 0)
        def _():
            mate_gates(t + 1).wait_send()

        mate_gates(t).start()

        @pl.when(t > 0)
        def _():
            @pl.when(i > 0)
            def _():
                rim_copies(rstage, rrim, t + 1, rs_send, r_recv_rim, layer, settle)

            recurrent[...] = spread_out(t, 1, rstage)
            rim_copies(rstage, rrim, t, rs_send, r_recv_rim, layer, begin)

        @pl.when(i > 0)
        def _():
            settle_inputs(t + 1)

        own = spread_out(t, 0, gstage)
        gown[t] = own.astype(BF16).reshape(COLS, ROWS, C)

        @pl.when(layer > 0)
        def _():
            below_grad(t).start()
            rim_copies(gstage, urim, t, us_send, u_recv_rim, layer - 1, begin)

        rim_copies(gstage, grim, t, gs_send, g_recv_rim, layer, begin)
        gsum[t] = own

        @pl.when(i > 0)
        def _():
            wait_mate(t + 1)
            for p in range(3):
                for q in range(3):
                    for n in range(2):
                        low = 512 * (3 * p + q) + C * n
                        acc[low : low + C] += weight_terms(t + 1, n, p, q)
            finish_inputs(t + 1)

        return 0

    lax.fori_loop(0, STEPS, backward, 0)
    rim_copies(rstage, rrim, 1, rs_send, r_recv_rim, layer, settle)
    wait_mate(0)
    mate_gates(0).wait_send()
    for p in range(3):
        for q in range(3):
            for n in range(2):
                start = 512 * (3 * p + q) + C * n
                value = (acc[start : start + C] + weight_terms(0, n, p, q)).astype(BF16)
                low = start
                while low < start + C:
                    block = low // ROWS_OUT
                    high = min(start + C, ROWS_OUT * (block + 1))
                    rows = slice(low - ROWS_OUT * block, high - ROWS_OUT * block)
                    z, y = block // 4, block % 4
                    part[0, y, z, rows] = value[low - start : high - start, 0:256]
                    part[1, z, y, rows] = value[low - start : high - start, 256:512]
                    low = high

    def plus(left, right):
        return (left.astype(F32) + right.astype(F32)).astype(BF16)

    def own(n):
        return (ypos, trow) if n == 0 else (trow, ypos)

    rights, lefts = (2, 1), (3, 0)
    sent = []

    def go(copy):
        copy.start()
        sent.append(copy)
        return copy

    def hop(n, first, to_right):
        return at_ring((n == 0) == first, 1 if to_right else 3)

    hand = {}
    full = {}
    for n in range(2):
        a, b = own(n)
        for m in range(2):
            for right in (True, False):
                j = (rights if right else lefts)[m]
                hand[n, m, right] = go(remote(
                    part.at[n, lax.rem(a + 2, 4), lax.rem(b + j, 4)], (from_l if right else from_r).at[n, m],
                    t_send.at[n, m, int(right)], t_recv.at[n, m, int(right)], layer, hop(n, True, right),
                ))

    def send_full(n, j, right):
        a, b = own(n)
        full[n, j, right] = go(remote(
            part.at[n, lax.rem(a + (1 if right else 3), 4), lax.rem(b + j, 4)], (full_l if right else full_r).at[n, j],
            f_send.at[n, j, int(right)], f_recv.at[n, j, int(right)], layer, hop(n, True, right),
        ))

    for m in range(2):
        for n in range(2):
            send_full(n, lefts[m], True)
            send_full(n, rights[m], False)
    finish_inputs(0)
    gin_copy = pltpu.make_async_copy(gin, gin_out, out_sem.at[1])
    gin_copy.start()
    settle_inputs(0)
    for m in range(2):
        for n in range(2):
            a, b = own(n)
            for right in (True, False):
                j = (rights if right else lefts)[m]
                hand[n, m, right].wait_recv()
                to = (n, lax.rem(a + (1 if right else 3), 4), lax.rem(b + j, 4))
                part[to] = plus(part[to], (from_l if right else from_r)[n, m])
                send_full(n, j, right)

    def gather(n, j):
        a, b = own(n)
        full[n, j, True].wait_recv()
        full[n, j, False].wait_recv()
        total[n, j] = (
            part[n, a, lax.rem(b + j, 4)].astype(F32) + full_l[n, j].astype(F32) + full_r[n, j].astype(F32)
        ).astype(BF16)

    upper, lower = pl.ds(0, HALF), pl.ds(HALF, HALF)
    hand2 = {}
    full2 = {}

    def send_full2(n, right, first):
        rows = lower if right == first else upper
        full2[n, right, first] = go(remote(
            total.at[n, 1 if right else 3, rows], (full2_l if right else full2_r).at[n, rows],
            f2_send.at[n, int(right), int(first)], f2_recv.at[n, int(right), int(first)], layer, hop(n, False, right),
        ))

    for n in range(2):
        gather(n, 2)
        for right in (True, False):
            hand2[n, right] = go(remote(
                total.at[n, 2, upper if right else lower], (from2_l if right else from2_r).at[n],
                t2_send.at[n, int(right)], t2_recv.at[n, int(right)], layer, hop(n, False, right),
            ))
    for right in (True, False):
        for n in range(2):
            gather(n, 1 if right else 3)
            send_full2(n, right, True)
    for n in range(2):
        for right in (True, False):
            hand2[n, right].wait_recv()
            at = (n, 1 if right else 3, upper if right else lower)
            total[at] = plus(total[at], (from2_l if right else from2_r)[n])
            send_full2(n, right, False)
    for n in range(2):
        gather(n, 0)
    for n in range(2):
        for right in (True, False):
            for first in (True, False):
                full2[n, right, first].wait_recv()
        res[:, 256 * n : 256 * n + 256] = plus(
            total[n, 0].astype(F32) + full2_l[n].astype(F32), full2_r[n]
        )
    last = go(remote(
        res.at[pl.ds(pl.multiple_of((1 - core) * HALF, HALF), HALF)], pres, r_send, r_recv, layer, mate
    ))
    wg_out[:, mine] = res[pl.ds(pl.multiple_of(core * HALF, HALF), HALF), :].astype(F32)
    last.wait_recv()
    wg_out[:, theirs] = pres[...].astype(F32)
    for copy in sent:
        copy.wait_send()
    hid_copy.wait()
    gin_copy.wait()


def copy_out(a, b, c, a_out, b_out, c_out, a_held, b_held, c_held, in_sem, out_sem):
    ways = ((a, a_held, a_out), (b, b_held, b_out), (c, c_held, c_out))
    come = [pltpu.make_async_copy(way[0], way[1], in_sem.at[n]) for n, way in enumerate(ways)]
    leave = [pltpu.make_async_copy(way[1], way[2], out_sem.at[n]) for n, way in enumerate(ways)]
    for copy in come:
        copy.start()
    for arrived, copy in zip(come, leave):
        arrived.wait()
        copy.start()
    for copy in leave:
        copy.wait()


def local(frames, weight, cotangent):
    maps = jax.ShapeDtypeStruct((STEPS, PIX, C), BF16)
    vmem = pltpu.VMEM
    dma = pltpu.SemaphoreType.DMA
    shape = (STEPS, COLS, ROWS, C)
    block = (ROWS_OUT, 256)
    hidden, grads, weight_grad = pl.pallas_call(
        kernel,
        out_shape=(maps, maps, jax.ShapeDtypeStruct((HALF, GC), F32)),
        in_specs=[pl.BlockSpec(memory_space=pl.ANY)] * 3,
        out_specs=(
            pl.BlockSpec(memory_space=pl.ANY),
            pl.BlockSpec(memory_space=pl.ANY),
            pl.BlockSpec(memory_space=pltpu.VMEM),
        ),
        scratch_shapes=[
            vmem((2, 9, C, GC), BF16),
            vmem((2, 9, GC, C), BF16),
            vmem((4608, 512), F32),
            vmem(shape, BF16),
            vmem((STEPS, 2, ROWS, C), BF16),
            vmem((8, STEPS, ROWS, C), BF16),
            vmem(shape, BF16),
            vmem((STEPS, 2, ROWS, C), BF16),
            vmem((8, STEPS, ROWS, C), BF16),
            vmem((STEPS, 2, 3, COLS + 2, ROWS, C), BF16),
            vmem((STEPS, 2, 3, COLS + 2, ROWS, C), BF16),
            vmem((STEPS, PIX, GC), F32),
            vmem((STEPS + 1, PIX, C), F32),
            vmem((STEPS, PIX, C), F32),
            vmem(shape, BF16),
            vmem((STEPS, PIX, GC), BF16),
            vmem((STEPS, PIX, 512), BF16),
            vmem((STEPS, PIX, C), BF16),
            vmem((STEPS, PIX, C), BF16),
            vmem((8, STEPS, ROWS, C), F32),
            vmem((8, STEPS, ROWS, C), F32),
            vmem((8, STEPS, ROWS, C), F32),
            vmem((8, ROWS, C), F32),
            vmem((8, ROWS, C), F32),
            vmem(shape, BF16),
            vmem((STEPS, PIX, C), F32),
            vmem((3, PIX + 2 * ROWS, C), F32),
            vmem((PIX, C), F32),
            vmem((PIX, C), F32),
            vmem((PIX, GC), F32),
            vmem((2, 4, 4) + block, BF16),
            vmem((2, 2) + block, BF16),
            vmem((2, 2) + block, BF16),
            vmem((2, 4) + block, BF16),
            vmem((2, 4) + block, BF16),
            vmem((2, 4) + block, BF16),
            vmem((2, HALF, 256), BF16),
            vmem((2, HALF, 256), BF16),
            vmem((2,) + block, BF16),
            vmem((2,) + block, BF16),
            vmem((ROWS_OUT, 512), BF16),
            vmem((HALF, 512), BF16),
            dma((2,)), dma, dma((2,)),
            dma((9,)), dma((8,)), dma((8,)), dma((8,)), dma((9,)), dma((8,)), dma, dma,
            dma((STEPS,)), dma((8, STEPS)), dma((8, STEPS)),
            dma((8, STEPS)), dma((8, STEPS)), dma((8, STEPS)),
            dma((STEPS,)), dma((STEPS,)), dma((STEPS,)),
            dma((2, 2, 2)), dma((2, 2, 2)), dma((2, 4, 2)), dma((2, 4, 2)),
            dma((2, 2)), dma((2, 2)), dma((2, 2, 2)), dma((2, 2, 2)), dma, dma,
        ],
        compiler_params=pltpu.CompilerParams(
            collective_id=0, has_side_effects=True, vmem_limit_bytes=63 * 2**20
        ),
    )(
        frames.reshape(STEPS, PIX, C),
        weight.reshape(9, 2, C, GC),
        cotangent.reshape(STEPS, PIX, C),
    )
    hidden, grads, weight_grad = pl.pallas_call(
        copy_out,
        out_shape=(maps, maps, jax.ShapeDtypeStruct((HALF, GC), F32)),
        in_specs=[pl.BlockSpec(memory_space=pl.ANY)] * 3,
        out_specs=(pl.BlockSpec(memory_space=pl.ANY),) * 3,
        scratch_shapes=[vmem((STEPS, PIX, C), BF16), vmem((STEPS, PIX, C), BF16), vmem((HALF, GC), F32), dma((3,)), dma((3,))],
    )(hidden, grads, weight_grad)
    tiled = (1, STEPS, 1, ROWS, COLS, C)
    return hidden.reshape(tiled), grads.reshape(tiled), weight_grad[None]


def solution(mesh):
    in_specs = (
        P(None, "tile", None, None, None),
        P("layer", None, None),
        P(None, "tile", None, None, None),
    )
    out_specs = (
        P("layer", None, "tile", None, None, None),
        P("layer", None, "tile", None, None, None),
        P("layer", "tile", None),
    )
    return jax.shard_map(local, mesh=mesh, in_specs=in_specs, out_specs=out_specs, check_vma=False)
```

```python
import jax
import jax.numpy as jnp
from jax import lax
from jax.experimental import pallas as pl
from jax.experimental.pallas import tpu as pltpu
from jax.sharding import PartitionSpec as P

MESH = pl.DeviceIdType.MESH
F32 = jnp.float32
BF16 = jnp.bfloat16

C = 256
GC = 1024
STEPS = 6
COLS = 8
ROWS = 16
PIX = COLS * ROWS
ROWS_OUT = 288
HALF = 144
FORGET_SHIFT = 1.0
PIECE = ((2, 0), (1, 0), (2, 1), (0, 0), (0, 1), (2, 2), (1, 1), (2, 3))
DIRS = ((-1, -1), (-1, 0), (-1, 1), (0, -1), (0, 1), (1, -1), (1, 0), (1, 1))


def sigmoid(value):
    return 0.5 * jnp.tanh(0.5 * value) + 0.5


def kernel(
    frames, weight, cotangent, hid_out, gin_out, wg_out,
    w, wt, acc, xc, x_rows, x_corners, xrim0, xrim1, xrim2, hs, h_rows, h_corners, hrim0, hrim1, hrim2, st, pst, act, cell, squash, up, gates, pg, hrow, gin,
    rrim0, rrim1, rrim2, urim0, urim1, urim2, grim0, grim1, grim2,
    rstage0, rstage1, rstage2, gstage0, gstage1, gstage2, gown, gsum, spread,
    recurrent, carried, sums, part, from_l, from_r, full_l, full_r, total, from2_l, from2_r, full2_l, full2_r, res, pres,
    w_sem, in_sem, out_sem, xs_send, fr_send, hs_send, rs_send, us_send, gs_send, ps_send, pg_send,
    xc_recv, x_recv, h_recv, r_recv_rim, u_recv_rim, g_recv_rim, u_recv, ps_recv, pg_recv,
    t_send, t_recv, f_send, f_recv, t2_send, t2_recv, f2_send, f2_recv, r_send, r_recv,
):
    xrim, hrim, rrim = (xrim0, xrim1, xrim2), (hrim0, hrim1, hrim2), (rrim0, rrim1, rrim2)
    urim, grim = (urim0, urim1, urim2), (grim0, grim1, grim2)
    rstage, gstage = (rstage0, rstage1, rstage2), (gstage0, gstage1, gstage2)
    layer = lax.axis_index("layer")
    tile = lax.axis_index("tile")
    trow, tcol = tile // 8, lax.rem(tile, 8)
    ypos, core = tcol // 2, lax.rem(tcol, 2)
    mate = tile + 1 - 2 * core

    def there(d):
        dy, dx = DIRS[d]
        found = jnp.bool_(True)
        if dy < 0:
            found = found & (trow > 0)
        if dy > 0:
            found = found & (trow < 3)
        if dx < 0:
            found = found & (tcol > 0)
        if dx > 0:
            found = found & (tcol < 7)
        return found, tile + 8 * dy + dx

    def remote(src, dst, send, recv, to_layer, to_tile):
        return pltpu.make_async_remote_copy(
            src_ref=src, dst_ref=dst, send_sem=send, recv_sem=recv,
            device_id={"layer": to_layer, "tile": to_tile}, device_id_type=MESH,
        )

    def at_ring(along_y, step):
        if along_y:
            return trow * 8 + lax.rem(ypos + step, 4) * 2 + core
        return lax.rem(trow + step, 4) * 8 + tcol

    @pl.when(layer == 0)
    def _():
        pltpu.make_async_copy(frames, gin, in_sem).start()

    @pl.when(layer == 3)
    def _():
        pltpu.make_async_copy(cotangent, gin, in_sem).start()

    w_copies = [pltpu.make_async_copy(weight.at[:, n], w.at[n], w_sem.at[n]) for n in range(2)]
    for copy in w_copies:
        copy.start()

    barrier = pltpu.get_barrier_semaphore()
    expected = jnp.int32(0)

    def greet(found, to_layer, to_tile):
        @pl.when(found)
        def _():
            pl.semaphore_signal(barrier, inc=1, device_id={"layer": to_layer, "tile": to_tile}, device_id_type=MESH)

        return found.astype(jnp.int32)

    for d in range(8):
        found, other = there(d)
        expected += greet(found, layer, other)
        expected += greet(found & (layer > 0), layer - 1, other)
        expected += greet(found & (layer < 3), layer + 1, other)
    expected += greet(layer > 0, layer - 1, tile)
    expected += greet(layer < 3, layer + 1, tile)
    for along_y in (True, False):
        for step in (1, 3):
            expected += greet(jnp.bool_(True), layer, at_ring(along_y, step))

    acc[...] = jnp.zeros_like(acc)
    recurrent[...] = jnp.zeros_like(recurrent)
    carried[...] = jnp.zeros_like(carried)
    cell[0] = jnp.zeros((PIX, C), F32)
    st[0, 1] = jnp.zeros((3, COLS + 2, ROWS, C), BF16)
    for d in range(8):
        found, _ = there(d)

        @pl.when(jnp.logical_not(found))
        def _(d=d):
            kind, n = PIECE[d]
            for rims in (xrim, hrim, rrim, urim, grim):
                rims[kind][n] = jnp.zeros(rims[kind].shape[1:], rims[kind].dtype)

    pl.semaphore_wait(barrier, expected)

    pixel_row = lax.broadcasted_iota(jnp.int32, (ROWS, 1), 0)
    is_top = pixel_row == 0
    is_bottom = pixel_row == ROWS - 1

    def put_centre(dst, value):
        dst[0, 1:9] = pltpu.roll(value, 1, 0).astype(BF16).reshape(COLS, ROWS, C)
        dst[1, 1:9] = value.astype(BF16).reshape(COLS, ROWS, C)
        dst[2, 1:9] = pltpu.roll(value, PIX - 1, 0).astype(BF16).reshape(COLS, ROWS, C)

    def row_of(rims, n, t):
        held = rims[1][n, t].astype(F32)
        if held.shape[1] == C:
            return held
        return jnp.concatenate([held[0:8], held[8:16]], axis=1)

    def corner_of(rims, n, t):
        held = rims[2][n, t]
        return jnp.concatenate([held[0:1], held[1:2]], axis=1)

    def fold_row(row):
        return jnp.concatenate([row[:, 0:128], row[:, 128:256]], axis=0)

    def put_rim(dst, rims, t):
        top = row_of(rims, 0, t).reshape(COLS, 1, C)
        bottom = row_of(rims, 1, t).reshape(COLS, 1, C)
        dst[0, 1:9] = jnp.where(is_top[None], top, dst[0, 1:9].astype(F32)).astype(BF16)
        dst[2, 1:9] = jnp.where(is_bottom[None], bottom, dst[2, 1:9].astype(F32)).astype(BF16)
        for n, column in ((0, 0), (1, 9)):
            value = rims[0][n, t].astype(F32)
            dst[0, column] = jnp.where(is_top, corner_of(rims, n, t), pltpu.roll(value, 1, 0)).astype(BF16)
            dst[1, column] = rims[0][n, t]
            lower = corner_of(rims, n + 2, t)
            dst[2, column] = jnp.where(is_bottom, lower, pltpu.roll(value, ROWS - 1, 0)).astype(BF16)

    def put_stage(rows, corners, t, value):
        cut = value.reshape(COLS, ROWS, C)
        rows[0, t] = fold_row(cut[:, 0, :]).astype(BF16)
        rows[1, t] = fold_row(cut[:, ROWS - 1, :]).astype(BF16)
        for n, at in enumerate((0, PIX - ROWS, ROWS - 1, PIX - 1)):
            corners[n, t] = fold_row(value[at : at + 1])

    def add_rims(value, rims, t):
        cut = value.reshape(COLS, ROWS, C)
        cut = cut + jnp.where(is_top[None], row_of(rims, 0, t).reshape(COLS, 1, C), 0.0)
        cut = cut + jnp.where(is_bottom[None], row_of(rims, 1, t).reshape(COLS, 1, C), 0.0)
        sides = []
        for n in range(2):
            column = rims[0][n, t].astype(F32) + jnp.where(is_top, corner_of(rims, n, t), 0.0)
            sides.append((column + jnp.where(is_bottom, corner_of(rims, n + 2, t), 0.0))[None])
        cut = jnp.concatenate([cut[0:1] + sides[0], cut[1:7], cut[7:8] + sides[1]], axis=0)
        return cut.reshape(PIX, C)

    def by_columns(value):
        return jnp.transpose(value.astype(F32).reshape(ROWS, COLS, C), (1, 0, 2))

    def by_rows(value):
        return jnp.transpose(value.reshape(COLS, ROWS, C), (1, 0, 2)).reshape(PIX, C).astype(BF16)

    def map_rims(store, rows, corners, t):
        return (store.at[t, 0], store.at[t, COLS - 1]), (rows.at[0, t], rows.at[1, t]), [corners.at[n, t] for n in range(4)]

    def grad_rims(stage):
        return [[held.at[n] for n in range(held.shape[0])] for held in stage]

    def rim_copies(source, rims, t, send, recv, to_layer, act_on):
        for d in range(8):
            found, other = there(d)
            kind, n = PIECE[d]
            far = PIECE[7 - d][1]

            @pl.when(found)
            def _(d=d, other=other, kind=kind, n=n, far=far):
                act_on(remote(
                    source[kind][n], rims[kind].at[far, t], send.at[d], recv.at[7 - d, t], to_layer, other
                ))

    def rim_arrivals(rims, t, send, recv):
        for d in range(8):
            found, other = there(d)
            kind, n = PIECE[d]

            @pl.when(found)
            def _(d=d, other=other, kind=kind, n=n):
                here = rims[kind].at[n, t]
                remote(here, here, send.at[d], recv.at[d, t], layer, other).wait_recv()

    def begin(copy):
        copy.start()

    def settle(copy):
        copy.wait_send()

    def send_map(store, rows, corners, rims, t, send, recv, to_layer):
        source = map_rims(store, rows, corners, t)

        @pl.when(t > 0)
        def _():
            rim_copies(source, rims, t, send, recv, to_layer, settle)

        rim_copies(source, rims, t, send, recv, to_layer, begin)

    def end_map(store, rows, corners, rims, send, recv, to_layer):
        rim_copies(map_rims(store, rows, corners, 0), rims, 0, send, recv, to_layer, settle)

    def turn_weight():
        def one(k, _):
            for n in range(2):
                wt[n, k] = w[n, k].T
            return 0

        lax.fori_loop(0, 9, one, 0)

    @pl.when(layer == 0)
    def _():
        pltpu.make_async_copy(frames, gin, in_sem).wait()

        def one(t, _):
            value = by_columns(gin[t])
            xc[t] = value.astype(BF16)
            put_stage(x_rows, x_corners, t, value.reshape(PIX, C))
            send_map(xc, x_rows, x_corners, xrim, t, fr_send, x_recv, layer)
            return 0

        lax.fori_loop(0, STEPS, one, 0)
        end_map(xc, x_rows, x_corners, xrim, fr_send, x_recv, layer)

    for copy in w_copies:
        copy.wait()

    @pl.when(layer == 3)
    def _():
        pltpu.make_async_copy(cotangent, gin, in_sem).wait()

        def one(t, _):
            up[t] = by_columns(gin[t]).astype(BF16)
            return 0

        lax.fori_loop(0, STEPS, one, 0)
        turn_weight()

    def mate_patches(t):
        return remote(st.at[t], pst.at[t], ps_send, ps_recv.at[t], layer, mate)

    def above_map(t):
        return remote(hs.at[t], xc.at[t], xs_send.at[8], xc_recv.at[t], layer + 1, tile)

    def patches(t, n):
        taps = [st[t, n, p, q : q + 8].reshape(PIX, C) for p in range(3) for q in range(3)]
        return jnp.concatenate(taps, axis=1)

    def forward(t, _):
        @pl.when(layer > 0)
        def _():
            remote(xc.at[t], xc.at[t], xs_send.at[8], xc_recv.at[t], layer - 1, tile).wait_recv()

        put_centre(st.at[t, 0], xc[t].astype(F32).reshape(PIX, C))
        rim_arrivals(xrim, t, xs_send, x_recv)
        put_rim(st.at[t, 0], xrim, t)
        sums[...] = jnp.dot(patches(t, 0), w[0].reshape(9 * C, GC), preferred_element_type=F32)

        @pl.when(t > 0)
        def _():
            rim_arrivals(hrim, t - 1, hs_send, h_recv)
            put_rim(st.at[t, 1], hrim, t - 1)
            mate_patches(t - 1).wait_send()
            sums[...] += jnp.dot(patches(t, 1), w[1].reshape(9 * C, GC), preferred_element_type=F32)

        in_gate = sigmoid(sums[:, 0:C])
        forget = sigmoid(sums[:, C : 2 * C] + FORGET_SHIFT)
        out_gate = sigmoid(sums[:, 2 * C : 3 * C])
        update = jnp.tanh(sums[:, 3 * C :])
        fresh = forget * cell[t] + in_gate * update
        squashed = jnp.tanh(fresh)
        hidden = out_gate * squashed
        hs[t] = hidden.astype(BF16).reshape(COLS, ROWS, C)
        put_stage(h_rows, h_corners, t, hidden)

        @pl.when(t < STEPS - 1)
        def _():
            send_map(hs, h_rows, h_corners, hrim, t, hs_send, h_recv, layer)

        @pl.when(layer < 3)
        def _():
            @pl.when(t > 0)
            def _():
                above_map(t - 1).wait_send()

            above_map(t).start()
            send_map(hs, h_rows, h_corners, xrim, t, xs_send, x_recv, layer + 1)

        mate_patches(t).start()
        act[t, :, 0:C] = in_gate
        act[t, :, C : 2 * C] = forget
        act[t, :, 2 * C : 3 * C] = out_gate
        act[t, :, 3 * C :] = update
        cell[t + 1] = fresh
        squash[t] = squashed
        hrow[t] = by_rows(hidden)

        @pl.when(t < STEPS - 1)
        def _():
            put_centre(st.at[t + 1, 1], hidden)

        return 0

    lax.fori_loop(0, STEPS, forward, 0)
    mate_patches(STEPS - 1).wait_send()
    end_map(hs, h_rows, h_corners, hrim, hs_send, h_recv, layer)

    hid_copy = pltpu.make_async_copy(hrow, hid_out, out_sem.at[0])
    hid_copy.start()

    @pl.when(layer < 3)
    def _():
        turn_weight()
        above_map(STEPS - 1).wait_send()
        end_map(hs, h_rows, h_corners, xrim, xs_send, x_recv, layer + 1)

    mine = pl.ds(pl.multiple_of(core * 512, 512), 512)
    theirs = pl.ds(pl.multiple_of((1 - core) * 512, 512), 512)

    def mate_gates(t):
        return remote(gates.at[t, :, theirs], pg.at[t], pg_send, pg_recv.at[t], layer, mate)

    def weight_terms(t, n, p, q):
        lhs = jnp.concatenate(
            [st[t, n, p, q : q + 8].reshape(PIX, C), pst[t, n, p, q : q + 8].reshape(PIX, C)], axis=0
        )
        rhs = jnp.concatenate([gates[t, :, mine], pg[t]], axis=0)
        return lax.dot_general(lhs, rhs, (((0,), (0,)), ((), ())), preferred_element_type=F32)

    def wait_mate(t):
        mate_patches(t).wait_recv()
        mate_gates(t).wait_recv()

    def below_grad(t):
        return remote(gown.at[t], up.at[t], us_send.at[8], u_recv.at[t], layer - 1, tile)

    def spread_out(t, n, stage):
        for p in range(3):
            for q in range(3):
                term = jnp.dot(gates[t], wt[n, 3 * p + q], preferred_element_type=F32)
                if q == 0:
                    spread[p, 0:PIX] = term
                    spread[p, PIX:] = jnp.zeros((2 * ROWS, C), F32)
                else:
                    spread[p, ROWS * q : ROWS * q + PIX] += term
        row = lax.rem(lax.broadcasted_iota(jnp.int32, (PIX + 2 * ROWS, 1), 0), ROWS)
        upper, lower = spread[0], spread[2]
        centre = spread[1] + jnp.where(row == ROWS - 1, 0.0, pltpu.roll(upper, PIX + 2 * ROWS - 1, 0))
        centre = centre + jnp.where(row == 0, 0.0, pltpu.roll(lower, 1, 0))
        rows = (upper.reshape(COLS + 2, ROWS, C)[1:9, 0, :], lower.reshape(COLS + 2, ROWS, C)[1:9, ROWS - 1, :])
        stage[0][0] = centre[0:ROWS].astype(stage[0].dtype)
        stage[0][1] = centre[PIX + ROWS :].astype(stage[0].dtype)
        for m in range(2):
            stage[1][m] = (rows[m] if stage[1].shape[2] == C else fold_row(rows[m])).astype(stage[1].dtype)
        ends = ((upper, 0), (upper, PIX + ROWS), (lower, ROWS - 1), (lower, PIX + 2 * ROWS - 1))
        for m, (source, at) in enumerate(ends):
            stage[2][m] = fold_row(source[at : at + 1])
        return centre[ROWS : PIX + ROWS]

    def settle_inputs(t):
        rim_copies(grad_rims(gstage), grim, t, gs_send, g_recv_rim, layer, settle)

        @pl.when(layer > 0)
        def _():
            below_grad(t).wait_send()
            rim_copies(grad_rims(gstage), urim, t, us_send, u_recv_rim, layer - 1, settle)

    def finish_inputs(t):
        rim_arrivals(grim, t, gs_send, g_recv_rim)
        gin[t] = by_rows(add_rims(gsum[t], grim, t))

    @pl.when(layer == 3)
    def _():
        for held in urim:
            held[...] = jnp.zeros_like(held)

    def backward(i, _):
        t = STEPS - 1 - i

        @pl.when(i > 0)
        def _():
            rim_arrivals(rrim, t + 1, rs_send, r_recv_rim)
            recurrent[...] = add_rims(recurrent[...], rrim, t + 1)

        @pl.when(layer < 3)
        def _():
            remote(up.at[t], up.at[t], us_send.at[8], u_recv.at[t], layer + 1, tile).wait_recv()
            rim_arrivals(urim, t, us_send, u_recv_rim)

        grad_hidden = add_rims(up[t].astype(F32).reshape(PIX, C) + recurrent[...], urim, t)
        in_gate = act[t, :, 0:C]
        forget = act[t, :, C : 2 * C]
        out_gate = act[t, :, 2 * C : 3 * C]
        update = act[t, :, 3 * C :]
        squashed = squash[t]
        grad_cell = grad_hidden * out_gate * (1.0 - squashed * squashed) + carried[...]
        carried[...] = grad_cell * forget
        gates[t, :, 0:C] = (grad_cell * update * in_gate * (1.0 - in_gate)).astype(BF16)
        gates[t, :, C : 2 * C] = (grad_cell * cell[t] * forget * (1.0 - forget)).astype(BF16)
        gates[t, :, 2 * C : 3 * C] = (grad_hidden * squashed * out_gate * (1.0 - out_gate)).astype(BF16)
        gates[t, :, 3 * C :] = (grad_cell * in_gate * (1.0 - update * update)).astype(BF16)

        @pl.when(i > 0)
        def _():
            mate_gates(t + 1).wait_send()

        mate_gates(t).start()

        @pl.when(t > 0)
        def _():
            @pl.when(i > 0)
            def _():
                rim_copies(grad_rims(rstage), rrim, t + 1, rs_send, r_recv_rim, layer, settle)

            recurrent[...] = spread_out(t, 1, rstage)
            rim_copies(grad_rims(rstage), rrim, t, rs_send, r_recv_rim, layer, begin)

        @pl.when(i > 0)
        def _():
            settle_inputs(t + 1)

        own = spread_out(t, 0, gstage)
        gown[t] = own.astype(BF16).reshape(COLS, ROWS, C)

        @pl.when(layer > 0)
        def _():
            below_grad(t).start()
            rim_copies(grad_rims(gstage), urim, t, us_send, u_recv_rim, layer - 1, begin)

        rim_copies(grad_rims(gstage), grim, t, gs_send, g_recv_rim, layer, begin)
        gsum[t] = own

        @pl.when(i > 0)
        def _():
            wait_mate(t + 1)
            for p in range(3):
                for q in range(3):
                    for n in range(2):
                        low = 512 * (3 * p + q) + C * n
                        acc[low : low + C] += weight_terms(t + 1, n, p, q)
            finish_inputs(t + 1)

        return 0

    lax.fori_loop(0, STEPS, backward, 0)
    rim_copies(grad_rims(rstage), rrim, 1, rs_send, r_recv_rim, layer, settle)
    wait_mate(0)
    mate_gates(0).wait_send()
    for p in range(3):
        for q in range(3):
            for n in range(2):
                start = 512 * (3 * p + q) + C * n
                value = (acc[start : start + C] + weight_terms(0, n, p, q)).astype(BF16)
                low = start
                while low < start + C:
                    block = low // ROWS_OUT
                    high = min(start + C, ROWS_OUT * (block + 1))
                    rows = slice(low - ROWS_OUT * block, high - ROWS_OUT * block)
                    z, y = block // 4, block % 4
                    part[0, y, z, rows] = value[low - start : high - start, 0:256]
                    part[1, z, y, rows] = value[low - start : high - start, 256:512]
                    low = high

    def plus(left, right):
        return (left.astype(F32) + right.astype(F32)).astype(BF16)

    def own(n):
        return (ypos, trow) if n == 0 else (trow, ypos)

    rights, lefts = (2, 1), (3, 0)
    sent = []

    def go(copy):
        copy.start()
        sent.append(copy)
        return copy

    def hop(n, first, to_right):
        return at_ring((n == 0) == first, 1 if to_right else 3)

    hand = {}
    full = {}
    for n in range(2):
        a, b = own(n)
        for m in range(2):
            for right in (True, False):
                j = (rights if right else lefts)[m]
                hand[n, m, right] = go(remote(
                    part.at[n, lax.rem(a + 2, 4), lax.rem(b + j, 4)], (from_l if right else from_r).at[n, m],
                    t_send.at[n, m, int(right)], t_recv.at[n, m, int(right)], layer, hop(n, True, right),
                ))

    def send_full(n, j, right):
        a, b = own(n)
        full[n, j, right] = go(remote(
            part.at[n, lax.rem(a + (1 if right else 3), 4), lax.rem(b + j, 4)], (full_l if right else full_r).at[n, j],
            f_send.at[n, j, int(right)], f_recv.at[n, j, int(right)], layer, hop(n, True, right),
        ))

    for m in range(2):
        for n in range(2):
            send_full(n, lefts[m], True)
            send_full(n, rights[m], False)
    finish_inputs(0)
    gin_copy = pltpu.make_async_copy(gin, gin_out, out_sem.at[1])
    gin_copy.start()
    settle_inputs(0)
    for m in range(2):
        for n in range(2):
            a, b = own(n)
            for right in (True, False):
                j = (rights if right else lefts)[m]
                hand[n, m, right].wait_recv()
                to = (n, lax.rem(a + (1 if right else 3), 4), lax.rem(b + j, 4))
                part[to] = plus(part[to], (from_l if right else from_r)[n, m])
                send_full(n, j, right)

    def gather(n, j):
        a, b = own(n)
        full[n, j, True].wait_recv()
        full[n, j, False].wait_recv()
        total[n, j] = (
            part[n, a, lax.rem(b + j, 4)].astype(F32) + full_l[n, j].astype(F32) + full_r[n, j].astype(F32)
        ).astype(BF16)

    upper, lower = pl.ds(0, HALF), pl.ds(HALF, HALF)
    hand2 = {}
    full2 = {}

    def send_full2(n, right, first):
        rows = lower if right == first else upper
        full2[n, right, first] = go(remote(
            total.at[n, 1 if right else 3, rows], (full2_l if right else full2_r).at[n, rows],
            f2_send.at[n, int(right), int(first)], f2_recv.at[n, int(right), int(first)], layer, hop(n, False, right),
        ))

    for n in range(2):
        gather(n, 2)
        for right in (True, False):
            hand2[n, right] = go(remote(
                total.at[n, 2, upper if right else lower], (from2_l if right else from2_r).at[n],
                t2_send.at[n, int(right)], t2_recv.at[n, int(right)], layer, hop(n, False, right),
            ))
    for right in (True, False):
        for n in range(2):
            gather(n, 1 if right else 3)
            send_full2(n, right, True)
    for n in range(2):
        for right in (True, False):
            hand2[n, right].wait_recv()
            at = (n, 1 if right else 3, upper if right else lower)
            total[at] = plus(total[at], (from2_l if right else from2_r)[n])
            send_full2(n, right, False)
    for n in range(2):
        gather(n, 0)
    for n in range(2):
        for right in (True, False):
            for first in (True, False):
                full2[n, right, first].wait_recv()
        res[:, 256 * n : 256 * n + 256] = plus(
            total[n, 0].astype(F32) + full2_l[n].astype(F32), full2_r[n]
        )
    last = go(remote(
        res.at[pl.ds(pl.multiple_of((1 - core) * HALF, HALF), HALF)], pres, r_send, r_recv, layer, mate
    ))
    wg_out[:, mine] = res[pl.ds(pl.multiple_of(core * HALF, HALF), HALF), :].astype(F32)
    last.wait_recv()
    wg_out[:, theirs] = pres[...].astype(F32)
    for copy in sent:
        copy.wait_send()
    hid_copy.wait()
    gin_copy.wait()


def copy_out(a, b, c, a_out, b_out, c_out, a_held, b_held, c_held, in_sem, out_sem):
    ways = ((a, a_held, a_out), (b, b_held, b_out), (c, c_held, c_out))
    come = [pltpu.make_async_copy(way[0], way[1], in_sem.at[n]) for n, way in enumerate(ways)]
    leave = [pltpu.make_async_copy(way[1], way[2], out_sem.at[n]) for n, way in enumerate(ways)]
    for copy in come:
        copy.start()
    for arrived, copy in zip(come, leave):
        arrived.wait()
        copy.start()
    for copy in leave:
        copy.wait()


def local(frames, weight, cotangent):
    maps = jax.ShapeDtypeStruct((STEPS, PIX, C), BF16)
    vmem = pltpu.VMEM
    dma = pltpu.SemaphoreType.DMA
    shape = (STEPS, COLS, ROWS, C)
    block = (ROWS_OUT, 256)

    def rims_of(dtype):
        row = (ROWS, 128) if dtype == BF16 else (8, C)
        return vmem((2, STEPS, ROWS, C), dtype), vmem((2, STEPS) + row, dtype), vmem((4, STEPS, 2, 128), F32)

    def stage_of(steps):
        return vmem((2, steps, ROWS, 128), BF16), vmem((4, steps, 2, 128), F32)

    hidden, grads, weight_grad = pl.pallas_call(
        kernel,
        out_shape=(maps, maps, jax.ShapeDtypeStruct((HALF, GC), F32)),
        in_specs=[pl.BlockSpec(memory_space=pl.ANY)] * 3,
        out_specs=(
            pl.BlockSpec(memory_space=pl.ANY),
            pl.BlockSpec(memory_space=pl.ANY),
            pl.BlockSpec(memory_space=pltpu.VMEM),
        ),
        scratch_shapes=[
            vmem((2, 9, C, GC), BF16),
            vmem((2, 9, GC, C), BF16),
            vmem((4608, 512), F32),
            vmem(shape, BF16),
            *stage_of(STEPS),
            *rims_of(BF16),
            vmem(shape, BF16),
            *stage_of(STEPS),
            *rims_of(BF16),
            vmem((STEPS, 2, 3, COLS + 2, ROWS, C), BF16),
            vmem((STEPS, 2, 3, COLS + 2, ROWS, C), BF16),
            vmem((STEPS, PIX, GC), F32),
            vmem((STEPS + 1, PIX, C), F32),
            vmem((STEPS, PIX, C), F32),
            vmem(shape, BF16),
            vmem((STEPS, PIX, GC), BF16),
            vmem((STEPS, PIX, 512), BF16),
            vmem((STEPS, PIX, C), BF16),
            vmem((STEPS, PIX, C), BF16),
            *rims_of(F32),
            *rims_of(BF16),
            *rims_of(BF16),
            vmem((2, ROWS, C), F32), vmem((2, 8, C), F32), vmem((4, 2, 128), F32),
            vmem((2, ROWS, C), BF16), vmem((2, ROWS, 128), BF16), vmem((4, 2, 128), F32),
            vmem(shape, BF16),
            vmem((STEPS, PIX, C), F32),
            vmem((3, PIX + 2 * ROWS, C), F32),
            vmem((PIX, C), F32),
            vmem((PIX, C), F32),
            vmem((PIX, GC), F32),
            vmem((2, 4, 4) + block, BF16),
            vmem((2, 2) + block, BF16),
            vmem((2, 2) + block, BF16),
            vmem((2, 4) + block, BF16),
            vmem((2, 4) + block, BF16),
            vmem((2, 4) + block, BF16),
            vmem((2, HALF, 256), BF16),
            vmem((2, HALF, 256), BF16),
            vmem((2,) + block, BF16),
            vmem((2,) + block, BF16),
            vmem((ROWS_OUT, 512), BF16),
            vmem((HALF, 512), BF16),
            dma((2,)), dma, dma((2,)),
            dma((9,)), dma((8,)), dma((8,)), dma((8,)), dma((9,)), dma((8,)), dma, dma,
            dma((STEPS,)), dma((8, STEPS)), dma((8, STEPS)),
            dma((8, STEPS)), dma((8, STEPS)), dma((8, STEPS)),
            dma((STEPS,)), dma((STEPS,)), dma((STEPS,)),
            dma((2, 2, 2)), dma((2, 2, 2)), dma((2, 4, 2)), dma((2, 4, 2)),
            dma((2, 2)), dma((2, 2)), dma((2, 2, 2)), dma((2, 2, 2)), dma, dma,
        ],
        compiler_params=pltpu.CompilerParams(
            collective_id=0, has_side_effects=True, vmem_limit_bytes=63 * 2**20
        ),
    )(
        frames.reshape(STEPS, PIX, C),
        weight.reshape(9, 2, C, GC),
        cotangent.reshape(STEPS, PIX, C),
    )
    hidden, grads, weight_grad = pl.pallas_call(
        copy_out,
        out_shape=(maps, maps, jax.ShapeDtypeStruct((HALF, GC), F32)),
        in_specs=[pl.BlockSpec(memory_space=pl.ANY)] * 3,
        out_specs=(pl.BlockSpec(memory_space=pl.ANY),) * 3,
        scratch_shapes=[vmem((STEPS, PIX, C), BF16), vmem((STEPS, PIX, C), BF16), vmem((HALF, GC), F32), dma((3,)), dma((3,))],
    )(hidden, grads, weight_grad)
    tiled = (1, STEPS, 1, ROWS, COLS, C)
    return hidden.reshape(tiled), grads.reshape(tiled), weight_grad[None]


def solution(mesh):
    in_specs = (
        P(None, "tile", None, None, None),
        P("layer", None, None),
        P(None, "tile", None, None, None),
    )
    out_specs = (
        P("layer", None, "tile", None, None, None),
        P("layer", None, "tile", None, None, None),
        P("layer", "tile", None),
    )
    return jax.shard_map(local, mesh=mesh, in_specs=in_specs, out_specs=out_specs, check_vma=False)
```

```python
import jax
import jax.numpy as jnp
from jax import lax
from jax.experimental import pallas as pl
from jax.experimental.pallas import tpu as pltpu
from jax.sharding import PartitionSpec as P

MESH = pl.DeviceIdType.MESH
F32 = jnp.float32
BF16 = jnp.bfloat16

C = 256
GC = 1024
STEPS = 6
COLS = 8
ROWS = 16
PIX = COLS * ROWS
ROWS_OUT = 288
HALF = 144
FORGET_SHIFT = 1.0
PIECE = ((2, 0), (1, 0), (2, 1), (0, 0), (0, 1), (2, 2), (1, 1), (2, 3))
DIRS = ((-1, -1), (-1, 0), (-1, 1), (0, -1), (0, 1), (1, -1), (1, 0), (1, 1))


def sigmoid(value):
    return 0.5 * jnp.tanh(0.5 * value) + 0.5


def kernel(
    frames, weight, cotangent, hid_out, gin_out, wg_out,
    w, wt, acc, xc, x_rows, x_corners, xrim0, xrim1, xrim2, hs, h_rows, h_corners, hrim0, hrim1, hrim2, st, pst, act, cell, squash, up, gates, pg, hrow, gin,
    rrim0, rrim1, rrim2, urim0, urim1, urim2, grim0, grim1, grim2,
    rstage0, rstage1, rstage2, gstage0, gstage1, gstage2, gown, gsum, spread,
    recurrent, carried, sums, part, from_l, from_r, full_l, full_r, total, got,
    w_sem, in_sem, out_sem, xs_send, fr_send, hs_send, rs_send, us_send, gs_send, ps_send, pg_send,
    xc_recv, x_recv, h_recv, r_recv_rim, u_recv_rim, g_recv_rim, u_recv, ps_recv, pg_recv,
    t_send, t_recv, f_send, f_recv, d_send, d_recv,
):
    xrim, hrim, rrim = (xrim0, xrim1, xrim2), (hrim0, hrim1, hrim2), (rrim0, rrim1, rrim2)
    urim, grim = (urim0, urim1, urim2), (grim0, grim1, grim2)
    rstage, gstage = (rstage0, rstage1, rstage2), (gstage0, gstage1, gstage2)
    layer = lax.axis_index("layer")
    tile = lax.axis_index("tile")
    trow, tcol = tile // 8, lax.rem(tile, 8)
    ypos, core = tcol // 2, lax.rem(tcol, 2)
    mate = tile + 1 - 2 * core

    def there(d):
        dy, dx = DIRS[d]
        found = jnp.bool_(True)
        if dy < 0:
            found = found & (trow > 0)
        if dy > 0:
            found = found & (trow < 3)
        if dx < 0:
            found = found & (tcol > 0)
        if dx > 0:
            found = found & (tcol < 7)
        return found, tile + 8 * dy + dx

    def remote(src, dst, send, recv, to_layer, to_tile):
        return pltpu.make_async_remote_copy(
            src_ref=src, dst_ref=dst, send_sem=send, recv_sem=recv,
            device_id={"layer": to_layer, "tile": to_tile}, device_id_type=MESH,
        )

    def at_ring(along_y, step, which):
        if along_y:
            return trow * 8 + lax.rem(ypos + step, 4) * 2 + which
        return lax.rem(trow + step, 4) * 8 + ypos * 2 + which

    @pl.when(layer == 0)
    def _():
        pltpu.make_async_copy(frames, gin, in_sem).start()

    @pl.when(layer == 3)
    def _():
        pltpu.make_async_copy(cotangent, gin, in_sem).start()

    w_copies = [pltpu.make_async_copy(weight.at[:, n], w.at[n], w_sem.at[n]) for n in range(2)]
    for copy in w_copies:
        copy.start()

    barrier = pltpu.get_barrier_semaphore()
    expected = jnp.int32(0)

    def greet(found, to_layer, to_tile):
        @pl.when(found)
        def _():
            pl.semaphore_signal(barrier, inc=1, device_id={"layer": to_layer, "tile": to_tile}, device_id_type=MESH)

        return found.astype(jnp.int32)

    for d in range(8):
        found, other = there(d)
        expected += greet(found, layer, other)
        expected += greet(found & (layer > 0), layer - 1, other)
        expected += greet(found & (layer < 3), layer + 1, other)
    expected += greet(layer > 0, layer - 1, tile)
    expected += greet(layer < 3, layer + 1, tile)
    for along_y in (True, False):
        for step in (1, 2, 3):
            for other in range(2):
                expected += greet(jnp.bool_(True), layer, at_ring(along_y, step, other))

    acc[...] = jnp.zeros_like(acc)
    recurrent[...] = jnp.zeros_like(recurrent)
    carried[...] = jnp.zeros_like(carried)
    cell[0] = jnp.zeros((PIX, C), F32)
    st[0, 1] = jnp.zeros((3, COLS + 2, ROWS, C), BF16)
    for d in range(8):
        found, _ = there(d)

        @pl.when(jnp.logical_not(found))
        def _(d=d):
            kind, n = PIECE[d]
            for rims in (xrim, hrim, rrim, urim, grim):
                rims[kind][n] = jnp.zeros(rims[kind].shape[1:], rims[kind].dtype)

    pl.semaphore_wait(barrier, expected)

    pixel_row = lax.broadcasted_iota(jnp.int32, (ROWS, 1), 0)
    is_top = pixel_row == 0
    is_bottom = pixel_row == ROWS - 1

    def put_centre(dst, value):
        dst[0, 1:9] = pltpu.roll(value, 1, 0).astype(BF16).reshape(COLS, ROWS, C)
        dst[1, 1:9] = value.astype(BF16).reshape(COLS, ROWS, C)
        dst[2, 1:9] = pltpu.roll(value, PIX - 1, 0).astype(BF16).reshape(COLS, ROWS, C)

    def row_of(rims, n, t):
        held = rims[1][n, t].astype(F32)
        if held.shape[1] == C:
            return held
        return jnp.concatenate([held[0:8], held[8:16]], axis=1)

    def corner_of(rims, n, t):
        held = rims[2][n, t]
        return jnp.concatenate([held[0:1], held[1:2]], axis=1)

    def fold_row(row):
        return jnp.concatenate([row[:, 0:128], row[:, 128:256]], axis=0)

    def put_rim(dst, rims, t):
        top = row_of(rims, 0, t).reshape(COLS, 1, C)
        bottom = row_of(rims, 1, t).reshape(COLS, 1, C)
        dst[0, 1:9] = jnp.where(is_top[None], top, dst[0, 1:9].astype(F32)).astype(BF16)
        dst[2, 1:9] = jnp.where(is_bottom[None], bottom, dst[2, 1:9].astype(F32)).astype(BF16)
        for n, column in ((0, 0), (1, 9)):
            value = rims[0][n, t].astype(F32)
            dst[0, column] = jnp.where(is_top, corner_of(rims, n, t), pltpu.roll(value, 1, 0)).astype(BF16)
            dst[1, column] = rims[0][n, t]
            lower = corner_of(rims, n + 2, t)
            dst[2, column] = jnp.where(is_bottom, lower, pltpu.roll(value, ROWS - 1, 0)).astype(BF16)

    def put_stage(rows, corners, t, value):
        cut = value.reshape(COLS, ROWS, C)
        rows[0, t] = fold_row(cut[:, 0, :]).astype(BF16)
        rows[1, t] = fold_row(cut[:, ROWS - 1, :]).astype(BF16)
        for n, at in enumerate((0, PIX - ROWS, ROWS - 1, PIX - 1)):
            corners[n, t] = fold_row(value[at : at + 1])

    def add_rims(value, rims, t):
        cut = value.reshape(COLS, ROWS, C)
        cut = cut + jnp.where(is_top[None], row_of(rims, 0, t).reshape(COLS, 1, C), 0.0)
        cut = cut + jnp.where(is_bottom[None], row_of(rims, 1, t).reshape(COLS, 1, C), 0.0)
        sides = []
        for n in range(2):
            column = rims[0][n, t].astype(F32) + jnp.where(is_top, corner_of(rims, n, t), 0.0)
            sides.append((column + jnp.where(is_bottom, corner_of(rims, n + 2, t), 0.0))[None])
        cut = jnp.concatenate([cut[0:1] + sides[0], cut[1:7], cut[7:8] + sides[1]], axis=0)
        return cut.reshape(PIX, C)

    def by_columns(value):
        return jnp.transpose(value.astype(F32).reshape(ROWS, COLS, C), (1, 0, 2))

    def by_rows(value):
        return jnp.transpose(value.reshape(COLS, ROWS, C), (1, 0, 2)).reshape(PIX, C).astype(BF16)

    def map_rims(store, rows, corners, t):
        return (store.at[t, 0], store.at[t, COLS - 1]), (rows.at[0, t], rows.at[1, t]), [corners.at[n, t] for n in range(4)]

    def grad_rims(stage):
        return [[held.at[n] for n in range(held.shape[0])] for held in stage]

    def rim_copies(source, rims, t, send, recv, to_layer, act_on):
        for d in range(8):
            found, other = there(d)
            kind, n = PIECE[d]
            far = PIECE[7 - d][1]

            @pl.when(found)
            def _(d=d, other=other, kind=kind, n=n, far=far):
                act_on(remote(
                    source[kind][n], rims[kind].at[far, t], send.at[d], recv.at[7 - d, t], to_layer, other
                ))

    def rim_arrivals(rims, t, send, recv):
        for d in range(8):
            found, other = there(d)
            kind, n = PIECE[d]

            @pl.when(found)
            def _(d=d, other=other, kind=kind, n=n):
                here = rims[kind].at[n, t]
                remote(here, here, send.at[d], recv.at[d, t], layer, other).wait_recv()

    def begin(copy):
        copy.start()

    def settle(copy):
        copy.wait_send()

    def send_map(store, rows, corners, rims, t, send, recv, to_layer):
        source = map_rims(store, rows, corners, t)

        @pl.when(t > 0)
        def _():
            rim_copies(source, rims, t, send, recv, to_layer, settle)

        rim_copies(source, rims, t, send, recv, to_layer, begin)

    def end_map(store, rows, corners, rims, send, recv, to_layer):
        rim_copies(map_rims(store, rows, corners, 0), rims, 0, send, recv, to_layer, settle)

    def turn_weight():
        def one(k, _):
            for n in range(2):
                wt[n, k] = w[n, k].T
            return 0

        lax.fori_loop(0, 9, one, 0)

    @pl.when(layer == 0)
    def _():
        pltpu.make_async_copy(frames, gin, in_sem).wait()

        def one(t, _):
            value = by_columns(gin[t])
            xc[t] = value.astype(BF16)
            put_stage(x_rows, x_corners, t, value.reshape(PIX, C))
            rim_copies(map_rims(xc, x_rows, x_corners, t), xrim, t, fr_send.at[t], x_recv, layer, begin)
            return 0

        lax.fori_loop(0, STEPS, one, 0)

    for copy in w_copies:
        copy.wait()

    @pl.when(layer == 3)
    def _():
        pltpu.make_async_copy(cotangent, gin, in_sem).wait()

        def one(t, _):
            up[t] = by_columns(gin[t]).astype(BF16)
            return 0

        lax.fori_loop(0, STEPS, one, 0)
        turn_weight()

    def mate_patches(t):
        return remote(st.at[t], pst.at[t], ps_send, ps_recv.at[t], layer, mate)

    def above_map(t):
        return remote(hs.at[t], xc.at[t], xs_send.at[8], xc_recv.at[t], layer + 1, tile)

    def patches(t, n):
        taps = [st[t, n, p, q : q + 8].reshape(PIX, C) for p in range(3) for q in range(3)]
        return jnp.concatenate(taps, axis=1)

    def forward(t, _):
        @pl.when(layer > 0)
        def _():
            remote(xc.at[t], xc.at[t], xs_send.at[8], xc_recv.at[t], layer - 1, tile).wait_recv()

        put_centre(st.at[t, 0], xc[t].astype(F32).reshape(PIX, C))
        rim_arrivals(xrim, t, xs_send, x_recv)
        put_rim(st.at[t, 0], xrim, t)
        sums[...] = jnp.dot(patches(t, 0), w[0].reshape(9 * C, GC), preferred_element_type=F32)

        @pl.when(t > 0)
        def _():
            rim_arrivals(hrim, t - 1, hs_send, h_recv)
            put_rim(st.at[t, 1], hrim, t - 1)
            mate_patches(t - 1).wait_send()
            sums[...] += jnp.dot(patches(t, 1), w[1].reshape(9 * C, GC), preferred_element_type=F32)

        in_gate = sigmoid(sums[:, 0:C])
        forget = sigmoid(sums[:, C : 2 * C] + FORGET_SHIFT)
        out_gate = sigmoid(sums[:, 2 * C : 3 * C])
        update = jnp.tanh(sums[:, 3 * C :])
        fresh = forget * cell[t] + in_gate * update
        squashed = jnp.tanh(fresh)
        hidden = out_gate * squashed
        hs[t] = hidden.astype(BF16).reshape(COLS, ROWS, C)
        put_stage(h_rows, h_corners, t, hidden)

        @pl.when(t < STEPS - 1)
        def _():
            send_map(hs, h_rows, h_corners, hrim, t, hs_send, h_recv, layer)

        @pl.when(layer < 3)
        def _():
            @pl.when(t > 0)
            def _():
                above_map(t - 1).wait_send()

            above_map(t).start()
            send_map(hs, h_rows, h_corners, xrim, t, xs_send, x_recv, layer + 1)

        mate_patches(t).start()
        act[t, :, 0:C] = in_gate
        act[t, :, C : 2 * C] = forget
        act[t, :, 2 * C : 3 * C] = out_gate
        act[t, :, 3 * C :] = update
        cell[t + 1] = fresh
        squash[t] = squashed
        hrow[t] = by_rows(hidden)

        @pl.when(t < STEPS - 1)
        def _():
            put_centre(st.at[t + 1, 1], hidden)

        return 0

    lax.fori_loop(0, STEPS, forward, 0)
    mate_patches(STEPS - 1).wait_send()
    end_map(hs, h_rows, h_corners, hrim, hs_send, h_recv, layer)

    hid_copy = pltpu.make_async_copy(hrow, hid_out, out_sem.at[0])
    hid_copy.start()

    @pl.when(layer < 3)
    def _():
        turn_weight()
        above_map(STEPS - 1).wait_send()
        end_map(hs, h_rows, h_corners, xrim, xs_send, x_recv, layer + 1)

    @pl.when(layer == 0)
    def _():
        def one(t, _):
            rim_copies(map_rims(xc, x_rows, x_corners, t), xrim, t, fr_send.at[t], x_recv, layer, settle)
            return 0

        lax.fori_loop(0, STEPS, one, 0)

    mine = pl.ds(pl.multiple_of(core * 512, 512), 512)
    theirs = pl.ds(pl.multiple_of((1 - core) * 512, 512), 512)

    def mate_gates(t):
        return remote(gates.at[t, :, theirs], pg.at[t], pg_send, pg_recv.at[t], layer, mate)

    def weight_terms(t, n, p, q):
        lhs = jnp.concatenate(
            [st[t, n, p, q : q + 8].reshape(PIX, C), pst[t, n, p, q : q + 8].reshape(PIX, C)], axis=0
        )
        rhs = jnp.concatenate([gates[t, :, mine], pg[t]], axis=0)
        return lax.dot_general(lhs, rhs, (((0,), (0,)), ((), ())), preferred_element_type=F32)

    def wait_mate(t):
        mate_patches(t).wait_recv()
        mate_gates(t).wait_recv()

    def below_grad(t):
        return remote(gown.at[t], up.at[t], us_send.at[8], u_recv.at[t], layer - 1, tile)

    def spread_out(t, n, stage):
        for p in range(3):
            for q in range(3):
                term = jnp.dot(gates[t], wt[n, 3 * p + q], preferred_element_type=F32)
                if q == 0:
                    spread[p, 0:PIX] = term
                    spread[p, PIX:] = jnp.zeros((2 * ROWS, C), F32)
                else:
                    spread[p, ROWS * q : ROWS * q + PIX] += term
        row = lax.rem(lax.broadcasted_iota(jnp.int32, (PIX + 2 * ROWS, 1), 0), ROWS)
        upper, lower = spread[0], spread[2]
        centre = spread[1] + jnp.where(row == ROWS - 1, 0.0, pltpu.roll(upper, PIX + 2 * ROWS - 1, 0))
        centre = centre + jnp.where(row == 0, 0.0, pltpu.roll(lower, 1, 0))
        rows = (upper.reshape(COLS + 2, ROWS, C)[1:9, 0, :], lower.reshape(COLS + 2, ROWS, C)[1:9, ROWS - 1, :])
        stage[0][0] = centre[0:ROWS].astype(stage[0].dtype)
        stage[0][1] = centre[PIX + ROWS :].astype(stage[0].dtype)
        for m in range(2):
            stage[1][m] = (rows[m] if stage[1].shape[2] == C else fold_row(rows[m])).astype(stage[1].dtype)
        ends = ((upper, 0), (upper, PIX + ROWS), (lower, ROWS - 1), (lower, PIX + 2 * ROWS - 1))
        for m, (source, at) in enumerate(ends):
            stage[2][m] = fold_row(source[at : at + 1])
        return centre[ROWS : PIX + ROWS]

    def settle_inputs(t):
        rim_copies(grad_rims(gstage), grim, t, gs_send, g_recv_rim, layer, settle)

        @pl.when(layer > 0)
        def _():
            below_grad(t).wait_send()
            rim_copies(grad_rims(gstage), urim, t, us_send, u_recv_rim, layer - 1, settle)

    def finish_inputs(t):
        rim_arrivals(grim, t, gs_send, g_recv_rim)
        gin[t] = by_rows(add_rims(gsum[t], grim, t))

    def input_part(t):
        @pl.when(t < STEPS - 1)
        def _():
            settle_inputs(t + 1)

        own = spread_out(t, 0, gstage)
        gown[t] = own.astype(BF16).reshape(COLS, ROWS, C)

        @pl.when(layer > 0)
        def _():
            below_grad(t).start()
            rim_copies(grad_rims(gstage), urim, t, us_send, u_recv_rim, layer - 1, begin)

        rim_copies(grad_rims(gstage), grim, t, gs_send, g_recv_rim, layer, begin)
        gsum[t] = own

    @pl.when(layer == 3)
    def _():
        for held in urim:
            held[...] = jnp.zeros_like(held)

    def backward(i, _):
        t = STEPS - 1 - i

        @pl.when(i > 0)
        def _():
            rim_arrivals(rrim, t + 1, rs_send, r_recv_rim)
            recurrent[...] = add_rims(recurrent[...], rrim, t + 1)

        @pl.when(layer < 3)
        def _():
            remote(up.at[t], up.at[t], us_send.at[8], u_recv.at[t], layer + 1, tile).wait_recv()
            rim_arrivals(urim, t, us_send, u_recv_rim)

        grad_hidden = add_rims(up[t].astype(F32).reshape(PIX, C) + recurrent[...], urim, t)
        in_gate = act[t, :, 0:C]
        forget = act[t, :, C : 2 * C]
        out_gate = act[t, :, 2 * C : 3 * C]
        update = act[t, :, 3 * C :]
        squashed = squash[t]
        grad_cell = grad_hidden * out_gate * (1.0 - squashed * squashed) + carried[...]
        carried[...] = grad_cell * forget
        gates[t, :, 0:C] = (grad_cell * update * in_gate * (1.0 - in_gate)).astype(BF16)
        gates[t, :, C : 2 * C] = (grad_cell * cell[t] * forget * (1.0 - forget)).astype(BF16)
        gates[t, :, 2 * C : 3 * C] = (grad_hidden * squashed * out_gate * (1.0 - out_gate)).astype(BF16)
        gates[t, :, 3 * C :] = (grad_cell * in_gate * (1.0 - update * update)).astype(BF16)

        @pl.when(i > 0)
        def _():
            mate_gates(t + 1).wait_send()

        mate_gates(t).start()

        @pl.when(t > 0)
        def _():
            @pl.when(i > 0)
            def _():
                rim_copies(grad_rims(rstage), rrim, t + 1, rs_send, r_recv_rim, layer, settle)

            recurrent[...] = spread_out(t, 1, rstage)
            rim_copies(grad_rims(rstage), rrim, t, rs_send, r_recv_rim, layer, begin)

        @pl.when((layer > 0) | (t > 0))
        def _():
            input_part(t)

        @pl.when(t > 0)
        def _():
            wait_mate(t)
            for p in range(3):
                for q in range(3):
                    for n in range(2):
                        low = 512 * (3 * p + q) + C * n
                        acc[low : low + C] += weight_terms(t, n, p, q)

        @pl.when((i > 0) & (t > 0))
        def _():
            finish_inputs(t + 1)

        return 0

    lax.fori_loop(0, STEPS, backward, 0)

    def plus(left, right):
        return (left.astype(F32) + right.astype(F32)).astype(BF16)

    def own(n):
        return (ypos, trow) if n == 0 else (trow, ypos)

    rights, lefts = (2, 1), (3, 0)
    sent = []

    def go(copy):
        copy.start()
        sent.append(copy)
        return copy

    hand = {}
    full = {}

    def last_terms(half):
        columns = slice(256 * half, 256 * half + 256)
        rhs = jnp.concatenate(
            [gates[0, :, pl.ds(pl.multiple_of(core * 512 + 256 * half, 256), 256)], pg[0, :, columns]], axis=0
        )
        for p in range(3):
            for q in range(3):
                for n in range(2):
                    start = 512 * (3 * p + q) + C * n
                    lhs = jnp.concatenate(
                        [st[0, n, p, q : q + 8].reshape(PIX, C), pst[0, n, p, q : q + 8].reshape(PIX, C)], axis=0
                    )
                    term = lax.dot_general(lhs, rhs, (((0,), (0,)), ((), ())), preferred_element_type=F32)
                    value = (acc[start : start + C, columns] + term).astype(BF16)
                    low = start
                    while low < start + C:
                        block = low // ROWS_OUT
                        high = min(start + C, ROWS_OUT * (block + 1))
                        rows = slice(low - ROWS_OUT * block, high - ROWS_OUT * block)
                        z, y = block // 4, block % 4
                        at = (0, y, z, rows) if half == 0 else (1, z, y, rows)
                        part[at] = value[low - start : high - start]
                        low = high

    def send_full(n, j, right):
        a, b = own(n)
        full[n, j, right] = go(remote(
            part.at[n, lax.rem(a + (1 if right else 3), 4), lax.rem(b + j, 4)], (full_l if right else full_r).at[n, j],
            f_send.at[n, j, int(right)], f_recv.at[n, j, int(right)], layer, at_ring(n == 0, 1 if right else 3, core),
        ))

    wait_mate(0)
    mate_gates(0).wait_send()
    for n in range(2):
        a, b = own(n)
        last_terms(n)
        for m in range(2):
            for right in (True, False):
                j = (rights if right else lefts)[m]
                hand[n, m, right] = go(remote(
                    part.at[n, lax.rem(a + 2, 4), lax.rem(b + j, 4)], (from_l if right else from_r).at[n, m],
                    t_send.at[n, m, int(right)], t_recv.at[n, m, int(right)], layer,
                    at_ring(n == 0, 1 if right else 3, core),
                ))
        for m in range(2):
            send_full(n, lefts[m], True)
            send_full(n, rights[m], False)

    @pl.when(layer == 0)
    def _():
        input_part(0)

    finish_inputs(1)
    rim_copies(grad_rims(rstage), rrim, 1, rs_send, r_recv_rim, layer, settle)
    for m in range(2):
        for n in range(2):
            a, b = own(n)
            for right in (True, False):
                j = (rights if right else lefts)[m]
                hand[n, m, right].wait_recv()
                to = (n, lax.rem(a + (1 if right else 3), 4), lax.rem(b + j, 4))
                part[to] = plus(part[to], (from_l if right else from_r)[n, m])
                send_full(n, j, right)
    finish_inputs(0)
    gin_copy = pltpu.make_async_copy(gin, gin_out, out_sem.at[1])
    gin_copy.start()
    settle_inputs(0)

    def gather(n, j):
        a, b = own(n)
        full[n, j, True].wait_recv()
        full[n, j, False].wait_recv()
        total[n, j] = (
            part[n, a, lax.rem(b + j, 4)].astype(F32) + full_l[n, j].astype(F32) + full_r[n, j].astype(F32)
        ).astype(BF16)

    def half_rows(which):
        return pl.ds(pl.multiple_of(which * HALF, HALF), HALF)

    def to_owner(n, j, which, slot):
        return remote(
            total.at[n, j, half_rows(which)], got.at[n, j, core], d_send.at[n, j, slot], d_recv.at[n, j, core],
            layer, at_ring(n == 1, j, which),
        )

    for j in (2, 1, 3, 0):
        for n in range(2):
            gather(n, j)
            if j == 0:
                go(to_owner(n, 0, 1 - core, 0))
                got[n, 0, core] = total[n, 0, half_rows(core), :]
            else:
                for which in range(2):
                    go(to_owner(n, j, which, which))
    for n in range(2):
        remote(got.at[n, 0, 1 - core], got.at[n, 0, 1 - core], d_send.at[n, 0, 0], d_recv.at[n, 0, 1 - core], layer, mate).wait_recv()
        for j in (1, 3, 2):
            for which in range(2):
                here = got.at[n, j, which]
                remote(here, here, d_send.at[n, j, which], d_recv.at[n, j, which], layer, at_ring(n == 1, 4 - j, which)).wait_recv()
    for which in range(2):
        for n in range(2):
            low = 512 * which + 256 * n
            wg_out[:, low : low + 256] = (got[n, 0, which].astype(F32) + got[n, 1, which].astype(F32)) + (
                got[n, 2, which].astype(F32) + got[n, 3, which].astype(F32)
            )
    for copy in sent:
        copy.wait_send()

    hid_copy.wait()
    gin_copy.wait()


def copy_out(a, b, c, a_out, b_out, c_out, a_held, b_held, c_held, in_sem, out_sem):
    ways = ((a, a_held, a_out), (b, b_held, b_out), (c, c_held, c_out))
    come = [pltpu.make_async_copy(way[0], way[1], in_sem.at[n]) for n, way in enumerate(ways)]
    leave = [pltpu.make_async_copy(way[1], way[2], out_sem.at[n]) for n, way in enumerate(ways)]
    for copy in come:
        copy.start()
    for arrived, copy in zip(come, leave):
        arrived.wait()
        copy.start()
    for copy in leave:
        copy.wait()


def local(frames, weight, cotangent):
    maps = jax.ShapeDtypeStruct((STEPS, PIX, C), BF16)
    vmem = pltpu.VMEM
    dma = pltpu.SemaphoreType.DMA
    shape = (STEPS, COLS, ROWS, C)
    block = (ROWS_OUT, 256)

    def rims_of(dtype):
        row = (ROWS, 128) if dtype == BF16 else (8, C)
        return vmem((2, STEPS, ROWS, C), dtype), vmem((2, STEPS) + row, dtype), vmem((4, STEPS, 2, 128), F32)

    def stage_of(steps):
        return vmem((2, steps, ROWS, 128), BF16), vmem((4, steps, 2, 128), F32)

    hidden, grads, weight_grad = pl.pallas_call(
        kernel,
        out_shape=(maps, maps, jax.ShapeDtypeStruct((HALF, GC), F32)),
        in_specs=[pl.BlockSpec(memory_space=pl.ANY)] * 3,
        out_specs=(
            pl.BlockSpec(memory_space=pl.ANY),
            pl.BlockSpec(memory_space=pl.ANY),
            pl.BlockSpec(memory_space=pltpu.VMEM),
        ),
        scratch_shapes=[
            vmem((2, 9, C, GC), BF16),
            vmem((2, 9, GC, C), BF16),
            vmem((4608, 512), F32),
            vmem(shape, BF16),
            *stage_of(STEPS),
            *rims_of(BF16),
            vmem(shape, BF16),
            *stage_of(STEPS),
            *rims_of(BF16),
            vmem((STEPS, 2, 3, COLS + 2, ROWS, C), BF16),
            vmem((STEPS, 2, 3, COLS + 2, ROWS, C), BF16),
            vmem((STEPS, PIX, GC), F32),
            vmem((STEPS + 1, PIX, C), F32),
            vmem((STEPS, PIX, C), F32),
            vmem(shape, BF16),
            vmem((STEPS, PIX, GC), BF16),
            vmem((STEPS, PIX, 512), BF16),
            vmem((STEPS, PIX, C), BF16),
            vmem((STEPS, PIX, C), BF16),
            *rims_of(F32),
            *rims_of(BF16),
            *rims_of(BF16),
            vmem((2, ROWS, C), F32), vmem((2, 8, C), F32), vmem((4, 2, 128), F32),
            vmem((2, ROWS, C), BF16), vmem((2, ROWS, 128), BF16), vmem((4, 2, 128), F32),
            vmem(shape, BF16),
            vmem((STEPS, PIX, C), F32),
            vmem((3, PIX + 2 * ROWS, C), F32),
            vmem((PIX, C), F32),
            vmem((PIX, C), F32),
            vmem((PIX, GC), F32),
            vmem((2, 4, 4) + block, BF16),
            vmem((2, 2) + block, BF16),
            vmem((2, 2) + block, BF16),
            vmem((2, 4) + block, BF16),
            vmem((2, 4) + block, BF16),
            vmem((2, 4) + block, BF16),
            vmem((2, 4, 2, HALF, 256), BF16),
            dma((2,)), dma, dma((2,)),
            dma((9,)), dma((STEPS, 8)), dma((8,)), dma((8,)), dma((9,)), dma((8,)), dma, dma,
            dma((STEPS,)), dma((8, STEPS)), dma((8, STEPS)),
            dma((8, STEPS)), dma((8, STEPS)), dma((8, STEPS)),
            dma((STEPS,)), dma((STEPS,)), dma((STEPS,)),
            dma((2, 2, 2)), dma((2, 2, 2)), dma((2, 4, 2)), dma((2, 4, 2)),
            dma((2, 4, 2)), dma((2, 4, 2)),
        ],
        compiler_params=pltpu.CompilerParams(
            collective_id=0, has_side_effects=True, vmem_limit_bytes=63 * 2**20
        ),
    )(
        frames.reshape(STEPS, PIX, C),
        weight.reshape(9, 2, C, GC),
        cotangent.reshape(STEPS, PIX, C),
    )
    hidden, grads, weight_grad = pl.pallas_call(
        copy_out,
        out_shape=(maps, maps, jax.ShapeDtypeStruct((HALF, GC), F32)),
        in_specs=[pl.BlockSpec(memory_space=pl.ANY)] * 3,
        out_specs=(pl.BlockSpec(memory_space=pl.ANY),) * 3,
        scratch_shapes=[vmem((STEPS, PIX, C), BF16), vmem((STEPS, PIX, C), BF16), vmem((HALF, GC), F32), dma((3,)), dma((3,))],
    )(hidden, grads, weight_grad)
    tiled = (1, STEPS, 1, ROWS, COLS, C)
    return hidden.reshape(tiled), grads.reshape(tiled), weight_grad[None]


def solution(mesh):
    in_specs = (
        P(None, "tile", None, None, None),
        P("layer", None, None),
        P(None, "tile", None, None, None),
    )
    out_specs = (
        P("layer", None, "tile", None, None, None),
        P("layer", None, "tile", None, None, None),
        P("layer", "tile", None),
    )
    return jax.shard_map(local, mesh=mesh, in_specs=in_specs, out_specs=out_specs, check_vma=False)
```

```python
import jax
import jax.numpy as jnp
from jax import lax
from jax.experimental import pallas as pl
from jax.experimental.pallas import tpu as pltpu
from jax.sharding import PartitionSpec as P

MESH = pl.DeviceIdType.MESH
F32 = jnp.float32
BF16 = jnp.bfloat16

C = 256
GC = 1024
STEPS = 6
COLS = 8
ROWS = 16
PIX = COLS * ROWS
ROWS_OUT = 288
HALF = 144
FORGET_SHIFT = 1.0
PIECE = ((2, 0), (1, 0), (2, 1), (0, 0), (0, 1), (2, 2), (1, 1), (2, 3))
DIRS = ((-1, -1), (-1, 0), (-1, 1), (0, -1), (0, 1), (1, -1), (1, 0), (1, 1))


def sigmoid(value):
    return 0.5 * jnp.tanh(0.5 * value) + 0.5


def kernel(
    frames, weight, cotangent, hid_out, gin_out, wg_out,
    w, wt, acc, xc, x_rows, x_corners, xrim0, xrim1, xrim2, hs, h_rows, h_corners, hrim0, hrim1, hrim2, st, pst, act, cell, squash, up, gates, pg, hrow, gin,
    rrim0, rrim1, rrim2, urim0, urim1, urim2, grim0, grim1, grim2,
    rstage0, rstage1, rstage2, gstage0, gstage1, gstage2, gown, gsum, spread,
    recurrent, carried, sums, part, from_l, from_r, full_l, full_r, total, from2, got,
    w_sem, in_sem, out_sem, xs_send, fr_send, hs_send, rs_send, us_send, gs_send, ps_send, pg_send,
    xc_recv, x_recv, h_recv, r_recv_rim, u_recv_rim, g_recv_rim, u_recv, ps_recv, pg_recv,
    t_send, t_recv, f_send, f_recv, h2_send, h2_recv, d_send, d_recv,
):
    xrim, hrim, rrim = (xrim0, xrim1, xrim2), (hrim0, hrim1, hrim2), (rrim0, rrim1, rrim2)
    urim, grim = (urim0, urim1, urim2), (grim0, grim1, grim2)
    rstage, gstage = (rstage0, rstage1, rstage2), (gstage0, gstage1, gstage2)
    layer = lax.axis_index("layer")
    tile = lax.axis_index("tile")
    trow, tcol = tile // 8, lax.rem(tile, 8)
    ypos, core = tcol // 2, lax.rem(tcol, 2)
    mate = tile + 1 - 2 * core

    def there(d):
        dy, dx = DIRS[d]
        found = jnp.bool_(True)
        if dy < 0:
            found = found & (trow > 0)
        if dy > 0:
            found = found & (trow < 3)
        if dx < 0:
            found = found & (tcol > 0)
        if dx > 0:
            found = found & (tcol < 7)
        return found, tile + 8 * dy + dx

    def remote(src, dst, send, recv, to_layer, to_tile):
        return pltpu.make_async_remote_copy(
            src_ref=src, dst_ref=dst, send_sem=send, recv_sem=recv,
            device_id={"layer": to_layer, "tile": to_tile}, device_id_type=MESH,
        )

    def at_ring(along_y, step, which):
        if along_y:
            return trow * 8 + lax.rem(ypos + step, 4) * 2 + which
        return lax.rem(trow + step, 4) * 8 + ypos * 2 + which

    @pl.when(layer == 0)
    def _():
        pltpu.make_async_copy(frames, gin, in_sem).start()

    @pl.when(layer == 3)
    def _():
        pltpu.make_async_copy(cotangent, gin, in_sem).start()

    w_copies = [pltpu.make_async_copy(weight.at[:, n], w.at[n], w_sem.at[n]) for n in range(2)]
    for copy in w_copies:
        copy.start()

    barrier = pltpu.get_barrier_semaphore()
    expected = jnp.int32(0)

    def greet(found, to_layer, to_tile):
        @pl.when(found)
        def _():
            pl.semaphore_signal(barrier, inc=1, device_id={"layer": to_layer, "tile": to_tile}, device_id_type=MESH)

        return found.astype(jnp.int32)

    for d in range(8):
        found, other = there(d)
        expected += greet(found, layer, other)
        expected += greet(found & (layer > 0), layer - 1, other)
        expected += greet(found & (layer < 3), layer + 1, other)
    expected += greet(layer > 0, layer - 1, tile)
    expected += greet(layer < 3, layer + 1, tile)
    for along_y in (True, False):
        for step in (1, 2, 3):
            for other in range(2):
                expected += greet(jnp.bool_(True), layer, at_ring(along_y, step, other))

    recurrent[...] = jnp.zeros_like(recurrent)
    carried[...] = jnp.zeros_like(carried)
    cell[0] = jnp.zeros((PIX, C), F32)
    st[0, 1] = jnp.zeros((3, COLS + 2, ROWS, C), BF16)
    for d in range(8):
        found, _ = there(d)

        @pl.when(jnp.logical_not(found))
        def _(d=d):
            kind, n = PIECE[d]
            for rims in (xrim, hrim, rrim, urim, grim):
                rims[kind][n] = jnp.zeros(rims[kind].shape[1:], rims[kind].dtype)

    pl.semaphore_wait(barrier, expected)

    pixel_row = lax.broadcasted_iota(jnp.int32, (ROWS, 1), 0)
    is_top = pixel_row == 0
    is_bottom = pixel_row == ROWS - 1

    def put_centre(dst, value):
        dst[0, 1:9] = pltpu.roll(value, 1, 0).astype(BF16).reshape(COLS, ROWS, C)
        dst[1, 1:9] = value.astype(BF16).reshape(COLS, ROWS, C)
        dst[2, 1:9] = pltpu.roll(value, PIX - 1, 0).astype(BF16).reshape(COLS, ROWS, C)

    def row_of(rims, n, t):
        held = rims[1][n, t].astype(F32)
        if held.shape[1] == C:
            return held
        return jnp.concatenate([held[0:8], held[8:16]], axis=1)

    def corner_of(rims, n, t):
        held = rims[2][n, t]
        return jnp.concatenate([held[0:1], held[1:2]], axis=1)

    def fold_row(row):
        return jnp.concatenate([row[:, 0:128], row[:, 128:256]], axis=0)

    def put_rim(dst, rims, t):
        top = row_of(rims, 0, t).reshape(COLS, 1, C)
        bottom = row_of(rims, 1, t).reshape(COLS, 1, C)
        dst[0, 1:9] = jnp.where(is_top[None], top, dst[0, 1:9].astype(F32)).astype(BF16)
        dst[2, 1:9] = jnp.where(is_bottom[None], bottom, dst[2, 1:9].astype(F32)).astype(BF16)
        for n, column in ((0, 0), (1, 9)):
            value = rims[0][n, t].astype(F32)
            dst[0, column] = jnp.where(is_top, corner_of(rims, n, t), pltpu.roll(value, 1, 0)).astype(BF16)
            dst[1, column] = rims[0][n, t]
            lower = corner_of(rims, n + 2, t)
            dst[2, column] = jnp.where(is_bottom, lower, pltpu.roll(value, ROWS - 1, 0)).astype(BF16)

    def put_stage(rows, corners, t, value):
        cut = value.reshape(COLS, ROWS, C)
        rows[0, t] = fold_row(cut[:, 0, :]).astype(BF16)
        rows[1, t] = fold_row(cut[:, ROWS - 1, :]).astype(BF16)
        for n, at in enumerate((0, PIX - ROWS, ROWS - 1, PIX - 1)):
            corners[n, t] = fold_row(value[at : at + 1])

    def add_rims(value, rims, t):
        cut = value.reshape(COLS, ROWS, C)
        cut = cut + jnp.where(is_top[None], row_of(rims, 0, t).reshape(COLS, 1, C), 0.0)
        cut = cut + jnp.where(is_bottom[None], row_of(rims, 1, t).reshape(COLS, 1, C), 0.0)
        sides = []
        for n in range(2):
            column = rims[0][n, t].astype(F32) + jnp.where(is_top, corner_of(rims, n, t), 0.0)
            sides.append((column + jnp.where(is_bottom, corner_of(rims, n + 2, t), 0.0))[None])
        cut = jnp.concatenate([cut[0:1] + sides[0], cut[1:7], cut[7:8] + sides[1]], axis=0)
        return cut.reshape(PIX, C)

    def by_columns(value):
        return jnp.transpose(value.astype(F32).reshape(ROWS, COLS, C), (1, 0, 2))

    def by_rows(value):
        return jnp.transpose(value.reshape(COLS, ROWS, C), (1, 0, 2)).reshape(PIX, C).astype(BF16)

    def map_rims(store, rows, corners, t):
        return (store.at[t, 0], store.at[t, COLS - 1]), (rows.at[0, t], rows.at[1, t]), [corners.at[n, t] for n in range(4)]

    def grad_rims(stage):
        return [[held.at[n] for n in range(held.shape[0])] for held in stage]

    def rim_copies(source, rims, t, send, recv, to_layer, act_on):
        for d in range(8):
            found, other = there(d)
            kind, n = PIECE[d]
            far = PIECE[7 - d][1]

            @pl.when(found)
            def _(d=d, other=other, kind=kind, n=n, far=far):
                act_on(remote(
                    source[kind][n], rims[kind].at[far, t], send.at[d], recv.at[7 - d, t], to_layer, other
                ))

    def rim_arrivals(rims, t, send, recv):
        for d in range(8):
            found, other = there(d)
            kind, n = PIECE[d]

            @pl.when(found)
            def _(d=d, other=other, kind=kind, n=n):
                here = rims[kind].at[n, t]
                remote(here, here, send.at[d], recv.at[d, t], layer, other).wait_recv()

    def begin(copy):
        copy.start()

    def settle(copy):
        copy.wait_send()

    def send_map(store, rows, corners, rims, t, send, recv, to_layer):
        source = map_rims(store, rows, corners, t)

        @pl.when(t > 0)
        def _():
            rim_copies(source, rims, t, send, recv, to_layer, settle)

        rim_copies(source, rims, t, send, recv, to_layer, begin)

    def end_map(store, rows, corners, rims, send, recv, to_layer):
        rim_copies(map_rims(store, rows, corners, 0), rims, 0, send, recv, to_layer, settle)

    def turn_weight():
        acc[...] = jnp.zeros_like(acc)

        def one(k, _):
            for n in range(2):
                wt[n, k] = w[n, k].T
            return 0

        lax.fori_loop(0, 9, one, 0)

    @pl.when(layer == 0)
    def _():
        pltpu.make_async_copy(frames, gin, in_sem).wait()

        def one(t, _):
            value = by_columns(gin[t])
            xc[t] = value.astype(BF16)
            put_stage(x_rows, x_corners, t, value.reshape(PIX, C))
            rim_copies(map_rims(xc, x_rows, x_corners, t), xrim, t, fr_send.at[t], x_recv, layer, begin)
            return 0

        lax.fori_loop(0, STEPS, one, 0)

    for copy in w_copies:
        copy.wait()

    @pl.when(layer == 3)
    def _():
        pltpu.make_async_copy(cotangent, gin, in_sem).wait()

        def one(t, _):
            up[t] = by_columns(gin[t]).astype(BF16)
            return 0

        lax.fori_loop(0, STEPS, one, 0)
        turn_weight()

    def mate_patches(t):
        return remote(st.at[t], pst.at[t], ps_send.at[t], ps_recv.at[t], layer, mate)

    def above_map(t):
        return remote(hs.at[t], xc.at[t], xs_send.at[8], xc_recv.at[t], layer + 1, tile)

    def patches(t, n):
        taps = [st[t, n, p, q : q + 8].reshape(PIX, C) for p in range(3) for q in range(3)]
        return jnp.concatenate(taps, axis=1)

    def forward(t, _):
        @pl.when(layer > 0)
        def _():
            remote(xc.at[t], xc.at[t], xs_send.at[8], xc_recv.at[t], layer - 1, tile).wait_recv()

        put_centre(st.at[t, 0], xc[t].astype(F32).reshape(PIX, C))
        rim_arrivals(xrim, t, xs_send, x_recv)
        put_rim(st.at[t, 0], xrim, t)
        sums[...] = jnp.dot(patches(t, 0), w[0].reshape(9 * C, GC), preferred_element_type=F32)

        @pl.when(t > 0)
        def _():
            rim_arrivals(hrim, t - 1, hs_send, h_recv)
            put_rim(st.at[t, 1], hrim, t - 1)
            sums[...] += jnp.dot(patches(t, 1), w[1].reshape(9 * C, GC), preferred_element_type=F32)

        in_gate = sigmoid(sums[:, 0:C])
        forget = sigmoid(sums[:, C : 2 * C] + FORGET_SHIFT)
        out_gate = sigmoid(sums[:, 2 * C : 3 * C])
        update = jnp.tanh(sums[:, 3 * C :])
        fresh = forget * cell[t] + in_gate * update
        squashed = jnp.tanh(fresh)
        hidden = out_gate * squashed
        hs[t] = hidden.astype(BF16).reshape(COLS, ROWS, C)
        put_stage(h_rows, h_corners, t, hidden)

        @pl.when(t < STEPS - 1)
        def _():
            send_map(hs, h_rows, h_corners, hrim, t, hs_send, h_recv, layer)

        @pl.when(layer < 3)
        def _():
            @pl.when(t > 0)
            def _():
                above_map(t - 1).wait_send()

            above_map(t).start()
            send_map(hs, h_rows, h_corners, xrim, t, xs_send, x_recv, layer + 1)

        @pl.when(layer == 3)
        def _():
            mate_patches(t).start()

        act[t, :, 0:C] = in_gate
        act[t, :, C : 2 * C] = forget
        act[t, :, 2 * C : 3 * C] = out_gate
        act[t, :, 3 * C :] = update
        cell[t + 1] = fresh
        squash[t] = squashed
        hrow[t] = by_rows(hidden)

        @pl.when(t < STEPS - 1)
        def _():
            put_centre(st.at[t + 1, 1], hidden)

        return 0

    lax.fori_loop(0, STEPS, forward, 0)
    end_map(hs, h_rows, h_corners, hrim, hs_send, h_recv, layer)

    hid_copy = pltpu.make_async_copy(hrow, hid_out, out_sem.at[0])
    hid_copy.start()

    @pl.when(layer < 3)
    def _():
        def one(i, _):
            mate_patches(STEPS - 1 - i).start()
            return 0

        lax.fori_loop(0, STEPS, one, 0)
        turn_weight()
        above_map(STEPS - 1).wait_send()
        end_map(hs, h_rows, h_corners, xrim, xs_send, x_recv, layer + 1)

    @pl.when(layer == 0)
    def _():
        def one(t, _):
            rim_copies(map_rims(xc, x_rows, x_corners, t), xrim, t, fr_send.at[t], x_recv, layer, settle)
            return 0

        lax.fori_loop(0, STEPS, one, 0)

    mine = pl.ds(pl.multiple_of(core * 512, 512), 512)
    theirs = pl.ds(pl.multiple_of((1 - core) * 512, 512), 512)

    def mate_gates(t):
        return remote(gates.at[t, :, theirs], pg.at[t], pg_send, pg_recv.at[t], layer, mate)

    def weight_terms(t, n, p, q):
        lhs = jnp.concatenate(
            [st[t, n, p, q : q + 8].reshape(PIX, C), pst[t, n, p, q : q + 8].reshape(PIX, C)], axis=0
        )
        rhs = jnp.concatenate([gates[t, :, mine], pg[t]], axis=0)
        return lax.dot_general(lhs, rhs, (((0,), (0,)), ((), ())), preferred_element_type=F32)

    def wait_mate(t):
        mate_patches(t).wait_recv()
        mate_gates(t).wait_recv()

    def below_grad(t):
        return remote(gown.at[t], up.at[t], us_send.at[8], u_recv.at[t], layer - 1, tile)

    def spread_out(t, n, stage):
        for p in range(3):
            for q in range(3):
                term = jnp.dot(gates[t], wt[n, 3 * p + q], preferred_element_type=F32)
                if q == 0:
                    spread[p, 0:PIX] = term
                    spread[p, PIX:] = jnp.zeros((2 * ROWS, C), F32)
                else:
                    spread[p, ROWS * q : ROWS * q + PIX] += term
        row = lax.rem(lax.broadcasted_iota(jnp.int32, (PIX + 2 * ROWS, 1), 0), ROWS)
        upper, lower = spread[0], spread[2]
        centre = spread[1] + jnp.where(row == ROWS - 1, 0.0, pltpu.roll(upper, PIX + 2 * ROWS - 1, 0))
        centre = centre + jnp.where(row == 0, 0.0, pltpu.roll(lower, 1, 0))
        rows = (upper.reshape(COLS + 2, ROWS, C)[1:9, 0, :], lower.reshape(COLS + 2, ROWS, C)[1:9, ROWS - 1, :])
        stage[0][0] = centre[0:ROWS].astype(stage[0].dtype)
        stage[0][1] = centre[PIX + ROWS :].astype(stage[0].dtype)
        for m in range(2):
            stage[1][m] = (rows[m] if stage[1].shape[2] == C else fold_row(rows[m])).astype(stage[1].dtype)
        ends = ((upper, 0), (upper, PIX + ROWS), (lower, ROWS - 1), (lower, PIX + 2 * ROWS - 1))
        for m, (source, at) in enumerate(ends):
            stage[2][m] = fold_row(source[at : at + 1])
        return centre[ROWS : PIX + ROWS]

    def settle_inputs(t):
        rim_copies(grad_rims(gstage), grim, t, gs_send, g_recv_rim, layer, settle)

        @pl.when(layer > 0)
        def _():
            below_grad(t).wait_send()
            rim_copies(grad_rims(gstage), urim, t, us_send, u_recv_rim, layer - 1, settle)

    def finish_inputs(t):
        rim_arrivals(grim, t, gs_send, g_recv_rim)
        gin[t] = by_rows(add_rims(gsum[t], grim, t))

    def input_part(t):
        @pl.when(t < STEPS - 1)
        def _():
            settle_inputs(t + 1)

        own = spread_out(t, 0, gstage)
        gown[t] = own.astype(BF16).reshape(COLS, ROWS, C)

        @pl.when(layer > 0)
        def _():
            below_grad(t).start()
            rim_copies(grad_rims(gstage), urim, t, us_send, u_recv_rim, layer - 1, begin)

        rim_copies(grad_rims(gstage), grim, t, gs_send, g_recv_rim, layer, begin)
        gsum[t] = own

    @pl.when(layer == 3)
    def _():
        for held in urim:
            held[...] = jnp.zeros_like(held)

    def backward(i, _):
        t = STEPS - 1 - i

        @pl.when(i > 0)
        def _():
            rim_arrivals(rrim, t + 1, rs_send, r_recv_rim)
            recurrent[...] = add_rims(recurrent[...], rrim, t + 1)

        @pl.when(layer < 3)
        def _():
            remote(up.at[t], up.at[t], us_send.at[8], u_recv.at[t], layer + 1, tile).wait_recv()
            rim_arrivals(urim, t, us_send, u_recv_rim)

        grad_hidden = add_rims(up[t].astype(F32).reshape(PIX, C) + recurrent[...], urim, t)
        in_gate = act[t, :, 0:C]
        forget = act[t, :, C : 2 * C]
        out_gate = act[t, :, 2 * C : 3 * C]
        update = act[t, :, 3 * C :]
        squashed = squash[t]
        grad_cell = grad_hidden * out_gate * (1.0 - squashed * squashed) + carried[...]
        carried[...] = grad_cell * forget
        gates[t, :, 0:C] = (grad_cell * update * in_gate * (1.0 - in_gate)).astype(BF16)
        gates[t, :, C : 2 * C] = (grad_cell * cell[t] * forget * (1.0 - forget)).astype(BF16)
        gates[t, :, 2 * C : 3 * C] = (grad_hidden * squashed * out_gate * (1.0 - out_gate)).astype(BF16)
        gates[t, :, 3 * C :] = (grad_cell * in_gate * (1.0 - update * update)).astype(BF16)

        @pl.when(i > 0)
        def _():
            mate_gates(t + 1).wait_send()

        mate_gates(t).start()

        @pl.when(t > 0)
        def _():
            @pl.when(i > 0)
            def _():
                rim_copies(grad_rims(rstage), rrim, t + 1, rs_send, r_recv_rim, layer, settle)

            recurrent[...] = spread_out(t, 1, rstage)
            rim_copies(grad_rims(rstage), rrim, t, rs_send, r_recv_rim, layer, begin)

        @pl.when((layer > 0) | (t > 0))
        def _():
            input_part(t)

        @pl.when(t > 0)
        def _():
            wait_mate(t)
            for p in range(3):
                for q in range(3):
                    for n in range(2):
                        low = 512 * (3 * p + q) + C * n
                        acc[low : low + C] += weight_terms(t, n, p, q)

        @pl.when((i > 0) & (t > 0))
        def _():
            finish_inputs(t + 1)

        return 0

    lax.fori_loop(0, STEPS, backward, 0)

    def plus(left, right):
        return (left.astype(F32) + right.astype(F32)).astype(BF16)

    def own(n):
        return (ypos, trow) if n == 0 else (trow, ypos)

    rights, lefts = (2, 1), (3, 0)
    sent = []

    def go(copy):
        copy.start()
        sent.append(copy)
        return copy

    hand = {}
    full = {}

    def last_terms(half):
        columns = slice(256 * half, 256 * half + 256)
        rhs = jnp.concatenate(
            [gates[0, :, pl.ds(pl.multiple_of(core * 512 + 256 * half, 256), 256)], pg[0, :, columns]], axis=0
        )
        for p in range(3):
            for q in range(3):
                for n in range(2):
                    start = 512 * (3 * p + q) + C * n
                    value = acc[start : start + C, columns]
                    if n == 0:
                        lhs = jnp.concatenate(
                            [st[0, n, p, q : q + 8].reshape(PIX, C), pst[0, n, p, q : q + 8].reshape(PIX, C)], axis=0
                        )
                        value += lax.dot_general(lhs, rhs, (((0,), (0,)), ((), ())), preferred_element_type=F32)
                    value = value.astype(BF16)
                    low = start
                    while low < start + C:
                        block = low // ROWS_OUT
                        high = min(start + C, ROWS_OUT * (block + 1))
                        rows = slice(low - ROWS_OUT * block, high - ROWS_OUT * block)
                        z, y = block // 4, block % 4
                        at = (0, y, z, rows) if half == 0 else (1, z, y, rows)
                        part[at] = value[low - start : high - start]
                        low = high

    def send_full(n, j, right):
        a, b = own(n)
        full[n, j, right] = go(remote(
            part.at[n, lax.rem(a + (1 if right else 3), 4), lax.rem(b + j, 4)], (full_l if right else full_r).at[n, j],
            f_send.at[n, j, int(right)], f_recv.at[n, j, int(right)], layer, at_ring(n == 0, 1 if right else 3, core),
        ))

    wait_mate(0)
    mate_gates(0).wait_send()
    for n in range(2):
        a, b = own(n)
        last_terms(n)
        for m in range(2):
            for right in (True, False):
                j = (rights if right else lefts)[m]
                hand[n, m, right] = go(remote(
                    part.at[n, lax.rem(a + 2, 4), lax.rem(b + j, 4)], (from_l if right else from_r).at[n, m],
                    t_send.at[n, m, int(right)], t_recv.at[n, m, int(right)], layer,
                    at_ring(n == 0, 1 if right else 3, core),
                ))
        for m in range(2):
            send_full(n, lefts[m], True)
            send_full(n, rights[m], False)

    @pl.when(layer == 0)
    def _():
        input_part(0)

    finish_inputs(1)
    rim_copies(grad_rims(rstage), rrim, 1, rs_send, r_recv_rim, layer, settle)
    for m in range(2):
        for n in range(2):
            a, b = own(n)
            for right in (True, False):
                j = (rights if right else lefts)[m]
                hand[n, m, right].wait_recv()
                to = (n, lax.rem(a + (1 if right else 3), 4), lax.rem(b + j, 4))
                part[to] = plus(part[to], (from_l if right else from_r)[n, m])
                send_full(n, j, right)
    finish_inputs(0)
    gin_copy = pltpu.make_async_copy(gin, gin_out, out_sem.at[1])
    gin_copy.start()
    settle_inputs(0)

    def gather(n, j):
        a, b = own(n)
        full[n, j, True].wait_recv()
        full[n, j, False].wait_recv()
        total[n, j] = (
            part[n, a, lax.rem(b + j, 4)].astype(F32) + full_l[n, j].astype(F32) + full_r[n, j].astype(F32)
        ).astype(BF16)

    def half_rows(which):
        return pl.ds(pl.multiple_of(which * HALF, HALF), HALF)

    def to_owner(n, j, which, slot):
        return remote(
            total.at[n, j, half_rows(which)], got.at[n, j, core], d_send.at[n, j, slot], d_recv.at[n, j, core],
            layer, at_ring(n == 1, j, which),
        )

    hand2 = {}
    for j in (2, 3, 1, 0):
        for n in range(2):
            gather(n, j)
            if j == 0:
                go(to_owner(n, 0, 1 - core, 0))
                got[n, 0, core] = total[n, 0, half_rows(core), :]
            elif j == 2:
                for which in range(2):
                    hand2[n, which] = go(remote(
                        total.at[n, 2, half_rows(which)], from2.at[n, which], h2_send.at[n, which],
                        h2_recv.at[n, which], layer, at_ring(n == 1, 1 if which == 0 else 3, core),
                    ))
            else:
                which = 1 if j == 1 else 0
                go(to_owner(n, j, which, which))
    for n in range(2):
        for which, j in ((0, 1), (1, 3)):
            hand2[n, which].wait_recv()
            total[n, j, half_rows(which), :] = plus(total[n, j, half_rows(which), :], from2[n, which])
            go(to_owner(n, j, which, which))
    for n in range(2):
        here = got.at[n, 0, 1 - core]
        remote(here, here, d_send.at[n, 0, 0], d_recv.at[n, 0, 1 - core], layer, mate).wait_recv()
        for j in (1, 3):
            for which in range(2):
                here = got.at[n, j, which]
                remote(here, here, d_send.at[n, j, which], d_recv.at[n, j, which], layer, at_ring(n == 1, 4 - j, which)).wait_recv()
    for which in range(2):
        for n in range(2):
            low = 512 * which + 256 * n
            wg_out[:, low : low + 256] = (
                got[n, 0, which].astype(F32) + got[n, 1, which].astype(F32) + got[n, 3, which].astype(F32)
            )
    for copy in sent:
        copy.wait_send()

    def left(t, _):
        mate_patches(t).wait_send()
        return 0

    lax.fori_loop(0, STEPS, left, 0)
    hid_copy.wait()
    gin_copy.wait()


def copy_out(a, b, c, a_out, b_out, c_out, a_held, b_held, c_held, in_sem, out_sem):
    ways = ((a, a_held, a_out), (b, b_held, b_out), (c, c_held, c_out))
    come = [pltpu.make_async_copy(way[0], way[1], in_sem.at[n]) for n, way in enumerate(ways)]
    leave = [pltpu.make_async_copy(way[1], way[2], out_sem.at[n]) for n, way in enumerate(ways)]
    for copy in come:
        copy.start()
    for arrived, copy in zip(come, leave):
        arrived.wait()
        copy.start()
    for copy in leave:
        copy.wait()


def local(frames, weight, cotangent):
    maps = jax.ShapeDtypeStruct((STEPS, PIX, C), BF16)
    vmem = pltpu.VMEM
    dma = pltpu.SemaphoreType.DMA
    shape = (STEPS, COLS, ROWS, C)
    block = (ROWS_OUT, 256)

    def rims_of(dtype):
        row = (ROWS, 128) if dtype == BF16 else (8, C)
        return vmem((2, STEPS, ROWS, C), dtype), vmem((2, STEPS) + row, dtype), vmem((4, STEPS, 2, 128), F32)

    def stage_of(steps):
        return vmem((2, steps, ROWS, 128), BF16), vmem((4, steps, 2, 128), F32)

    hidden, grads, weight_grad = pl.pallas_call(
        kernel,
        out_shape=(maps, maps, jax.ShapeDtypeStruct((HALF, GC), F32)),
        in_specs=[pl.BlockSpec(memory_space=pl.ANY)] * 3,
        out_specs=(
            pl.BlockSpec(memory_space=pl.ANY),
            pl.BlockSpec(memory_space=pl.ANY),
            pl.BlockSpec(memory_space=pltpu.VMEM),
        ),
        scratch_shapes=[
            vmem((2, 9, C, GC), BF16),
            vmem((2, 9, GC, C), BF16),
            vmem((4608, 512), F32),
            vmem(shape, BF16),
            *stage_of(STEPS),
            *rims_of(BF16),
            vmem(shape, BF16),
            *stage_of(STEPS),
            *rims_of(BF16),
            vmem((STEPS, 2, 3, COLS + 2, ROWS, C), BF16),
            vmem((STEPS, 2, 3, COLS + 2, ROWS, C), BF16),
            vmem((STEPS, PIX, GC), F32),
            vmem((STEPS + 1, PIX, C), F32),
            vmem((STEPS, PIX, C), F32),
            vmem(shape, BF16),
            vmem((STEPS, PIX, GC), BF16),
            vmem((STEPS, PIX, 512), BF16),
            vmem((STEPS, PIX, C), BF16),
            vmem((STEPS, PIX, C), BF16),
            *rims_of(F32),
            *rims_of(BF16),
            *rims_of(BF16),
            vmem((2, ROWS, C), F32), vmem((2, 8, C), F32), vmem((4, 2, 128), F32),
            vmem((2, ROWS, C), BF16), vmem((2, ROWS, 128), BF16), vmem((4, 2, 128), F32),
            vmem(shape, BF16),
            vmem((STEPS, PIX, C), F32),
            vmem((3, PIX + 2 * ROWS, C), F32),
            vmem((PIX, C), F32),
            vmem((PIX, C), F32),
            vmem((PIX, GC), F32),
            vmem((2, 4, 4) + block, BF16),
            vmem((2, 2) + block, BF16),
            vmem((2, 2) + block, BF16),
            vmem((2, 4) + block, BF16),
            vmem((2, 4) + block, BF16),
            vmem((2, 4) + block, BF16),
            vmem((2, 2, HALF, 256), BF16),
            vmem((2, 4, 2, HALF, 256), BF16),
            dma((2,)), dma, dma((2,)),
            dma((9,)), dma((STEPS, 8)), dma((8,)), dma((8,)), dma((9,)), dma((8,)), dma((STEPS,)), dma,
            dma((STEPS,)), dma((8, STEPS)), dma((8, STEPS)),
            dma((8, STEPS)), dma((8, STEPS)), dma((8, STEPS)),
            dma((STEPS,)), dma((STEPS,)), dma((STEPS,)),
            dma((2, 2, 2)), dma((2, 2, 2)), dma((2, 4, 2)), dma((2, 4, 2)),
            dma((2, 2)), dma((2, 2)), dma((2, 4, 2)), dma((2, 4, 2)),
        ],
        compiler_params=pltpu.CompilerParams(
            collective_id=0, has_side_effects=True, vmem_limit_bytes=63 * 2**20
        ),
    )(
        frames.reshape(STEPS, PIX, C),
        weight.reshape(9, 2, C, GC),
        cotangent.reshape(STEPS, PIX, C),
    )
    hidden, grads, weight_grad = pl.pallas_call(
        copy_out,
        out_shape=(maps, maps, jax.ShapeDtypeStruct((HALF, GC), F32)),
        in_specs=[pl.BlockSpec(memory_space=pl.ANY)] * 3,
        out_specs=(pl.BlockSpec(memory_space=pl.ANY),) * 3,
        scratch_shapes=[vmem((STEPS, PIX, C), BF16), vmem((STEPS, PIX, C), BF16), vmem((HALF, GC), F32), dma((3,)), dma((3,))],
    )(hidden, grads, weight_grad)
    tiled = (1, STEPS, 1, ROWS, COLS, C)
    return hidden.reshape(tiled), grads.reshape(tiled), weight_grad[None]


def solution(mesh):
    in_specs = (
        P(None, "tile", None, None, None),
        P("layer", None, None),
        P(None, "tile", None, None, None),
    )
    out_specs = (
        P("layer", None, "tile", None, None, None),
        P("layer", None, "tile", None, None, None),
        P("layer", "tile", None),
    )
    return jax.shard_map(local, mesh=mesh, in_specs=in_specs, out_specs=out_specs, check_vma=False)
```

```python
import jax
import jax.numpy as jnp
from jax import lax
from jax.experimental import pallas as pl
from jax.experimental.pallas import tpu as pltpu
from jax.sharding import PartitionSpec as P

MESH = pl.DeviceIdType.MESH
F32 = jnp.float32
BF16 = jnp.bfloat16

C = 256
GC = 1024
STEPS = 6
COLS = 8
ROWS = 16
PIX = COLS * ROWS
ROWS_OUT = 288
HALF = 144
FORGET_SHIFT = 1.0
CUTS = tuple(slice(low, low + 32) for low in range(0, PIX, 32))
PIECE = ((2, 0), (1, 0), (2, 1), (0, 0), (0, 1), (2, 2), (1, 1), (2, 3))
DIRS = ((-1, -1), (-1, 0), (-1, 1), (0, -1), (0, 1), (1, -1), (1, 0), (1, 1))


def sigmoid(value):
    return 0.5 * jnp.tanh(0.5 * value) + 0.5


def kernel(
    frames, weight, cotangent, hid_out, gin_out, wg_out,
    w, wt, acc, xc, x_rows, x_corners, xrim0, xrim1, xrim2, hs, h_rows, h_corners, hrim0, hrim1, hrim2, st, pst, act, cell, squash, up, gates, pg, hrow, gin,
    rrim0, rrim1, rrim2, urim0, urim1, urim2, grim0, grim1, grim2,
    rstage0, rstage1, rstage2, gstage0, gstage1, gstage2, gown, gsum, spread,
    recurrent, carried, sums, part, from_l, from_r, full_l, full_r, total, from2, got,
    w_sem, in_sem, out_sem, xs_send, fr_send, hs_send, rs_send, us_send, gs_send, ps_send, pg_send,
    xc_recv, x_recv, h_recv, r_recv_rim, u_recv_rim, g_recv_rim, u_recv, ps_recv, pg_recv,
    t_send, t_recv, f_send, f_recv, h2_send, h2_recv, d_send, d_recv,
):
    xrim, hrim, rrim = (xrim0, xrim1, xrim2), (hrim0, hrim1, hrim2), (rrim0, rrim1, rrim2)
    urim, grim = (urim0, urim1, urim2), (grim0, grim1, grim2)
    rstage, gstage = (rstage0, rstage1, rstage2), (gstage0, gstage1, gstage2)
    layer = lax.axis_index("layer")
    tile = lax.axis_index("tile")
    trow, tcol = tile // 8, lax.rem(tile, 8)
    ypos, core = tcol // 2, lax.rem(tcol, 2)
    mate = tile + 1 - 2 * core

    def there(d):
        dy, dx = DIRS[d]
        found = jnp.bool_(True)
        if dy < 0:
            found = found & (trow > 0)
        if dy > 0:
            found = found & (trow < 3)
        if dx < 0:
            found = found & (tcol > 0)
        if dx > 0:
            found = found & (tcol < 7)
        return found, tile + 8 * dy + dx

    def remote(src, dst, send, recv, to_layer, to_tile):
        return pltpu.make_async_remote_copy(
            src_ref=src, dst_ref=dst, send_sem=send, recv_sem=recv,
            device_id={"layer": to_layer, "tile": to_tile}, device_id_type=MESH,
        )

    def at_ring(along_y, step, which):
        if along_y:
            return trow * 8 + lax.rem(ypos + step, 4) * 2 + which
        return lax.rem(trow + step, 4) * 8 + ypos * 2 + which

    @pl.when(layer == 0)
    def _():
        pltpu.make_async_copy(frames, gin, in_sem).start()

    @pl.when(layer == 3)
    def _():
        pltpu.make_async_copy(cotangent, gin, in_sem).start()

    w_copies = [pltpu.make_async_copy(weight.at[:, n], w.at[n], w_sem.at[n]) for n in range(2)]
    for copy in w_copies:
        copy.start()

    barrier = pltpu.get_barrier_semaphore()
    expected = jnp.int32(0)

    def greet(found, to_layer, to_tile):
        @pl.when(found)
        def _():
            pl.semaphore_signal(barrier, inc=1, device_id={"layer": to_layer, "tile": to_tile}, device_id_type=MESH)

        return found.astype(jnp.int32)

    for d in range(8):
        found, other = there(d)
        expected += greet(found, layer, other)
        expected += greet(found & (layer > 0), layer - 1, other)
        expected += greet(found & (layer < 3), layer + 1, other)
    expected += greet(layer > 0, layer - 1, tile)
    expected += greet(layer < 3, layer + 1, tile)
    for along_y in (True, False):
        for step in (1, 2, 3):
            for other in range(2):
                expected += greet(jnp.bool_(True), layer, at_ring(along_y, step, other))

    recurrent[...] = jnp.zeros_like(recurrent)
    carried[...] = jnp.zeros_like(carried)
    cell[0] = jnp.zeros((PIX, C), F32)
    st[0, 1] = jnp.zeros((3, COLS + 2, ROWS, C), BF16)
    for d in range(8):
        found, _ = there(d)

        @pl.when(jnp.logical_not(found))
        def _(d=d):
            kind, n = PIECE[d]
            for rims in (xrim, hrim, rrim, urim, grim):
                rims[kind][n] = jnp.zeros(rims[kind].shape[1:], rims[kind].dtype)

    pl.semaphore_wait(barrier, expected)

    pixel_row = lax.broadcasted_iota(jnp.int32, (ROWS, 1), 0)
    is_top = pixel_row == 0
    is_bottom = pixel_row == ROWS - 1

    def put_centre(dst, value):
        dst[0, 1:9] = pltpu.roll(value, 1, 0).astype(BF16).reshape(COLS, ROWS, C)
        dst[1, 1:9] = value.astype(BF16).reshape(COLS, ROWS, C)
        dst[2, 1:9] = pltpu.roll(value, PIX - 1, 0).astype(BF16).reshape(COLS, ROWS, C)

    def row_of(rims, n, t):
        held = rims[1][n, t].astype(F32)
        if held.shape[1] == C:
            return held
        return jnp.concatenate([held[0:8], held[8:16]], axis=1)

    def corner_of(rims, n, t):
        held = rims[2][n, t]
        return jnp.concatenate([held[0:1], held[1:2]], axis=1)

    def fold_row(row):
        return jnp.concatenate([row[:, 0:128], row[:, 128:256]], axis=0)

    def put_rim(dst, rims, t):
        top = row_of(rims, 0, t).reshape(COLS, 1, C)
        bottom = row_of(rims, 1, t).reshape(COLS, 1, C)
        dst[0, 1:9] = jnp.where(is_top[None], top, dst[0, 1:9].astype(F32)).astype(BF16)
        dst[2, 1:9] = jnp.where(is_bottom[None], bottom, dst[2, 1:9].astype(F32)).astype(BF16)
        for n, column in ((0, 0), (1, 9)):
            value = rims[0][n, t].astype(F32)
            dst[0, column] = jnp.where(is_top, corner_of(rims, n, t), pltpu.roll(value, 1, 0)).astype(BF16)
            dst[1, column] = rims[0][n, t]
            lower = corner_of(rims, n + 2, t)
            dst[2, column] = jnp.where(is_bottom, lower, pltpu.roll(value, ROWS - 1, 0)).astype(BF16)

    def put_stage(rows, corners, t, value):
        cut = value.reshape(COLS, ROWS, C)
        rows[0, t] = fold_row(cut[:, 0, :]).astype(BF16)
        rows[1, t] = fold_row(cut[:, ROWS - 1, :]).astype(BF16)
        for n, at in enumerate((0, PIX - ROWS, ROWS - 1, PIX - 1)):
            corners[n, t] = fold_row(value[at : at + 1])

    def add_rims(value, rims, t):
        cut = value.reshape(COLS, ROWS, C)
        cut = cut + jnp.where(is_top[None], row_of(rims, 0, t).reshape(COLS, 1, C), 0.0)
        cut = cut + jnp.where(is_bottom[None], row_of(rims, 1, t).reshape(COLS, 1, C), 0.0)
        sides = []
        for n in range(2):
            column = rims[0][n, t].astype(F32) + jnp.where(is_top, corner_of(rims, n, t), 0.0)
            sides.append((column + jnp.where(is_bottom, corner_of(rims, n + 2, t), 0.0))[None])
        cut = jnp.concatenate([cut[0:1] + sides[0], cut[1:7], cut[7:8] + sides[1]], axis=0)
        return cut.reshape(PIX, C)

    def by_columns(value):
        return jnp.transpose(value.astype(F32).reshape(ROWS, COLS, C), (1, 0, 2))

    def by_rows(value):
        return jnp.transpose(value.reshape(COLS, ROWS, C), (1, 0, 2)).reshape(PIX, C).astype(BF16)

    def map_rims(store, rows, corners, t):
        return (store.at[t, 0], store.at[t, COLS - 1]), (rows.at[0, t], rows.at[1, t]), [corners.at[n, t] for n in range(4)]

    def grad_rims(stage):
        return [[held.at[n] for n in range(held.shape[0])] for held in stage]

    def rim_copies(source, rims, t, send, recv, to_layer, act_on):
        for d in range(8):
            found, other = there(d)
            kind, n = PIECE[d]
            far = PIECE[7 - d][1]

            @pl.when(found)
            def _(d=d, other=other, kind=kind, n=n, far=far):
                act_on(remote(
                    source[kind][n], rims[kind].at[far, t], send.at[d], recv.at[7 - d, t], to_layer, other
                ))

    def rim_arrivals(rims, t, send, recv):
        for d in range(8):
            found, other = there(d)
            kind, n = PIECE[d]

            @pl.when(found)
            def _(d=d, other=other, kind=kind, n=n):
                here = rims[kind].at[n, t]
                remote(here, here, send.at[d], recv.at[d, t], layer, other).wait_recv()

    def begin(copy):
        copy.start()

    def settle(copy):
        copy.wait_send()

    def send_map(store, rows, corners, rims, t, send, recv, to_layer):
        source = map_rims(store, rows, corners, t)

        @pl.when(t > 0)
        def _():
            rim_copies(source, rims, t, send, recv, to_layer, settle)

        rim_copies(source, rims, t, send, recv, to_layer, begin)

    def end_map(store, rows, corners, rims, send, recv, to_layer):
        rim_copies(map_rims(store, rows, corners, 0), rims, 0, send, recv, to_layer, settle)

    def turn_weight():
        acc[...] = jnp.zeros_like(acc)

        def one(k, _):
            for n in range(2):
                wt[n, k] = w[n, k].T
            return 0

        lax.fori_loop(0, 9, one, 0)

    @pl.when(layer == 0)
    def _():
        pltpu.make_async_copy(frames, gin, in_sem).wait()

        def one(t, _):
            value = by_columns(gin[t])
            xc[t] = value.astype(BF16)
            put_stage(x_rows, x_corners, t, value.reshape(PIX, C))
            rim_copies(map_rims(xc, x_rows, x_corners, t), xrim, t, fr_send.at[t], x_recv, layer, begin)
            return 0

        lax.fori_loop(0, STEPS, one, 0)

    for copy in w_copies:
        copy.wait()

    @pl.when(layer == 3)
    def _():
        pltpu.make_async_copy(cotangent, gin, in_sem).wait()

        def one(t, _):
            up[t] = by_columns(gin[t]).astype(BF16)
            return 0

        lax.fori_loop(0, STEPS, one, 0)
        turn_weight()

    def mate_patches(t):
        return remote(st.at[t], pst.at[t], ps_send.at[t], ps_recv.at[t], layer, mate)

    def above_map(t):
        return remote(hs.at[t], xc.at[t], xs_send.at[8], xc_recv.at[t], layer + 1, tile)

    def patches(t, n):
        taps = [st[t, n, p, q : q + 8].reshape(PIX, C) for p in range(3) for q in range(3)]
        return jnp.concatenate(taps, axis=1)

    def forward(t, _):
        @pl.when(layer > 0)
        def _():
            remote(xc.at[t], xc.at[t], xs_send.at[8], xc_recv.at[t], layer - 1, tile).wait_recv()

        put_centre(st.at[t, 0], xc[t].astype(F32).reshape(PIX, C))
        rim_arrivals(xrim, t, xs_send, x_recv)
        put_rim(st.at[t, 0], xrim, t)
        sums[...] = jnp.dot(patches(t, 0), w[0].reshape(9 * C, GC), preferred_element_type=F32)

        @pl.when(t > 0)
        def _():
            rim_arrivals(hrim, t - 1, hs_send, h_recv)
            put_rim(st.at[t, 1], hrim, t - 1)
            sums[...] += jnp.dot(patches(t, 1), w[1].reshape(9 * C, GC), preferred_element_type=F32)

        pieces = []
        for cut in CUTS:
            in_gate = sigmoid(sums[cut, 0:C])
            forget = sigmoid(sums[cut, C : 2 * C] + FORGET_SHIFT)
            out_gate = sigmoid(sums[cut, 2 * C : 3 * C])
            update = jnp.tanh(sums[cut, 3 * C :])
            fresh = forget * cell[t, cut] + in_gate * update
            squashed = jnp.tanh(fresh)
            pieces.append(out_gate * squashed)
            act[t, cut, 0:C] = in_gate
            act[t, cut, C : 2 * C] = forget
            act[t, cut, 2 * C : 3 * C] = out_gate
            act[t, cut, 3 * C :] = update
            cell[t + 1, cut] = fresh
            squash[t, cut] = squashed
        hidden = jnp.concatenate(pieces, axis=0)
        hs[t] = hidden.astype(BF16).reshape(COLS, ROWS, C)
        put_stage(h_rows, h_corners, t, hidden)

        @pl.when(t < STEPS - 1)
        def _():
            send_map(hs, h_rows, h_corners, hrim, t, hs_send, h_recv, layer)

        @pl.when(layer < 3)
        def _():
            @pl.when(t > 0)
            def _():
                above_map(t - 1).wait_send()

            above_map(t).start()
            send_map(hs, h_rows, h_corners, xrim, t, xs_send, x_recv, layer + 1)

        @pl.when(layer == 3)
        def _():
            mate_patches(t).start()

        hrow[t] = by_rows(hidden)

        @pl.when(t < STEPS - 1)
        def _():
            put_centre(st.at[t + 1, 1], hidden)

        return 0

    lax.fori_loop(0, STEPS, forward, 0)
    end_map(hs, h_rows, h_corners, hrim, hs_send, h_recv, layer)

    hid_copy = pltpu.make_async_copy(hrow, hid_out, out_sem.at[0])
    hid_copy.start()

    @pl.when(layer < 3)
    def _():
        def one(i, _):
            mate_patches(STEPS - 1 - i).start()
            return 0

        lax.fori_loop(0, STEPS, one, 0)
        turn_weight()
        above_map(STEPS - 1).wait_send()
        end_map(hs, h_rows, h_corners, xrim, xs_send, x_recv, layer + 1)

    @pl.when(layer == 0)
    def _():
        def one(t, _):
            rim_copies(map_rims(xc, x_rows, x_corners, t), xrim, t, fr_send.at[t], x_recv, layer, settle)
            return 0

        lax.fori_loop(0, STEPS, one, 0)

    mine = pl.ds(pl.multiple_of(core * 512, 512), 512)
    theirs = pl.ds(pl.multiple_of((1 - core) * 512, 512), 512)

    def mate_gates(t):
        return remote(gates.at[t, :, theirs], pg.at[t], pg_send, pg_recv.at[t], layer, mate)

    def weight_terms(t, n, p, q):
        lhs = jnp.concatenate(
            [st[t, n, p, q : q + 8].reshape(PIX, C), pst[t, n, p, q : q + 8].reshape(PIX, C)], axis=0
        )
        rhs = jnp.concatenate([gates[t, :, mine], pg[t]], axis=0)
        return lax.dot_general(lhs, rhs, (((0,), (0,)), ((), ())), preferred_element_type=F32)

    def wait_mate(t):
        mate_patches(t).wait_recv()
        mate_gates(t).wait_recv()

    def below_grad(t):
        return remote(gown.at[t], up.at[t], us_send.at[8], u_recv.at[t], layer - 1, tile)

    def spread_out(t, n, stage):
        for p in range(3):
            for q in range(3):
                term = jnp.dot(gates[t], wt[n, 3 * p + q], preferred_element_type=F32)
                if q == 0:
                    spread[p, 0:PIX] = term
                    spread[p, PIX:] = jnp.zeros((2 * ROWS, C), F32)
                else:
                    spread[p, ROWS * q : ROWS * q + PIX] += term
        row = lax.rem(lax.broadcasted_iota(jnp.int32, (PIX + 2 * ROWS, 1), 0), ROWS)
        upper, lower = spread[0], spread[2]
        centre = spread[1] + jnp.where(row == ROWS - 1, 0.0, pltpu.roll(upper, PIX + 2 * ROWS - 1, 0))
        centre = centre + jnp.where(row == 0, 0.0, pltpu.roll(lower, 1, 0))
        rows = (upper.reshape(COLS + 2, ROWS, C)[1:9, 0, :], lower.reshape(COLS + 2, ROWS, C)[1:9, ROWS - 1, :])
        stage[0][0] = centre[0:ROWS].astype(stage[0].dtype)
        stage[0][1] = centre[PIX + ROWS :].astype(stage[0].dtype)
        for m in range(2):
            stage[1][m] = (rows[m] if stage[1].shape[2] == C else fold_row(rows[m])).astype(stage[1].dtype)
        ends = ((upper, 0), (upper, PIX + ROWS), (lower, ROWS - 1), (lower, PIX + 2 * ROWS - 1))
        for m, (source, at) in enumerate(ends):
            stage[2][m] = fold_row(source[at : at + 1])
        return centre[ROWS : PIX + ROWS]

    def settle_inputs(t):
        rim_copies(grad_rims(gstage), grim, t, gs_send, g_recv_rim, layer, settle)

        @pl.when(layer > 0)
        def _():
            below_grad(t).wait_send()
            rim_copies(grad_rims(gstage), urim, t, us_send, u_recv_rim, layer - 1, settle)

    def finish_inputs(t):
        rim_arrivals(grim, t, gs_send, g_recv_rim)
        gin[t] = by_rows(add_rims(gsum[t], grim, t))

    def input_part(t):
        @pl.when(t < STEPS - 1)
        def _():
            settle_inputs(t + 1)

        own = spread_out(t, 0, gstage)
        gown[t] = own.astype(BF16).reshape(COLS, ROWS, C)

        @pl.when(layer > 0)
        def _():
            below_grad(t).start()
            rim_copies(grad_rims(gstage), urim, t, us_send, u_recv_rim, layer - 1, begin)

        rim_copies(grad_rims(gstage), grim, t, gs_send, g_recv_rim, layer, begin)
        gsum[t] = own

    @pl.when(layer == 3)
    def _():
        for held in urim:
            held[...] = jnp.zeros_like(held)

    def backward(i, _):
        t = STEPS - 1 - i

        @pl.when(i > 0)
        def _():
            rim_arrivals(rrim, t + 1, rs_send, r_recv_rim)
            recurrent[...] = add_rims(recurrent[...], rrim, t + 1)

        @pl.when(layer < 3)
        def _():
            remote(up.at[t], up.at[t], us_send.at[8], u_recv.at[t], layer + 1, tile).wait_recv()
            rim_arrivals(urim, t, us_send, u_recv_rim)

        grad_hidden = add_rims(up[t].astype(F32).reshape(PIX, C) + recurrent[...], urim, t)
        for cut in CUTS:
            arrived = grad_hidden[cut]
            in_gate = act[t, cut, 0:C]
            forget = act[t, cut, C : 2 * C]
            out_gate = act[t, cut, 2 * C : 3 * C]
            update = act[t, cut, 3 * C :]
            squashed = squash[t, cut]
            grad_cell = arrived * out_gate * (1.0 - squashed * squashed) + carried[cut]
            carried[cut] = grad_cell * forget
            gates[t, cut, 0:C] = (grad_cell * update * in_gate * (1.0 - in_gate)).astype(BF16)
            gates[t, cut, C : 2 * C] = (grad_cell * cell[t, cut] * forget * (1.0 - forget)).astype(BF16)
            gates[t, cut, 2 * C : 3 * C] = (arrived * squashed * out_gate * (1.0 - out_gate)).astype(BF16)
            gates[t, cut, 3 * C :] = (grad_cell * in_gate * (1.0 - update * update)).astype(BF16)

        @pl.when(i > 0)
        def _():
            mate_gates(t + 1).wait_send()

        mate_gates(t).start()

        @pl.when(t > 0)
        def _():
            @pl.when(i > 0)
            def _():
                rim_copies(grad_rims(rstage), rrim, t + 1, rs_send, r_recv_rim, layer, settle)

            recurrent[...] = spread_out(t, 1, rstage)
            rim_copies(grad_rims(rstage), rrim, t, rs_send, r_recv_rim, layer, begin)

        @pl.when((layer > 0) | (t > 0))
        def _():
            input_part(t)

        @pl.when(t > 0)
        def _():
            wait_mate(t)
            for p in range(3):
                for q in range(3):
                    for n in range(2):
                        low = 512 * (3 * p + q) + C * n
                        acc[low : low + C] += weight_terms(t, n, p, q)

        @pl.when((i > 0) & (t > 0))
        def _():
            finish_inputs(t + 1)

        return 0

    lax.fori_loop(0, STEPS, backward, 0)

    def plus(left, right):
        return (left.astype(F32) + right.astype(F32)).astype(BF16)

    def own(n):
        return (ypos, trow) if n == 0 else (trow, ypos)

    rights, lefts = (2, 1), (3, 0)
    sent = []

    def go(copy):
        copy.start()
        sent.append(copy)
        return copy

    hand = {}
    full = {}

    def last_terms(half, n):
        columns = slice(256 * half, 256 * half + 256)
        if n == 0:
            mine_now = pl.ds(pl.multiple_of(core * 512 + 256 * half, 256), 256)
            rhs = jnp.concatenate([gates[0, :, mine_now], pg[0, :, columns]], axis=0)
        for p in range(3):
            for q in range(3):
                start = 512 * (3 * p + q) + C * n
                value = acc[start : start + C, columns]
                if n == 0:
                    lhs = jnp.concatenate(
                        [st[0, n, p, q : q + 8].reshape(PIX, C), pst[0, n, p, q : q + 8].reshape(PIX, C)], axis=0
                    )
                    value += lax.dot_general(lhs, rhs, (((0,), (0,)), ((), ())), preferred_element_type=F32)
                value = value.astype(BF16)
                low = start
                while low < start + C:
                    block = low // ROWS_OUT
                    high = min(start + C, ROWS_OUT * (block + 1))
                    rows = slice(low - ROWS_OUT * block, high - ROWS_OUT * block)
                    z, y = block // 4, block % 4
                    at = (0, y, z, rows) if half == 0 else (1, z, y, rows)
                    part[at] = value[low - start : high - start]
                    low = high

    def send_full(n, j, right):
        a, b = own(n)
        full[n, j, right] = go(remote(
            part.at[n, lax.rem(a + (1 if right else 3), 4), lax.rem(b + j, 4)], (full_l if right else full_r).at[n, j],
            f_send.at[n, j, int(right)], f_recv.at[n, j, int(right)], layer, at_ring(n == 0, 1 if right else 3, core),
        ))

    for half in range(2):
        last_terms(half, 1)
    wait_mate(0)
    mate_gates(0).wait_send()
    for n in range(2):
        a, b = own(n)
        last_terms(n, 0)
        for m in range(2):
            for right in (True, False):
                j = (rights if right else lefts)[m]
                hand[n, m, right] = go(remote(
                    part.at[n, lax.rem(a + 2, 4), lax.rem(b + j, 4)], (from_l if right else from_r).at[n, m],
                    t_send.at[n, m, int(right)], t_recv.at[n, m, int(right)], layer,
                    at_ring(n == 0, 1 if right else 3, core),
                ))
        for m in range(2):
            send_full(n, lefts[m], True)
            send_full(n, rights[m], False)

    @pl.when(layer == 0)
    def _():
        input_part(0)

    finish_inputs(1)
    rim_copies(grad_rims(rstage), rrim, 1, rs_send, r_recv_rim, layer, settle)
    for m in range(2):
        for n in range(2):
            a, b = own(n)
            for right in (True, False):
                j = (rights if right else lefts)[m]
                hand[n, m, right].wait_recv()
                to = (n, lax.rem(a + (1 if right else 3), 4), lax.rem(b + j, 4))
                part[to] = plus(part[to], (from_l if right else from_r)[n, m])
                send_full(n, j, right)
    finish_inputs(0)
    gin_copy = pltpu.make_async_copy(gin, gin_out, out_sem.at[1])
    gin_copy.start()
    settle_inputs(0)

    def gather(n, j):
        a, b = own(n)
        full[n, j, True].wait_recv()
        full[n, j, False].wait_recv()
        total[n, j] = (
            part[n, a, lax.rem(b + j, 4)].astype(F32) + full_l[n, j].astype(F32) + full_r[n, j].astype(F32)
        ).astype(BF16)

    def half_rows(which):
        return pl.ds(pl.multiple_of(which * HALF, HALF), HALF)

    def to_owner(n, j, which, slot):
        return remote(
            total.at[n, j, half_rows(which)], got.at[n, j, core], d_send.at[n, j, slot], d_recv.at[n, j, core],
            layer, at_ring(n == 1, j, which),
        )

    hand2 = {}
    for j in (2, 3, 1, 0):
        for n in range(2):
            gather(n, j)
            if j == 0:
                go(to_owner(n, 0, 1 - core, 0))
                got[n, 0, core] = total[n, 0, half_rows(core), :]
            elif j == 2:
                for which in range(2):
                    hand2[n, which] = go(remote(
                        total.at[n, 2, half_rows(which)], from2.at[n, which], h2_send.at[n, which],
                        h2_recv.at[n, which], layer, at_ring(n == 1, 1 if which == 0 else 3, core),
                    ))
            else:
                which = 1 if j == 1 else 0
                go(to_owner(n, j, which, which))
    for n in range(2):
        for which, j in ((0, 1), (1, 3)):
            hand2[n, which].wait_recv()
            total[n, j, half_rows(which), :] = plus(total[n, j, half_rows(which), :], from2[n, which])
            go(to_owner(n, j, which, which))
    for n in range(2):
        here = got.at[n, 0, 1 - core]
        remote(here, here, d_send.at[n, 0, 0], d_recv.at[n, 0, 1 - core], layer, mate).wait_recv()
        for j in (1, 3):
            for which in range(2):
                here = got.at[n, j, which]
                remote(here, here, d_send.at[n, j, which], d_recv.at[n, j, which], layer, at_ring(n == 1, 4 - j, which)).wait_recv()
    for which in range(2):
        for n in range(2):
            low = 512 * which + 256 * n
            wg_out[:, low : low + 256] = (
                got[n, 0, which].astype(F32) + got[n, 1, which].astype(F32) + got[n, 3, which].astype(F32)
            )
    for copy in sent:
        copy.wait_send()

    def left(t, _):
        mate_patches(t).wait_send()
        return 0

    lax.fori_loop(0, STEPS, left, 0)
    hid_copy.wait()
    gin_copy.wait()


def copy_out(a, b, c, a_out, b_out, c_out, a_held, b_held, c_held, in_sem, out_sem):
    ways = ((a, a_held, a_out), (b, b_held, b_out), (c, c_held, c_out))
    come = [pltpu.make_async_copy(way[0], way[1], in_sem.at[n]) for n, way in enumerate(ways)]
    leave = [pltpu.make_async_copy(way[1], way[2], out_sem.at[n]) for n, way in enumerate(ways)]
    for copy in come:
        copy.start()
    for arrived, copy in zip(come, leave):
        arrived.wait()
        copy.start()
    for copy in leave:
        copy.wait()


def local(frames, weight, cotangent):
    maps = jax.ShapeDtypeStruct((STEPS, PIX, C), BF16)
    vmem = pltpu.VMEM
    dma = pltpu.SemaphoreType.DMA
    shape = (STEPS, COLS, ROWS, C)
    block = (ROWS_OUT, 256)

    def rims_of(dtype):
        row = (ROWS, 128) if dtype == BF16 else (8, C)
        return vmem((2, STEPS, ROWS, C), dtype), vmem((2, STEPS) + row, dtype), vmem((4, STEPS, 2, 128), F32)

    def stage_of(steps):
        return vmem((2, steps, ROWS, 128), BF16), vmem((4, steps, 2, 128), F32)

    hidden, grads, weight_grad = pl.pallas_call(
        kernel,
        out_shape=(maps, maps, jax.ShapeDtypeStruct((HALF, GC), F32)),
        in_specs=[pl.BlockSpec(memory_space=pl.ANY)] * 3,
        out_specs=(
            pl.BlockSpec(memory_space=pl.ANY),
            pl.BlockSpec(memory_space=pl.ANY),
            pl.BlockSpec(memory_space=pltpu.VMEM),
        ),
        scratch_shapes=[
            vmem((2, 9, C, GC), BF16),
            vmem((2, 9, GC, C), BF16),
            vmem((4608, 512), F32),
            vmem(shape, BF16),
            *stage_of(STEPS),
            *rims_of(BF16),
            vmem(shape, BF16),
            *stage_of(STEPS),
            *rims_of(BF16),
            vmem((STEPS, 2, 3, COLS + 2, ROWS, C), BF16),
            vmem((STEPS, 2, 3, COLS + 2, ROWS, C), BF16),
            vmem((STEPS, PIX, GC), F32),
            vmem((STEPS + 1, PIX, C), F32),
            vmem((STEPS, PIX, C), F32),
            vmem(shape, BF16),
            vmem((STEPS, PIX, GC), BF16),
            vmem((STEPS, PIX, 512), BF16),
            vmem((STEPS, PIX, C), BF16),
            vmem((STEPS, PIX, C), BF16),
            *rims_of(F32),
            *rims_of(BF16),
            *rims_of(BF16),
            vmem((2, ROWS, C), F32), vmem((2, 8, C), F32), vmem((4, 2, 128), F32),
            vmem((2, ROWS, C), BF16), vmem((2, ROWS, 128), BF16), vmem((4, 2, 128), F32),
            vmem(shape, BF16),
            vmem((STEPS, PIX, C), F32),
            vmem((3, PIX + 2 * ROWS, C), F32),
            vmem((PIX, C), F32),
            vmem((PIX, C), F32),
            vmem((PIX, GC), F32),
            vmem((2, 4, 4) + block, BF16),
            vmem((2, 2) + block, BF16),
            vmem((2, 2) + block, BF16),
            vmem((2, 4) + block, BF16),
            vmem((2, 4) + block, BF16),
            vmem((2, 4) + block, BF16),
            vmem((2, 2, HALF, 256), BF16),
            vmem((2, 4, 2, HALF, 256), BF16),
            dma((2,)), dma, dma((2,)),
            dma((9,)), dma((STEPS, 8)), dma((8,)), dma((8,)), dma((9,)), dma((8,)), dma((STEPS,)), dma,
            dma((STEPS,)), dma((8, STEPS)), dma((8, STEPS)),
            dma((8, STEPS)), dma((8, STEPS)), dma((8, STEPS)),
            dma((STEPS,)), dma((STEPS,)), dma((STEPS,)),
            dma((2, 2, 2)), dma((2, 2, 2)), dma((2, 4, 2)), dma((2, 4, 2)),
            dma((2, 2)), dma((2, 2)), dma((2, 4, 2)), dma((2, 4, 2)),
        ],
        compiler_params=pltpu.CompilerParams(
            collective_id=0, has_side_effects=True, vmem_limit_bytes=63 * 2**20
        ),
    )(
        frames.reshape(STEPS, PIX, C),
        weight.reshape(9, 2, C, GC),
        cotangent.reshape(STEPS, PIX, C),
    )
    hidden, grads, weight_grad = pl.pallas_call(
        copy_out,
        out_shape=(maps, maps, jax.ShapeDtypeStruct((HALF, GC), F32)),
        in_specs=[pl.BlockSpec(memory_space=pl.ANY)] * 3,
        out_specs=(pl.BlockSpec(memory_space=pl.ANY),) * 3,
        scratch_shapes=[vmem((STEPS, PIX, C), BF16), vmem((STEPS, PIX, C), BF16), vmem((HALF, GC), F32), dma((3,)), dma((3,))],
    )(hidden, grads, weight_grad)
    tiled = (1, STEPS, 1, ROWS, COLS, C)
    return hidden.reshape(tiled), grads.reshape(tiled), weight_grad[None]


def solution(mesh):
    in_specs = (
        P(None, "tile", None, None, None),
        P("layer", None, None),
        P(None, "tile", None, None, None),
    )
    out_specs = (
        P("layer", None, "tile", None, None, None),
        P("layer", None, "tile", None, None, None),
        P("layer", "tile", None),
    )
    return jax.shard_map(local, mesh=mesh, in_specs=in_specs, out_specs=out_specs, check_vma=False)
```

```python
import jax
import jax.numpy as jnp
from jax import lax
from jax.experimental import pallas as pl
from jax.experimental.pallas import tpu as pltpu
from jax.sharding import PartitionSpec as P

MESH = pl.DeviceIdType.MESH
F32 = jnp.float32
BF16 = jnp.bfloat16

C = 256
GC = 1024
STEPS = 6
COLS = 8
ROWS = 16
PIX = COLS * ROWS
ROWS_OUT = 288
HALF = 144
FORGET_SHIFT = 1.0
CUTS = tuple(slice(low, low + 32) for low in range(0, PIX, 32))
PIECE = ((2, 0), (1, 0), (2, 1), (0, 0), (0, 1), (2, 2), (1, 1), (2, 3))
DIRS = ((-1, -1), (-1, 0), (-1, 1), (0, -1), (0, 1), (1, -1), (1, 0), (1, 1))


def sigmoid(value):
    return 0.5 * jnp.tanh(0.5 * value) + 0.5


def kernel(
    frames, weight, cotangent, hid_out, gin_out, wg_out,
    w, wt, acc, xc, x_rows, x_corners, xrim0, xrim1, xrim2, hs, h_rows, h_corners, hrim0, hrim1, hrim2, st, pst, act, cell, squash, up, gates, pg, hrow, gin,
    rrim0, rrim1, rrim2, urim0, urim1, urim2, grim0, grim1, grim2,
    rstage0, rstage1, rstage2, gstage0, gstage1, gstage2, gown, gsum, spread,
    recurrent, carried, sums, part, from_l, from_r, full_l, full_r, total, from2, got,
    w_sem, in_sem, out_sem, xs_send, fr_send, hs_send, rs_send, us_send, gs_send, ps_send, pg_send,
    xc_recv, x_recv, h_recv, r_recv_rim, u_recv_rim, g_recv_rim, u_recv, ps_recv, pg_recv,
    t_send, t_recv, f_send, f_recv, h2_send, h2_recv, d_send, d_recv,
):
    xrim, hrim, rrim = (xrim0, xrim1, xrim2), (hrim0, hrim1, hrim2), (rrim0, rrim1, rrim2)
    urim, grim = (urim0, urim1, urim2), (grim0, grim1, grim2)
    rstage, gstage = (rstage0, rstage1, rstage2), (gstage0, gstage1, gstage2)
    layer = lax.axis_index("layer")
    tile = lax.axis_index("tile")
    trow, tcol = tile // 8, lax.rem(tile, 8)
    ypos, core = tcol // 2, lax.rem(tcol, 2)
    mate = tile + 1 - 2 * core

    def there(d):
        dy, dx = DIRS[d]
        found = jnp.bool_(True)
        if dy < 0:
            found = found & (trow > 0)
        if dy > 0:
            found = found & (trow < 3)
        if dx < 0:
            found = found & (tcol > 0)
        if dx > 0:
            found = found & (tcol < 7)
        return found, tile + 8 * dy + dx

    def remote(src, dst, send, recv, to_layer, to_tile):
        return pltpu.make_async_remote_copy(
            src_ref=src, dst_ref=dst, send_sem=send, recv_sem=recv,
            device_id={"layer": to_layer, "tile": to_tile}, device_id_type=MESH,
        )

    def at_ring(along_y, step, which):
        if along_y:
            return trow * 8 + lax.rem(ypos + step, 4) * 2 + which
        return lax.rem(trow + step, 4) * 8 + ypos * 2 + which

    @pl.when(layer == 0)
    def _():
        pltpu.make_async_copy(frames, gin, in_sem).start()

    @pl.when(layer == 3)
    def _():
        pltpu.make_async_copy(cotangent, gin, in_sem).start()

    w_copies = [pltpu.make_async_copy(weight.at[:, n], w.at[n], w_sem.at[n]) for n in range(2)]
    for copy in w_copies:
        copy.start()

    barrier = pltpu.get_barrier_semaphore()
    expected = jnp.int32(0)

    def greet(found, to_layer, to_tile):
        @pl.when(found)
        def _():
            pl.semaphore_signal(barrier, inc=1, device_id={"layer": to_layer, "tile": to_tile}, device_id_type=MESH)

        return found.astype(jnp.int32)

    for d in range(8):
        found, other = there(d)
        expected += greet(found, layer, other)
        expected += greet(found & (layer > 0), layer - 1, other)
        expected += greet(found & (layer < 3), layer + 1, other)
    expected += greet(layer > 0, layer - 1, tile)
    expected += greet(layer < 3, layer + 1, tile)
    for along_y in (True, False):
        for step in (1, 2, 3):
            for other in range(2):
                expected += greet(jnp.bool_(True), layer, at_ring(along_y, step, other))

    recurrent[...] = jnp.zeros_like(recurrent)
    carried[...] = jnp.zeros_like(carried)
    cell[0] = jnp.zeros((PIX, C), F32)
    st[0, 1] = jnp.zeros((3, COLS + 2, ROWS, C), BF16)
    for d in range(8):
        found, _ = there(d)

        @pl.when(jnp.logical_not(found))
        def _(d=d):
            kind, n = PIECE[d]
            for rims in (xrim, hrim, rrim, urim, grim):
                rims[kind][n] = jnp.zeros(rims[kind].shape[1:], rims[kind].dtype)

    pl.semaphore_wait(barrier, expected)

    pixel_row = lax.broadcasted_iota(jnp.int32, (ROWS, 1), 0)
    is_top = pixel_row == 0
    is_bottom = pixel_row == ROWS - 1

    def put_centre(dst, value):
        dst[0, 1:9] = pltpu.roll(value, 1, 0).astype(BF16).reshape(COLS, ROWS, C)
        dst[1, 1:9] = value.astype(BF16).reshape(COLS, ROWS, C)
        dst[2, 1:9] = pltpu.roll(value, PIX - 1, 0).astype(BF16).reshape(COLS, ROWS, C)

    def row_of(rims, n, t):
        held = rims[1][n, t].astype(F32)
        if held.shape[1] == C:
            return held
        return jnp.concatenate([held[0:8], held[8:16]], axis=1)

    def corner_of(rims, n, t):
        held = rims[2][n, t]
        return jnp.concatenate([held[0:1], held[1:2]], axis=1)

    def fold_row(row):
        return jnp.concatenate([row[:, 0:128], row[:, 128:256]], axis=0)

    def put_rim(dst, rims, t):
        top = row_of(rims, 0, t).reshape(COLS, 1, C)
        bottom = row_of(rims, 1, t).reshape(COLS, 1, C)
        dst[0, 1:9] = jnp.where(is_top[None], top, dst[0, 1:9].astype(F32)).astype(BF16)
        dst[2, 1:9] = jnp.where(is_bottom[None], bottom, dst[2, 1:9].astype(F32)).astype(BF16)
        for n, column in ((0, 0), (1, 9)):
            value = rims[0][n, t].astype(F32)
            dst[0, column] = jnp.where(is_top, corner_of(rims, n, t), pltpu.roll(value, 1, 0)).astype(BF16)
            dst[1, column] = rims[0][n, t]
            lower = corner_of(rims, n + 2, t)
            dst[2, column] = jnp.where(is_bottom, lower, pltpu.roll(value, ROWS - 1, 0)).astype(BF16)

    def put_stage(rows, corners, t, value):
        cut = value.reshape(COLS, ROWS, C)
        rows[0, t] = fold_row(cut[:, 0, :]).astype(BF16)
        rows[1, t] = fold_row(cut[:, ROWS - 1, :]).astype(BF16)
        for n, at in enumerate((0, PIX - ROWS, ROWS - 1, PIX - 1)):
            corners[n, t] = fold_row(value[at : at + 1])

    def add_rims(value, rims, t):
        cut = value.reshape(COLS, ROWS, C)
        cut = cut + jnp.where(is_top[None], row_of(rims, 0, t).reshape(COLS, 1, C), 0.0)
        cut = cut + jnp.where(is_bottom[None], row_of(rims, 1, t).reshape(COLS, 1, C), 0.0)
        sides = []
        for n in range(2):
            column = rims[0][n, t].astype(F32) + jnp.where(is_top, corner_of(rims, n, t), 0.0)
            sides.append((column + jnp.where(is_bottom, corner_of(rims, n + 2, t), 0.0))[None])
        cut = jnp.concatenate([cut[0:1] + sides[0], cut[1:7], cut[7:8] + sides[1]], axis=0)
        return cut.reshape(PIX, C)

    def by_columns(value):
        return jnp.transpose(value.astype(F32).reshape(ROWS, COLS, C), (1, 0, 2))

    def by_rows(value):
        return jnp.transpose(value.reshape(COLS, ROWS, C), (1, 0, 2)).reshape(PIX, C).astype(BF16)

    def map_rims(store, rows, corners, t):
        return (store.at[t, 0], store.at[t, COLS - 1]), (rows.at[0, t], rows.at[1, t]), [corners.at[n, t] for n in range(4)]

    def grad_rims(stage):
        return [[held.at[n] for n in range(held.shape[0])] for held in stage]

    def rim_copies(source, rims, t, send, recv, to_layer, act_on):
        for d in range(8):
            found, other = there(d)
            kind, n = PIECE[d]
            far = PIECE[7 - d][1]

            @pl.when(found)
            def _(d=d, other=other, kind=kind, n=n, far=far):
                act_on(remote(
                    source[kind][n], rims[kind].at[far, t], send.at[d], recv.at[7 - d, t], to_layer, other
                ))

    def rim_arrivals(rims, t, send, recv):
        for d in range(8):
            found, other = there(d)
            kind, n = PIECE[d]

            @pl.when(found)
            def _(d=d, other=other, kind=kind, n=n):
                here = rims[kind].at[n, t]
                remote(here, here, send.at[d], recv.at[d, t], layer, other).wait_recv()

    def begin(copy):
        copy.start()

    def settle(copy):
        copy.wait_send()

    def send_map(store, rows, corners, rims, t, send, recv, to_layer):
        source = map_rims(store, rows, corners, t)

        @pl.when(t > 0)
        def _():
            rim_copies(source, rims, t, send, recv, to_layer, settle)

        rim_copies(source, rims, t, send, recv, to_layer, begin)

    def end_map(store, rows, corners, rims, send, recv, to_layer):
        rim_copies(map_rims(store, rows, corners, 0), rims, 0, send, recv, to_layer, settle)

    def turn_weight():
        acc[...] = jnp.zeros_like(acc)

        def one(k, _):
            for n in range(2):
                wt[n, k] = w[n, k].T
            return 0

        lax.fori_loop(0, 9, one, 0)

    @pl.when(layer == 0)
    def _():
        pltpu.make_async_copy(frames, gin, in_sem).wait()

        def one(t, _):
            value = by_columns(gin[t])
            xc[t] = value.astype(BF16)
            put_stage(x_rows, x_corners, t, value.reshape(PIX, C))
            rim_copies(map_rims(xc, x_rows, x_corners, t), xrim, t, fr_send.at[t], x_recv, layer, begin)
            return 0

        lax.fori_loop(0, STEPS, one, 0)

    for copy in w_copies:
        copy.wait()

    @pl.when(layer == 3)
    def _():
        pltpu.make_async_copy(cotangent, gin, in_sem).wait()

        def one(t, _):
            up[t] = by_columns(gin[t]).astype(BF16)
            return 0

        lax.fori_loop(0, STEPS, one, 0)
        turn_weight()

    def mate_patches(t):
        return remote(st.at[t], pst.at[t], ps_send.at[t], ps_recv.at[t], layer, mate)

    def above_map(t, half):
        columns = pl.ds(4 * half, 4)
        return remote(
            hs.at[t, columns], xc.at[t, columns], xs_send.at[8 + half], xc_recv.at[t, half], layer + 1, tile
        )

    def patches(t, n):
        taps = [st[t, n, p, q : q + 8].reshape(PIX, C) for p in range(3) for q in range(3)]
        return jnp.concatenate(taps, axis=1)

    def send_above(t, half):
        @pl.when(layer < 3)
        def _():
            @pl.when(t > 0)
            def _():
                above_map(t - 1, half).wait_send()

            above_map(t, half).start()

    def forward(t, _):
        @pl.when(layer > 0)
        def _():
            for half in range(2):
                here = xc.at[t, pl.ds(4 * half, 4)]
                remote(here, here, xs_send.at[8 + half], xc_recv.at[t, half], layer - 1, tile).wait_recv()

        put_centre(st.at[t, 0], xc[t].astype(F32).reshape(PIX, C))
        rim_arrivals(xrim, t, xs_send, x_recv)
        put_rim(st.at[t, 0], xrim, t)
        sums[...] = jnp.dot(patches(t, 0), w[0].reshape(9 * C, GC), preferred_element_type=F32)

        @pl.when(t > 0)
        def _():
            rim_arrivals(hrim, t - 1, hs_send, h_recv)
            put_rim(st.at[t, 1], hrim, t - 1)
            sums[...] += jnp.dot(patches(t, 1), w[1].reshape(9 * C, GC), preferred_element_type=F32)

        pieces = []
        for m, cut in enumerate(CUTS):
            in_gate = sigmoid(sums[cut, 0:C])
            forget = sigmoid(sums[cut, C : 2 * C] + FORGET_SHIFT)
            out_gate = sigmoid(sums[cut, 2 * C : 3 * C])
            update = jnp.tanh(sums[cut, 3 * C :])
            fresh = forget * cell[t, cut] + in_gate * update
            squashed = jnp.tanh(fresh)
            pieces.append(out_gate * squashed)
            act[t, cut, 0:C] = in_gate
            act[t, cut, C : 2 * C] = forget
            act[t, cut, 2 * C : 3 * C] = out_gate
            act[t, cut, 3 * C :] = update
            cell[t + 1, cut] = fresh
            squash[t, cut] = squashed
            hs[t, 2 * m : 2 * m + 2] = pieces[m].astype(BF16).reshape(2, ROWS, C)
            if m == 1:
                send_above(t, 0)
        hidden = jnp.concatenate(pieces, axis=0)
        put_stage(h_rows, h_corners, t, hidden)

        @pl.when(t < STEPS - 1)
        def _():
            send_map(hs, h_rows, h_corners, hrim, t, hs_send, h_recv, layer)

        send_above(t, 1)

        @pl.when(layer < 3)
        def _():
            send_map(hs, h_rows, h_corners, xrim, t, xs_send, x_recv, layer + 1)

        @pl.when(layer == 3)
        def _():
            mate_patches(t).start()

        hrow[t] = by_rows(hidden)

        @pl.when(t < STEPS - 1)
        def _():
            put_centre(st.at[t + 1, 1], hidden)

        return 0

    lax.fori_loop(0, STEPS, forward, 0)
    end_map(hs, h_rows, h_corners, hrim, hs_send, h_recv, layer)

    hid_copy = pltpu.make_async_copy(hrow, hid_out, out_sem.at[0])
    hid_copy.start()

    @pl.when(layer < 3)
    def _():
        def one(i, _):
            mate_patches(STEPS - 1 - i).start()
            return 0

        lax.fori_loop(0, STEPS, one, 0)
        turn_weight()
        for half in range(2):
            above_map(STEPS - 1, half).wait_send()
        end_map(hs, h_rows, h_corners, xrim, xs_send, x_recv, layer + 1)

    @pl.when(layer == 0)
    def _():
        def one(t, _):
            rim_copies(map_rims(xc, x_rows, x_corners, t), xrim, t, fr_send.at[t], x_recv, layer, settle)
            return 0

        lax.fori_loop(0, STEPS, one, 0)

    mine = pl.ds(pl.multiple_of(core * 512, 512), 512)
    theirs = pl.ds(pl.multiple_of((1 - core) * 512, 512), 512)

    def mate_gates(t):
        return remote(gates.at[t, :, theirs], pg.at[t], pg_send, pg_recv.at[t], layer, mate)

    def weight_terms(t, n, p, q):
        lhs = jnp.concatenate(
            [st[t, n, p, q : q + 8].reshape(PIX, C), pst[t, n, p, q : q + 8].reshape(PIX, C)], axis=0
        )
        rhs = jnp.concatenate([gates[t, :, mine], pg[t]], axis=0)
        return lax.dot_general(lhs, rhs, (((0,), (0,)), ((), ())), preferred_element_type=F32)

    def wait_mate(t):
        mate_patches(t).wait_recv()
        mate_gates(t).wait_recv()

    def below_grad(t):
        return remote(gown.at[t], up.at[t], us_send.at[8], u_recv.at[t], layer - 1, tile)

    def spread_out(t, n, stage):
        for p in range(3):
            for q in range(3):
                term = jnp.dot(gates[t], wt[n, 3 * p + q], preferred_element_type=F32)
                if q == 0:
                    spread[p, 0:PIX] = term
                    spread[p, PIX:] = jnp.zeros((2 * ROWS, C), F32)
                else:
                    spread[p, ROWS * q : ROWS * q + PIX] += term
        row = lax.rem(lax.broadcasted_iota(jnp.int32, (PIX + 2 * ROWS, 1), 0), ROWS)
        upper, lower = spread[0], spread[2]
        centre = spread[1] + jnp.where(row == ROWS - 1, 0.0, pltpu.roll(upper, PIX + 2 * ROWS - 1, 0))
        centre = centre + jnp.where(row == 0, 0.0, pltpu.roll(lower, 1, 0))
        rows = (upper.reshape(COLS + 2, ROWS, C)[1:9, 0, :], lower.reshape(COLS + 2, ROWS, C)[1:9, ROWS - 1, :])
        stage[0][0] = centre[0:ROWS].astype(stage[0].dtype)
        stage[0][1] = centre[PIX + ROWS :].astype(stage[0].dtype)
        for m in range(2):
            stage[1][m] = (rows[m] if stage[1].shape[2] == C else fold_row(rows[m])).astype(stage[1].dtype)
        ends = ((upper, 0), (upper, PIX + ROWS), (lower, ROWS - 1), (lower, PIX + 2 * ROWS - 1))
        for m, (source, at) in enumerate(ends):
            stage[2][m] = fold_row(source[at : at + 1])
        return centre[ROWS : PIX + ROWS]

    def settle_inputs(t):
        rim_copies(grad_rims(gstage), grim, t, gs_send, g_recv_rim, layer, settle)

        @pl.when(layer > 0)
        def _():
            below_grad(t).wait_send()
            rim_copies(grad_rims(gstage), urim, t, us_send, u_recv_rim, layer - 1, settle)

    def finish_inputs(t):
        rim_arrivals(grim, t, gs_send, g_recv_rim)
        gin[t] = by_rows(add_rims(gsum[t], grim, t))

    def input_part(t):
        @pl.when(t < STEPS - 1)
        def _():
            settle_inputs(t + 1)

        own = spread_out(t, 0, gstage)
        gown[t] = own.astype(BF16).reshape(COLS, ROWS, C)

        @pl.when(layer > 0)
        def _():
            below_grad(t).start()
            rim_copies(grad_rims(gstage), urim, t, us_send, u_recv_rim, layer - 1, begin)

        rim_copies(grad_rims(gstage), grim, t, gs_send, g_recv_rim, layer, begin)
        gsum[t] = own

    @pl.when(layer == 3)
    def _():
        for held in urim:
            held[...] = jnp.zeros_like(held)

    def backward(i, _):
        t = STEPS - 1 - i

        @pl.when(i > 0)
        def _():
            rim_arrivals(rrim, t + 1, rs_send, r_recv_rim)
            recurrent[...] = add_rims(recurrent[...], rrim, t + 1)

        @pl.when(layer < 3)
        def _():
            remote(up.at[t], up.at[t], us_send.at[8], u_recv.at[t], layer + 1, tile).wait_recv()
            rim_arrivals(urim, t, us_send, u_recv_rim)

        grad_hidden = add_rims(up[t].astype(F32).reshape(PIX, C) + recurrent[...], urim, t)
        for cut in CUTS:
            arrived = grad_hidden[cut]
            in_gate = act[t, cut, 0:C]
            forget = act[t, cut, C : 2 * C]
            out_gate = act[t, cut, 2 * C : 3 * C]
            update = act[t, cut, 3 * C :]
            squashed = squash[t, cut]
            grad_cell = arrived * out_gate * (1.0 - squashed * squashed) + carried[cut]
            carried[cut] = grad_cell * forget
            gates[t, cut, 0:C] = (grad_cell * update * in_gate * (1.0 - in_gate)).astype(BF16)
            gates[t, cut, C : 2 * C] = (grad_cell * cell[t, cut] * forget * (1.0 - forget)).astype(BF16)
            gates[t, cut, 2 * C : 3 * C] = (arrived * squashed * out_gate * (1.0 - out_gate)).astype(BF16)
            gates[t, cut, 3 * C :] = (grad_cell * in_gate * (1.0 - update * update)).astype(BF16)

        @pl.when(i > 0)
        def _():
            mate_gates(t + 1).wait_send()

        mate_gates(t).start()

        @pl.when(t > 0)
        def _():
            @pl.when(i > 0)
            def _():
                rim_copies(grad_rims(rstage), rrim, t + 1, rs_send, r_recv_rim, layer, settle)

            recurrent[...] = spread_out(t, 1, rstage)
            rim_copies(grad_rims(rstage), rrim, t, rs_send, r_recv_rim, layer, begin)

        @pl.when((layer > 0) | (t > 0))
        def _():
            input_part(t)

        @pl.when(t > 0)
        def _():
            wait_mate(t)
            for p in range(3):
                for q in range(3):
                    for n in range(2):
                        low = 512 * (3 * p + q) + C * n
                        acc[low : low + C] += weight_terms(t, n, p, q)

        @pl.when((i > 0) & (t > 0))
        def _():
            finish_inputs(t + 1)

        return 0

    lax.fori_loop(0, STEPS, backward, 0)

    def plus(left, right):
        return (left.astype(F32) + right.astype(F32)).astype(BF16)

    def own(n):
        return (ypos, trow) if n == 0 else (trow, ypos)

    rights, lefts = (2, 1), (3, 0)
    sent = []

    def go(copy):
        copy.start()
        sent.append(copy)
        return copy

    hand = {}
    full = {}

    def last_terms(half, n):
        columns = slice(256 * half, 256 * half + 256)
        if n == 0:
            mine_now = pl.ds(pl.multiple_of(core * 512 + 256 * half, 256), 256)
            rhs = jnp.concatenate([gates[0, :, mine_now], pg[0, :, columns]], axis=0)
        for p in range(3):
            for q in range(3):
                start = 512 * (3 * p + q) + C * n
                value = acc[start : start + C, columns]
                if n == 0:
                    lhs = jnp.concatenate(
                        [st[0, n, p, q : q + 8].reshape(PIX, C), pst[0, n, p, q : q + 8].reshape(PIX, C)], axis=0
                    )
                    value += lax.dot_general(lhs, rhs, (((0,), (0,)), ((), ())), preferred_element_type=F32)
                value = value.astype(BF16)
                low = start
                while low < start + C:
                    block = low // ROWS_OUT
                    high = min(start + C, ROWS_OUT * (block + 1))
                    rows = slice(low - ROWS_OUT * block, high - ROWS_OUT * block)
                    z, y = block // 4, block % 4
                    at = (0, y, z, rows) if half == 0 else (1, z, y, rows)
                    part[at] = value[low - start : high - start]
                    low = high

    def send_full(n, j, right):
        a, b = own(n)
        full[n, j, right] = go(remote(
            part.at[n, lax.rem(a + (1 if right else 3), 4), lax.rem(b + j, 4)], (full_l if right else full_r).at[n, j],
            f_send.at[n, j, int(right)], f_recv.at[n, j, int(right)], layer, at_ring(n == 0, 1 if right else 3, core),
        ))

    for half in range(2):
        last_terms(half, 1)
    wait_mate(0)
    mate_gates(0).wait_send()
    for n in range(2):
        a, b = own(n)
        last_terms(n, 0)
        for m in range(2):
            for right in (True, False):
                j = (rights if right else lefts)[m]
                hand[n, m, right] = go(remote(
                    part.at[n, lax.rem(a + 2, 4), lax.rem(b + j, 4)], (from_l if right else from_r).at[n, m],
                    t_send.at[n, m, int(right)], t_recv.at[n, m, int(right)], layer,
                    at_ring(n == 0, 1 if right else 3, core),
                ))
        for m in range(2):
            send_full(n, lefts[m], True)
            send_full(n, rights[m], False)

    @pl.when(layer == 0)
    def _():
        input_part(0)

    finish_inputs(1)
    rim_copies(grad_rims(rstage), rrim, 1, rs_send, r_recv_rim, layer, settle)
    for m in range(2):
        for n in range(2):
            a, b = own(n)
            for right in (True, False):
                j = (rights if right else lefts)[m]
                hand[n, m, right].wait_recv()
                to = (n, lax.rem(a + (1 if right else 3), 4), lax.rem(b + j, 4))
                part[to] = plus(part[to], (from_l if right else from_r)[n, m])
                send_full(n, j, right)
    finish_inputs(0)
    gin_copy = pltpu.make_async_copy(gin, gin_out, out_sem.at[1])
    gin_copy.start()
    settle_inputs(0)

    def gather(n, j):
        a, b = own(n)
        full[n, j, True].wait_recv()
        full[n, j, False].wait_recv()
        total[n, j] = (
            part[n, a, lax.rem(b + j, 4)].astype(F32) + full_l[n, j].astype(F32) + full_r[n, j].astype(F32)
        ).astype(BF16)

    def half_rows(which):
        return pl.ds(pl.multiple_of(which * HALF, HALF), HALF)

    def to_owner(n, j, which, slot):
        return remote(
            total.at[n, j, half_rows(which)], got.at[n, j, core], d_send.at[n, j, slot], d_recv.at[n, j, core],
            layer, at_ring(n == 1, j, which),
        )

    hand2 = {}
    for j in (2, 3, 1, 0):
        for n in range(2):
            gather(n, j)
            if j == 0:
                go(to_owner(n, 0, 1 - core, 0))
                got[n, 0, core] = total[n, 0, half_rows(core), :]
            elif j == 2:
                for which in range(2):
                    hand2[n, which] = go(remote(
                        total.at[n, 2, half_rows(which)], from2.at[n, which], h2_send.at[n, which],
                        h2_recv.at[n, which], layer, at_ring(n == 1, 1 if which == 0 else 3, core),
                    ))
            else:
                which = 1 if j == 1 else 0
                go(to_owner(n, j, which, which))
    for n in range(2):
        for which, j in ((0, 1), (1, 3)):
            hand2[n, which].wait_recv()
            total[n, j, half_rows(which), :] = plus(total[n, j, half_rows(which), :], from2[n, which])
            go(to_owner(n, j, which, which))
    for n in range(2):
        here = got.at[n, 0, 1 - core]
        remote(here, here, d_send.at[n, 0, 0], d_recv.at[n, 0, 1 - core], layer, mate).wait_recv()
        for j in (1, 3):
            for which in range(2):
                here = got.at[n, j, which]
                remote(here, here, d_send.at[n, j, which], d_recv.at[n, j, which], layer, at_ring(n == 1, 4 - j, which)).wait_recv()
    for which in range(2):
        for n in range(2):
            low = 512 * which + 256 * n
            wg_out[:, low : low + 256] = (
                got[n, 0, which].astype(F32) + got[n, 1, which].astype(F32) + got[n, 3, which].astype(F32)
            )
    for copy in sent:
        copy.wait_send()

    def left(t, _):
        mate_patches(t).wait_send()
        return 0

    lax.fori_loop(0, STEPS, left, 0)
    hid_copy.wait()
    gin_copy.wait()


def copy_out(a, b, c, a_out, b_out, c_out, a_held, b_held, c_held, in_sem, out_sem):
    ways = ((a, a_held, a_out), (b, b_held, b_out), (c, c_held, c_out))
    come = [pltpu.make_async_copy(way[0], way[1], in_sem.at[n]) for n, way in enumerate(ways)]
    leave = [pltpu.make_async_copy(way[1], way[2], out_sem.at[n]) for n, way in enumerate(ways)]
    for copy in come:
        copy.start()
    for arrived, copy in zip(come, leave):
        arrived.wait()
        copy.start()
    for copy in leave:
        copy.wait()


def local(frames, weight, cotangent):
    maps = jax.ShapeDtypeStruct((STEPS, PIX, C), BF16)
    vmem = pltpu.VMEM
    dma = pltpu.SemaphoreType.DMA
    shape = (STEPS, COLS, ROWS, C)
    block = (ROWS_OUT, 256)

    def rims_of(dtype):
        row = (ROWS, 128) if dtype == BF16 else (8, C)
        return vmem((2, STEPS, ROWS, C), dtype), vmem((2, STEPS) + row, dtype), vmem((4, STEPS, 2, 128), F32)

    def stage_of(steps):
        return vmem((2, steps, ROWS, 128), BF16), vmem((4, steps, 2, 128), F32)

    hidden, grads, weight_grad = pl.pallas_call(
        kernel,
        out_shape=(maps, maps, jax.ShapeDtypeStruct((HALF, GC), F32)),
        in_specs=[pl.BlockSpec(memory_space=pl.ANY)] * 3,
        out_specs=(
            pl.BlockSpec(memory_space=pl.ANY),
            pl.BlockSpec(memory_space=pl.ANY),
            pl.BlockSpec(memory_space=pltpu.VMEM),
        ),
        scratch_shapes=[
            vmem((2, 9, C, GC), BF16),
            vmem((2, 9, GC, C), BF16),
            vmem((4608, 512), F32),
            vmem(shape, BF16),
            *stage_of(STEPS),
            *rims_of(BF16),
            vmem(shape, BF16),
            *stage_of(STEPS),
            *rims_of(BF16),
            vmem((STEPS, 2, 3, COLS + 2, ROWS, C), BF16),
            vmem((STEPS, 2, 3, COLS + 2, ROWS, C), BF16),
            vmem((STEPS, PIX, GC), F32),
            vmem((STEPS + 1, PIX, C), F32),
            vmem((STEPS, PIX, C), F32),
            vmem(shape, BF16),
            vmem((STEPS, PIX, GC), BF16),
            vmem((STEPS, PIX, 512), BF16),
            vmem((STEPS, PIX, C), BF16),
            vmem((STEPS, PIX, C), BF16),
            *rims_of(F32),
            *rims_of(BF16),
            *rims_of(BF16),
            vmem((2, ROWS, C), F32), vmem((2, 8, C), F32), vmem((4, 2, 128), F32),
            vmem((2, ROWS, C), BF16), vmem((2, ROWS, 128), BF16), vmem((4, 2, 128), F32),
            vmem(shape, BF16),
            vmem((STEPS, PIX, C), F32),
            vmem((3, PIX + 2 * ROWS, C), F32),
            vmem((PIX, C), F32),
            vmem((PIX, C), F32),
            vmem((PIX, GC), F32),
            vmem((2, 4, 4) + block, BF16),
            vmem((2, 2) + block, BF16),
            vmem((2, 2) + block, BF16),
            vmem((2, 4) + block, BF16),
            vmem((2, 4) + block, BF16),
            vmem((2, 4) + block, BF16),
            vmem((2, 2, HALF, 256), BF16),
            vmem((2, 4, 2, HALF, 256), BF16),
            dma((2,)), dma, dma((2,)),
            dma((10,)), dma((STEPS, 8)), dma((8,)), dma((8,)), dma((9,)), dma((8,)), dma((STEPS,)), dma,
            dma((STEPS, 2)), dma((8, STEPS)), dma((8, STEPS)),
            dma((8, STEPS)), dma((8, STEPS)), dma((8, STEPS)),
            dma((STEPS,)), dma((STEPS,)), dma((STEPS,)),
            dma((2, 2, 2)), dma((2, 2, 2)), dma((2, 4, 2)), dma((2, 4, 2)),
            dma((2, 2)), dma((2, 2)), dma((2, 4, 2)), dma((2, 4, 2)),
        ],
        compiler_params=pltpu.CompilerParams(
            collective_id=0, has_side_effects=True, vmem_limit_bytes=63 * 2**20
        ),
    )(
        frames.reshape(STEPS, PIX, C),
        weight.reshape(9, 2, C, GC),
        cotangent.reshape(STEPS, PIX, C),
    )
    hidden, grads, weight_grad = pl.pallas_call(
        copy_out,
        out_shape=(maps, maps, jax.ShapeDtypeStruct((HALF, GC), F32)),
        in_specs=[pl.BlockSpec(memory_space=pl.ANY)] * 3,
        out_specs=(pl.BlockSpec(memory_space=pl.ANY),) * 3,
        scratch_shapes=[vmem((STEPS, PIX, C), BF16), vmem((STEPS, PIX, C), BF16), vmem((HALF, GC), F32), dma((3,)), dma((3,))],
    )(hidden, grads, weight_grad)
    tiled = (1, STEPS, 1, ROWS, COLS, C)
    return hidden.reshape(tiled), grads.reshape(tiled), weight_grad[None]


def solution(mesh):
    in_specs = (
        P(None, "tile", None, None, None),
        P("layer", None, None),
        P(None, "tile", None, None, None),
    )
    out_specs = (
        P("layer", None, "tile", None, None, None),
        P("layer", None, "tile", None, None, None),
        P("layer", "tile", None),
    )
    return jax.shard_map(local, mesh=mesh, in_specs=in_specs, out_specs=out_specs, check_vma=False)
```
